32 devices in a mesh: dp: 4 (over z), ctx: 4 (over x, core), tp: 2 (over y).
Axes of the slice: x: 2, y: 2, z: 4, core: 2. Of those that a mesh axis runs over, the one named last changes fastest.
Arguments:
- hidden: bfloat16 [4, 2048, 1472], P(None, ('dp', 'ctx')), may hold values from -6 to 6
- cotangent: bfloat16 [4, 2048, 1472], P(None, ('dp', 'ctx')), may hold values from -6 to 6
- lengths: int32 [4, 4, 3], P(None, 'dp'), may hold values from 1 to 341, 512 in all within a row
- dealing: int32 [4, 4, 512], P(None, 'dp'), may hold values from 0 to 511, as said below
- keep_flags: int32 [4, 4, 512], P(None, 'dp'), may hold values 0 or 1
- norm1_gain: bfloat16 [1472], P('dp'), may hold values from 0.25 to 1.75
- w_query: bfloat16 [1472, 384], P('dp', 'tp'), may hold values from -0.0390625 to 0.0390625
- w_key: bfloat16 [1472, 384], P('dp', 'tp'), may hold values from -0.15625 to 0.15625
- w_value: bfloat16 [1472, 384], P('dp', 'tp'), may hold values from -0.15625 to 0.15625
- w_out: bfloat16 [384, 1472], P('tp', 'dp'), may hold values from -2.5 to 2.5
- rel_table: bfloat16 [32, 6], P(None, 'tp'), may hold values from -4 to 4
- del_weight: bfloat16 [1472], P('dp'), may hold values from -0.15625 to 0.15625
- norm2_gain: bfloat16 [1472], P('dp'), may hold values from 0.25 to 1.75
- w_gate: bfloat16 [1472, 3584], P('dp', 'tp'), may hold values from -0.15625 to 0.15625
- w_up: bfloat16 [1472, 3584], P('dp', 'tp'), may hold values from -0.15625 to 0.15625
- w_down: bfloat16 [3584, 1472], P('tp', 'dp'), may hold values from -0.09375 to 0.09375
Outputs:
- layer_out: bfloat16 [4, 2048, 1472], P(None, ('dp', 'ctx'))
- gate_values: bfloat16 [4, 2048], P(None, ('dp', 'ctx'))
- hidden_grad: bfloat16 [4, 2048, 1472], P(None, ('dp', 'ctx'))
- grad_norm1_gain: float32 [1472], P('dp')
- grad_w_query: float32 [1472, 384], P('dp', 'tp')
- grad_w_key: float32 [1472, 384], P('dp', 'tp')
- grad_w_value: float32 [1472, 384], P('dp', 'tp')
- grad_w_out: float32 [384, 1472], P('tp', 'dp')
- grad_rel_table: float32 [32, 6], P(None, 'tp')
- grad_del_weight: float32 [1472], P('dp')
- grad_norm2_gain: float32 [1472], P('dp')
- grad_w_gate: float32 [1472, 3584], P('dp', 'tp')
- grad_w_up: float32 [1472, 3584], P('dp', 'tp')
- grad_w_down: float32 [3584, 1472], P('tp', 'dp')
The draws below stay inside these ranges and needn't reach their ends.
Inputs may be any that keep to these rules, and one draw needn't show every extreme that they name: The 3 lengths of each micro-batch and group sum to 512, and the largest is exactly 341. dealing[m, g] is a permutation of the group's 512 tokens. Each aligned run of 128 dealt rows holds exactly 32 tokens of each aligned run of 128 tokens in token order.
All inputs are finite; a program needn't handle non-finite values. No bound on the sum of `keep_flags` on one device may be relied on, other than what follows from the above.
Results may differ from the reference program's by a relative error of at most 0.028.
Values may be sent and summed in bfloat16 or wider, within the bound.
No kernel may reach another device: no remote copies, remote signals or barrier semaphores. Data moves between devices by JAX's collectives and lax.ppermute only.
A program may use at most 256 MiB of HBM per device.

```python
import math
from functools import partial
import jax
import jax.numpy as jnp
import numpy as np
from jax import lax

D = 1472
HEADS = 6
HEAD = 64
FF = 3584
BUCKETS = 32
MAX_DIST = 128
TOK_CTX = 128
MICRO = 4
NSEQ = 3
GROUP_TOK = 512
SEQ_MOST = 341
GROUPS = 4
TOKENS = 2048
N_TP = 2


def draw_dealing(key, part):
    ctx_count = GROUP_TOK // TOK_CTX
    share_rows = TOK_CTX // ctx_count

    def one_group(group_key):
        split_keys = jax.random.split(group_key, 2 * ctx_count)
        spread = jnp.stack([jax.random.permutation(split_keys[member], TOK_CTX).astype(jnp.int32) for member in range(ctx_count)])
        token_ids = jnp.arange(ctx_count, dtype=jnp.int32)[:, None] * TOK_CTX + spread
        dealt_ids = jnp.transpose(token_ids.reshape(ctx_count, ctx_count, share_rows), (1, 0, 2)).reshape(ctx_count, TOK_CTX)
        mixed = jnp.stack([jax.random.permutation(split_keys[ctx_count + member], dealt_ids[member]) for member in range(ctx_count)])
        return mixed.reshape(GROUP_TOK).astype(jnp.int32)
    group_keys = jax.random.split(key, MICRO * GROUPS)
    return jax.vmap(one_group)(group_keys).reshape(MICRO, GROUPS, GROUP_TOK).astype(jnp.int32)


def with_ends(array, key, low, largest):
    shape = array.shape
    index_at = [jax.random.randint(jax.random.fold_in(key, axis), (), 0, shape[axis]) for axis in range(len(shape))]
    array = array.at[tuple(index_at)].set(low)
    longest = shape.index(max(shape))
    index_at[longest] = (index_at[longest] + 1) % shape[longest]
    return array.at[tuple(index_at)].set(largest)


def block_levels(own_key, dims, shards, least, largest):
    level, own = 1.0, jax.random.fold_in(own_key, 6)
    for dim, parts in shards:
        heights = jnp.exp(jax.random.uniform(jax.random.fold_in(own, dim), (parts,), jnp.float32, least / len(shards), largest / len(shards)))
        level = level * jnp.repeat(heights, dims[dim] // parts).reshape([-1 if axis == dim else 1 for axis in range(len(dims))])
    return level


def profile(count, total, limit, skew):
    weights = [(1 << 20) // math.isqrt(standing ** skew) + 1 for standing in range(2, count + 1)]
    rest, counts = total - limit - (count - 1), [1] * (count - 1)
    while rest > 0:
        candidates = [i for i in range(count - 1) if counts[i] < limit]
        pool, budget = sum([weights[i] for i in candidates]), rest
        for i in candidates:
            addition = min(limit - counts[i], max(1, budget * weights[i] // pool), rest)
            counts[i] = counts[i] + addition
            rest = rest - addition
    return np.array([limit] + counts)


def uneven_parts(key, count, total, reach, slope):
    if count == 2:
        one = jax.random.randint(key, (), max(1, total - reach), min(reach, total - 1) + 1)
        return jnp.stack([one, total - one])
    tallies = jnp.asarray(profile(count, total, reach, slope), jnp.int32)
    twos = (count - 1) // 2
    giver, taker = tallies[1:1 + 2 * twos:2], tallies[2:2 + 2 * twos:2]
    slack = jnp.minimum(giver - 1, reach - taker)
    moved = jax.random.randint(jax.random.fold_in(key, 1), (twos,), 0, 1 << 20) % (slack + 1)
    tallies = tallies.at[1:1 + 2 * twos:2].set(giver - moved).at[2:2 + 2 * twos:2].set(taker + moved)
    return tallies[jax.random.permutation(jax.random.fold_in(key, 2), count)]


def gaussian(stream_key, dims, scale, reach, cuts=(), held_as=jnp.bfloat16):
    drawn = scale * jax.random.normal(stream_key, dims, jnp.float32)
    if cuts:
        drawn = drawn * block_levels(stream_key, dims, cuts, -0.22, 0.18)
    return jnp.clip(drawn, -reach, reach).astype(held_as)


def setup_inputs(seed: int = 0) -> dict:
    key_of = jax.random.split(jax.random.key(seed), 17)
    hidden = gaussian(key_of[0], (MICRO, TOKENS, D), 1.0, 6.0, ((1, 16),))
    cotangent = gaussian(key_of[1], (MICRO, TOKENS, D), 1.0, 6.0, ((1, 16),))
    lengths = jax.vmap(lambda own: uneven_parts(own, NSEQ, GROUP_TOK, SEQ_MOST, 2))(jax.random.split(key_of[2], MICRO * GROUPS)).reshape((MICRO, GROUPS, NSEQ)).astype(jnp.int32)
    dealing = draw_dealing(jax.random.fold_in(key_of[16], 71), 0)
    keep_flags = with_ends((jax.random.randint(key_of[4], (MICRO, GROUPS, GROUP_TOK), 0, 4) < 3).astype(jnp.int32), jax.random.fold_in(key_of[4], 1), 0, 1)
    norm1_gain = jnp.clip(1.0 + 0.15 * jax.random.normal(key_of[5], (D,), jnp.float32), 0.25, 1.75).astype(jnp.bfloat16)
    w_query = gaussian(key_of[6], (D, HEADS * HEAD), (16 * D) ** -0.5, 0.0390625, ((0, 4), (1, 2)))
    w_key = gaussian(key_of[7], (D, HEADS * HEAD), D ** -0.5, 0.15625, ((0, 4), (1, 2)))
    w_value = gaussian(key_of[8], (D, HEADS * HEAD), D ** -0.5, 0.15625, ((0, 4), (1, 2)))
    w_out = gaussian(key_of[9], (HEADS * HEAD, D), (max(HEADS * HEAD // 64, 1)) ** -0.5, 2.5, ((0, 2), (1, 4)))
    rel_table = gaussian(key_of[10], (BUCKETS, HEADS), 1.0, 4.0, ((1, 2),))
    del_weight = gaussian(key_of[11], (D,), D ** -0.5, 0.15625, ((0, 4),))
    norm2_gain = jnp.clip(1.0 + 0.15 * jax.random.normal(key_of[12], (D,), jnp.float32), 0.25, 1.75).astype(jnp.bfloat16)
    w_gate = gaussian(key_of[13], (D, FF), D ** -0.5, 0.15625, ((0, 4), (1, 2)))
    w_up = gaussian(key_of[14], (D, FF), D ** -0.5, 0.15625, ((0, 4), (1, 2)))
    w_down = gaussian(key_of[15], (FF, D), FF ** -0.5, 0.09375, ((0, 2), (1, 4)))
    return dict(hidden=hidden, cotangent=cotangent, lengths=lengths, dealing=dealing, keep_flags=keep_flags, norm1_gain=norm1_gain, w_query=w_query, w_key=w_key, w_value=w_value, w_out=w_out, rel_table=rel_table, del_weight=del_weight, norm2_gain=norm2_gain, w_gate=w_gate, w_up=w_up, w_down=w_down)


@jax.custom_vjp
def low(v):
    return lax.optimization_barrier(v.astype(jnp.bfloat16)).astype(jnp.float32)

@jax.custom_vjp
def low_back(v):
    return v

def low_keep(v):
    return (low(v), None)

def low_pass(kept, grad):
    return (grad,)

def back_keep(v):
    return (v, None)

def back_low(kept, grad):
    return (low(grad),)
low.defvjp(low_keep, low_pass)
low_back.defvjp(back_keep, back_low)
epsilon = 1e-06
gate_scale = 4.0
masked_fill = -1e+30
highest = lax.Precision.HIGHEST

def product(left_side, right_side):
    return jnp.dot(left_side, right_side, precision=highest, preferred_element_type=jnp.float32)

def rms_scale(values, gain):
    return values * lax.rsqrt(lax.optimization_barrier(jnp.mean(values * values, axis=-1, keepdims=True)) + epsilon) * gain

def gelu_tanh(values):
    return jax.nn.gelu(values, approximate=True)

def bucket_of(relative):
    half_count = BUCKETS // 2
    exact_count = half_count // 2
    distance = jnp.abs(relative).astype(jnp.int32)
    ratio_bits = math.log2(MAX_DIST / exact_count)
    far_bucket = jnp.full(distance.shape, exact_count, jnp.int32)
    for level in range(1, half_count - exact_count):
        border = math.ceil(exact_count * 2.0 ** (level * ratio_bits / (half_count - exact_count)))
        far_bucket = far_bucket + (distance >= border).astype(jnp.int32)
    chosen = jnp.where(distance < exact_count, distance, far_bucket)
    return (chosen + half_count * (relative > 0).astype(jnp.int32)).astype(jnp.int32)

def seq_layout(lengths_row, places):
    lengths_row = lengths_row.astype(jnp.int32)
    seq_ends = jnp.cumsum(lengths_row).astype(jnp.int32)
    passed = (places[:, None] >= seq_ends[None, :]).astype(jnp.int32)
    segment = lax.optimization_barrier(jnp.sum(passed, axis=1)).astype(jnp.int32)
    position = (places - lax.optimization_barrier(jnp.sum(passed * lengths_row[None, :], axis=1))).astype(jnp.int32)
    return (segment, position)

def attend_block(query_block, query_segment, query_position, query_index, keys_all, values_all, gates_all, segment, position, keep_tokens, bias_table):
    key_index = jnp.arange(keys_all.shape[0], dtype=jnp.int32)
    query_heads = query_block.reshape(query_block.shape[0], HEADS, HEAD)
    key_heads = keys_all.reshape(keys_all.shape[0], HEADS, HEAD)
    value_heads = values_all.reshape(values_all.shape[0], HEADS, HEAD)
    raw_scores = jnp.einsum('qhe,khe->qkh', query_heads, key_heads, precision=highest)
    bucket = bucket_of(position[None, :] - query_position[:, None])
    onehot = (bucket[:, :, None] == jnp.arange(BUCKETS, dtype=jnp.int32)[None, None, :]).astype(jnp.float32)
    bias_term = jnp.einsum('qkb,bh->qkh', onehot, bias_table, precision=highest)
    scores = low_back(raw_scores + bias_term + gates_all[None, :, :])
    allowed = (segment[None, :] == query_segment[:, None]) & ((keep_tokens[None, :] == 1) | (key_index[None, :] == query_index[:, None]))
    scores = jnp.where(allowed[:, :, None], scores, masked_fill)
    row_top = lax.optimization_barrier(jnp.max(scores, axis=1, keepdims=True))
    weights = jnp.exp(scores - row_top)
    probs = low(weights / lax.optimization_barrier(jnp.sum(weights, axis=1, keepdims=True)))
    mixed = jnp.einsum('qkh,khe->qhe', probs, value_heads, precision=highest)
    return mixed.reshape(query_block.shape[0], HEADS * HEAD)

def attend_group(packed, bias_table):
    queries, keys_all, values_all, gates_all, segment, position, keep_tokens = packed
    row_count = queries.shape[0]
    block_size = min(512, row_count)
    block_count = row_count // block_size
    row_index = jnp.arange(row_count, dtype=jnp.int32)

    def one_block(block_pack):
        query_block, query_segment, query_position, query_index = block_pack
        return attend_block(query_block, query_segment, query_position, query_index, keys_all, values_all, gates_all, segment, position, keep_tokens, bias_table)
    mixed = lax.map(jax.checkpoint(one_block), (queries.reshape(block_count, block_size, -1), segment.reshape(block_count, block_size), position.reshape(block_count, block_size), row_index.reshape(block_count, block_size)))
    return mixed.reshape(row_count, -1)

def group_sum(left_side, right_side, width):
    total = jnp.zeros((left_side.shape[0], right_side.shape[1]), jnp.float32)
    for group_index in range(N_TP):
        col_start = group_index * width
        total = total + low(product(left_side[:, col_start:col_start + width], right_side[col_start:col_start + width]))
    return total

def layer(inputs, params, meta):
    gain_one, query_weight, key_weight, value_weight, out_weight, bias_table, delete_weight, gain_two, gate_weight, up_weight, down_weight = params
    segment, position, keep_tokens = meta
    head_cols = HEADS * HEAD // N_TP
    unit_cols = FF // N_TP
    heads_part = HEADS // N_TP
    normed_one = low(rms_scale(inputs, gain_one))
    gate_value = -gate_scale * jax.nn.sigmoid(product(normed_one, delete_weight[:, None])[:, 0])
    gate_low = low(gate_value)
    query_parts, key_parts, value_parts, gate_parts = ([], [], [], [])
    for group_index in range(N_TP):
        col_start = group_index * head_cols
        normed_part = low_back(normed_one)
        query_parts.append(low_back(low(product(normed_part, query_weight[:, col_start:col_start + head_cols]))))
        key_parts.append(low_back(low(product(normed_part, key_weight[:, col_start:col_start + head_cols]))))
        value_parts.append(low_back(low(product(normed_part, value_weight[:, col_start:col_start + head_cols]))))
        gate_part = low_back(gate_low)
        gate_parts.append(jnp.broadcast_to(gate_part[:, None], (gate_part.shape[0], heads_part)))
    queries = jnp.concatenate(query_parts, axis=1)
    keys_all = jnp.concatenate(key_parts, axis=1)
    values_all = jnp.concatenate(value_parts, axis=1)
    gate_heads = jnp.concatenate(gate_parts, axis=1)
    attention = lax.map(partial(attend_group, bias_table=bias_table), (queries.reshape(GROUPS, GROUP_TOK, HEADS * HEAD), keys_all.reshape(GROUPS, GROUP_TOK, HEADS * HEAD), values_all.reshape(GROUPS, GROUP_TOK, HEADS * HEAD), gate_heads.reshape(GROUPS, GROUP_TOK, HEADS), segment, position, keep_tokens))
    attention = low_back(low(attention.reshape(TOKENS, HEADS * HEAD)))
    residual = inputs + low_back(group_sum(attention, out_weight, head_cols))
    normed_two = low(rms_scale(residual, gain_two))
    inner_parts = []
    for group_index in range(N_TP):
        col_start = group_index * unit_cols
        normed_part = low_back(normed_two)
        gate_proj = low_back(product(normed_part, gate_weight[:, col_start:col_start + unit_cols]))
        up_proj = low_back(product(normed_part, up_weight[:, col_start:col_start + unit_cols]))
        inner_parts.append(low(gelu_tanh(gate_proj) * up_proj))
    inner_rows = jnp.concatenate(inner_parts, axis=1)
    return (residual + low_back(group_sum(inner_rows, down_weight, unit_cols)), gate_value)

def reference(hidden, cotangent, lengths, dealing, keep_flags, norm1_gain, w_query, w_key, w_value, w_out, rel_table, del_weight, norm2_gain, w_gate, w_up, w_down):
    params = tuple((item.astype(jnp.float32) for item in (norm1_gain, w_query, w_key, w_value, w_out, rel_table, del_weight, norm2_gain, w_gate, w_up, w_down)))
    totals = tuple((jnp.zeros_like(item) for item in params))
    outs_list, gates_list, grads_list = ([], [], [])
    places = jnp.arange(GROUP_TOK, dtype=jnp.int32)
    for micro_index in range(MICRO):
        dealt_ids = dealing[micro_index].astype(jnp.int32)

        def to_tokens(rows_in):

            def place_one(group_rows, group_order):
                return jnp.zeros_like(group_rows).at[group_order].set(group_rows)
            return jax.vmap(place_one)(rows_in, dealt_ids)
        inputs = to_tokens(hidden[micro_index].astype(jnp.float32).reshape(GROUPS, GROUP_TOK, D)).reshape(TOKENS, D)
        cot_tokens = to_tokens(cotangent[micro_index].astype(jnp.float32).reshape(GROUPS, GROUP_TOK, D)).reshape(TOKENS, D)
        keep_tokens = to_tokens(keep_flags[micro_index].astype(jnp.int32))

        def layout_one(lengths_row):
            return seq_layout(lengths_row, places)
        segment, position = jax.vmap(layout_one)(lengths[micro_index])

        def forward(layer_in, *weights):
            return layer(layer_in, weights, (segment, position, keep_tokens))
        result, back_fn, gate_value = jax.vjp(forward, inputs, *params, has_aux=True)
        grads = back_fn(cot_tokens)
        outs_list.append(result.astype(jnp.bfloat16))
        gates_list.append(gate_value.astype(jnp.bfloat16))
        grads_list.append(grads[0].astype(jnp.bfloat16))
        totals = tuple((total + grad for total, grad in zip(totals, grads[1:])))
    return (jnp.stack(outs_list), jnp.stack(gates_list), jnp.stack(grads_list), totals[0], totals[1], totals[2], totals[3], totals[4], totals[5], totals[6], totals[7], totals[8], totals[9], totals[10])
```

```python
import math

import numpy as np

import jax
import jax.numpy as jnp
from jax import lax
from jax.experimental import pallas as pl
from jax.experimental.pallas import tpu as pltpu
from jax.sharding import Mesh, PartitionSpec as P

BUCKETS = 32
MAX_DIST = 128
EPS = 1e-06
FILL = -1e30
BF = jnp.bfloat16
F32 = jnp.float32
SWAP = [(0, 1), (1, 0)]
SPAN = 1024
QB = 128


def bucket_np(relative):
    half_count = BUCKETS // 2
    exact_count = half_count // 2
    distance = np.abs(relative)
    ratio_bits = math.log2(MAX_DIST / exact_count)
    far = np.full(distance.shape, exact_count, np.int32)
    for level in range(1, half_count - exact_count):
        border = math.ceil(exact_count * 2.0 ** (level * ratio_bits / (half_count - exact_count)))
        far = far + (distance >= border).astype(np.int32)
    chosen = np.where(distance < exact_count, distance, far)
    return chosen + half_count * (relative > 0).astype(np.int32)


def span_onehot():
    k = np.arange(SPAN)
    d = np.where(k < SPAN // 2, k, k - SPAN)
    return (bucket_np(d)[:, None] == np.arange(BUCKETS)[None, :]).astype(np.float32)


def allowed_block(lens_ref, kf_ref, b, rows):
    e1 = lens_ref[0, 0]
    e2 = e1 + lens_ref[0, 1]
    tj = lax.broadcasted_iota(jnp.int32, (1, rows), 1)
    ti = lax.broadcasted_iota(jnp.int32, (QB, 1), 0) + b * QB
    sj = (tj >= e1).astype(jnp.int32) + (tj >= e2).astype(jnp.int32)
    si = (ti >= e1).astype(jnp.int32) + (ti >= e2).astype(jnp.int32)
    keep = kf_ref[...] == 1
    return (si == sj) & (keep | (ti == tj))


def window(full, b, rows):
    if b == 0:
        return full[:, :rows]
    return jnp.concatenate([full[:, SPAN - QB * b :], full[:, : rows - QB * b]], axis=1)


def toeplitz(vb_ref, h):
    row = jnp.broadcast_to(vb_ref[h : h + 1, :], (QB, SPAN))
    return pltpu.roll(row, 0, 1, stride=1, stride_axis=0)


def dot_t(a, b):
    return lax.dot_general(a, b, (((1,), (1,)), ((), ())), preferred_element_type=F32)


def dot_n(a, b):
    return lax.dot_general(a, b, (((1,), (0,)), ((), ())), preferred_element_type=F32)


def dot_0(a, b):
    return lax.dot_general(a, b, (((0,), (0,)), ((), ())), preferred_element_type=F32)


def probs(q, k, bias, gate, allowed):
    s = dot_t(q, k) + bias + gate
    s = jnp.where(allowed, s, FILL)
    e = jnp.exp(s - jnp.max(s, axis=1, keepdims=True))
    return e / jnp.sum(e, axis=1, keepdims=True)


def attn_fwd_kernel(heads, hw, lens_ref, qkv_ref, gate_ref, kf_ref, vb_ref, o_ref):
    rows = qkv_ref.shape[0]
    c = heads * hw
    gate = gate_ref[...]
    masks = [allowed_block(lens_ref, kf_ref, b, rows) for b in range(rows // QB)]
    for h in range(heads):
        full = toeplitz(vb_ref, h)
        k = qkv_ref[:, c + h * hw : c + (h + 1) * hw]
        v = qkv_ref[:, 2 * c + h * hw : 2 * c + (h + 1) * hw]
        for b in range(rows // QB):
            q = qkv_ref[b * QB : (b + 1) * QB, h * hw : (h + 1) * hw]
            p = probs(q, k, window(full, b, rows), gate, masks[b])
            o_ref[b * QB : (b + 1) * QB, h * hw : (h + 1) * hw] = dot_n(p.astype(BF), v).astype(BF)


def attn_bwd_kernel(heads, hw, lens_ref, qkv_ref, do_ref, gate_ref, kf_ref, vb_ref, g_ref, t_ref, ds_ref, pl_ref, acc_ref):
    rows = qkv_ref.shape[0]
    c = heads * hw
    gate = gate_ref[...]
    masks = [allowed_block(lens_ref, kf_ref, b, rows) for b in range(rows // QB)]
    ones = jnp.ones((rows, hw), BF)
    dgate = jnp.zeros((rows, hw), F32)
    t_ref[...] = jnp.zeros_like(t_ref)
    for h in range(heads):
        full = toeplitz(vb_ref, h)
        sl = slice(h * hw, (h + 1) * hw)
        q_all = qkv_ref[:, sl]
        k = qkv_ref[:, c + h * hw : c + (h + 1) * hw]
        v = qkv_ref[:, 2 * c + h * hw : 2 * c + (h + 1) * hw]
        do_all = do_ref[:, sl]
        acc_ref[...] = jnp.zeros_like(acc_ref)
        for b in range(rows // QB):
            rs = slice(b * QB, (b + 1) * QB)
            p = probs(qkv_ref[rs, sl], k, window(full, b, rows), gate, masks[b])
            dp = dot_t(do_ref[rs, sl], v)
            ds = (p * (dp - jnp.sum(p * dp, axis=1, keepdims=True))).astype(BF)
            ds_ref[rs, :] = ds
            pl_ref[rs, :] = p.astype(BF)
            wide = ds.astype(F32)
            if b == 0:
                acc_ref[:, :rows] += wide
            else:
                acc_ref[:, SPAN - QB * b :] += wide[:, : QB * b]
                acc_ref[:, : rows - QB * b] += wide[:, QB * b :]
        ds_all = ds_ref[...]
        g_ref[:, sl] = dot_n(ds_all, k).astype(BF)
        g_ref[:, c + h * hw : c + (h + 1) * hw] = dot_0(ds_all, q_all).astype(BF)
        g_ref[:, 2 * c + h * hw : 2 * c + (h + 1) * hw] = dot_0(pl_ref[...], do_all).astype(BF)
        dgate = dgate + dot_0(ds_all, ones)
        a = acc_ref[...]
        half = QB // 2
        while half >= 8:
            low = a[half:, :]
            a = a[:half, :] + pltpu.roll(low, SPAN - half, 1)
            half //= 2
        tot = a[0:1, :]
        for i in range(1, 8):
            tot = tot + pltpu.roll(a[i : i + 1, :], SPAN - i, 1)
        t_ref[h : h + 1, :] = tot
    g_ref[:, 3 * c : 3 * c + hw] = dgate.astype(BF)


SMEM_SPEC = pl.BlockSpec(memory_space=pltpu.SMEM)
VMEM_SPEC = pl.BlockSpec(memory_space=pltpu.VMEM)


def attn_fwd(heads, hw, lens, qkv, gate, kf, vb):
    rows = qkv.shape[0]
    return pl.pallas_call(
        lambda *refs: attn_fwd_kernel(heads, hw, *refs),
        out_shape=jax.ShapeDtypeStruct((rows, heads * hw), BF),
        in_specs=[SMEM_SPEC] + [VMEM_SPEC] * 4,
        out_specs=VMEM_SPEC,
        compiler_params=pltpu.CompilerParams(vmem_limit_bytes=48 * 2**20),
        cost_estimate=pl.CostEstimate(
            flops=4 * rows * rows * heads * hw, bytes_accessed=2 * rows * heads * hw * 4, transcendentals=rows * rows * heads
        ),
        name="attn_f",
    )(lens, qkv, gate, kf, vb)


def attn_bwd(heads, hw, lens, qkv, do, gate, kf, vb):
    rows = qkv.shape[0]
    return pl.pallas_call(
        lambda *refs: attn_bwd_kernel(heads, hw, *refs),
        out_shape=(
            jax.ShapeDtypeStruct((rows, (3 * heads + 1) * hw), BF),
            jax.ShapeDtypeStruct((8, SPAN), F32),
        ),
        in_specs=[SMEM_SPEC] + [VMEM_SPEC] * 5,
        out_specs=(VMEM_SPEC, VMEM_SPEC),
        scratch_shapes=[
            pltpu.VMEM((rows, rows), BF),
            pltpu.VMEM((rows, rows), BF),
            pltpu.VMEM((QB, SPAN), F32),
        ],
        compiler_params=pltpu.CompilerParams(vmem_limit_bytes=48 * 2**20),
        cost_estimate=pl.CostEstimate(
            flops=10 * rows * rows * heads * hw, bytes_accessed=2 * rows * heads * hw * 8, transcendentals=rows * rows * heads
        ),
        name="attn_b",
    )(lens, qkv, do, gate, kf, vb)


def mm(a, b):
    return jnp.dot(a, b, preferred_element_type=F32)


def mm_t(a, b):
    return lax.dot_general(a, b, (((1,), (1,)), ((), ())), preferred_element_type=F32)


def mm_0(a, b):
    return lax.dot_general(a, b, (((0,), (0,)), ((), ())), preferred_element_type=F32)


def pick(array, index, axis=0):
    return lax.dynamic_index_in_dim(array, index, axis, keepdims=False)


def cross(block, step):
    if step & 1:
        if step & 2:
            return lax.ppermute(block, ("cx", "core"), [(0, 3), (1, 2), (2, 1), (3, 0)])
        return lax.ppermute(block, "core", SWAP)
    return lax.ppermute(block, "cx", SWAP)


def norm_back(values, gain, cot, r):
    u = gain * cot
    return r * u - values * (r * r * r) * jnp.mean(values * u, axis=-1, keepdims=True), jnp.sum(cot * values * r, axis=0)


def scatter_dp(part, count, rank):
    if count <= 4:
        total = pick(part, rank).astype(F32)
        for k in range(1, count):
            sent = pick(part, lax.rem(rank + k, count))
            total = total + lax.ppermute(sent, "dp", [(i, (i + k) % count) for i in range(count)]).astype(F32)
        return total
    flat = part.reshape((-1,) + part.shape[2:])
    return lax.psum_scatter(flat, "dp", scatter_dimension=0, tiled=True).astype(F32)


def reduce_x_dp(grad, count, rank, cx):
    rows = grad.shape[0] // count
    half = rows // 2
    parts = grad.reshape(count, 2, half, grad.shape[1])
    got = lax.ppermute(pick(parts, 1 - cx, 1), "cx", SWAP)
    mine = (pick(parts, cx, 1).astype(F32) + got.astype(F32)).astype(BF)
    own = scatter_dp(mine, count, rank).astype(BF)
    other = lax.ppermute(own, "cx", SWAP)
    return jnp.concatenate([jnp.where(cx == 0, own, other), jnp.where(cx == 0, other, own)], axis=0)


def both_cores(part, core):
    other = lax.ppermute(part, "core", SWAP)
    return jnp.where(core == 0, part, other), jnp.where(core == 0, other, part)


def body(
    hidden,
    cotangent,
    lengths,
    dealing,
    keep_flags,
    norm1_gain,
    w_query,
    w_key,
    w_value,
    w_out,
    rel_table,
    del_weight,
    norm2_gain,
    w_gate,
    w_up,
    w_down,
):
    count = lax.axis_size("dp")
    rank = lax.axis_index("dp")
    cx = lax.axis_index("cx")
    core = lax.axis_index("core")
    tp = lax.axis_index("tp")
    ctx = cx * 2 + core
    local = hidden.shape[1]
    width = hidden.shape[2]
    rows = local * 4
    heads = rel_table.shape[1]
    cols = w_query.shape[1]
    hw = cols // heads
    shard = w_query.shape[0]
    half = shard // 2
    units = w_gate.shape[1] // 2

    vectors = jnp.stack([norm1_gain, del_weight, norm2_gain], axis=1)
    small = jnp.concatenate(
        [w_query, w_key, w_value, w_out.T, jnp.pad(vectors, ((0, 0), (0, 125)))], axis=1
    )
    piece = pick(small.reshape(2, half, -1), cx)
    att = lax.all_gather(piece, ("dp", "cx"), axis=0, tiled=True)
    w_qkv = att[:, : 3 * cols]
    w_out_t = att[:, 3 * cols : 4 * cols]
    vecs = att[:, 4 * cols : 4 * cols + 3].astype(F32).T
    gain1, delw, gain2 = vecs[0:1], vecs[1:2], vecs[2:3]

    order = jnp.arange(4) ^ ctx
    order = jnp.stack([ctx, ctx ^ 1, ctx ^ 2, ctx ^ 3])
    own_deal = pick(dealing, ctx)[0]
    deal = jnp.take(own_deal.reshape(4, local), order, axis=0).reshape(rows)
    keep = pick(keep_flags, ctx)[0]
    keep = jnp.take(keep.reshape(4, local), order, axis=0).reshape(rows)
    lens = pick(lengths, ctx)
    hit = deal[None, :] == jnp.arange(rows, dtype=jnp.int32)[:, None]
    place = hit.astype(BF)
    kf = jnp.sum(jnp.where(hit, keep[None, :], 0), axis=1)[None, :]

    def gather_tokens(array):
        blocks = [pick(array, ctx)]
        for k in range(1, 4):
            blocks.append(cross(pick(array, ctx ^ k), k))
        return mm(place, jnp.concatenate(blocks, axis=0)).astype(BF)

    x_low = gather_tokens(hidden)
    cot_low = gather_tokens(cotangent)
    x = x_low.astype(F32)

    def col_piece(w):
        return lax.dynamic_slice(w, (cx * half, core * units), (half, units))

    wd_piece = lax.dynamic_slice(w_down, (core * units, cx * half), (units, half)).T
    wg_full = lax.all_gather(col_piece(w_gate), ("dp", "cx"), axis=0, tiled=True)
    wu_full = lax.all_gather(col_piece(w_up), ("dp", "cx"), axis=0, tiled=True)
    wd_full = lax.all_gather(wd_piece, ("dp", "cx"), axis=0, tiled=True)

    r1 = lax.rsqrt(jnp.mean(x * x, axis=-1, keepdims=True) + EPS)
    n1 = (x * r1 * gain1).astype(BF)
    z = jnp.sum(n1.astype(F32) * delw, axis=1, keepdims=True)
    sig = jax.nn.sigmoid(z)
    gate_low = (-4.0 * sig).astype(BF)
    qkv = mm(n1, w_qkv).astype(BF)
    onehot = span_onehot()
    vb = jnp.pad(mm(rel_table.T, jnp.asarray(onehot.T, BF)), ((0, 8 - heads), (0, 0)))
    gate_row = gate_low.astype(F32).reshape(1, rows)
    attn = attn_fwd(heads, hw, lens, qkv, gate_row, kf, vb)
    attn_other = lax.ppermute(attn, "tp", SWAP)
    w_out_other = lax.ppermute(w_out_t, "tp", SWAP)
    w_qkv_other = lax.ppermute(w_qkv, "tp", SWAP)
    branch = mm_t(attn, w_out_t).astype(BF).astype(F32) + mm_t(attn_other, w_out_other).astype(BF).astype(F32)
    h1 = x + branch
    r2 = lax.rsqrt(jnp.mean(h1 * h1, axis=-1, keepdims=True) + EPS)
    n2_own = (h1 * r2 * gain2).astype(BF)

    n2 = jnp.concatenate([n2_own, lax.ppermute(n2_own, "core", SWAP)], axis=0)
    cot = jnp.concatenate([cot_low, lax.ppermute(cot_low, "core", SWAP)], axis=0)
    ga = mm(n2, wg_full)
    up = mm(n2, wu_full)
    dinner = mm(cot, wd_full)
    act, act_back = jax.vjp(lambda a: jax.nn.gelu(a, approximate=True), ga)
    inner = (act * up).astype(BF)
    dga = act_back(dinner * up)[0].astype(BF)
    dup = (dinner * act).astype(BF)
    dn2_part = mm_t(dga, wg_full) + mm_t(dup, wu_full)
    dn2_half = (dn2_part[:rows] + lax.ppermute(dn2_part[rows:].astype(BF), "core", SWAP).astype(F32)).astype(BF)
    dn2 = dn2_half.astype(F32) + lax.ppermute(dn2_half, "tp", SWAP).astype(F32)
    out_part = mm_t(inner, wd_full)
    out_half = (out_part[:rows] + lax.ppermute(out_part[rows:].astype(BF), "core", SWAP).astype(F32)).astype(BF)
    out = h1 + out_half.astype(F32) + lax.ppermute(out_half, "tp", SWAP).astype(F32)

    g_down = mm_0(cot, inner).astype(BF)
    g_gate = mm_0(n2, dga).astype(BF)
    g_up = mm_0(n2, dup).astype(BF)

    def finish(grad):
        return both_cores(reduce_x_dp(grad, count, rank, cx), core)

    g_down = jnp.concatenate(finish(g_down), axis=1).astype(F32).T
    g_gate = jnp.concatenate(finish(g_gate), axis=1).astype(F32)
    g_up = jnp.concatenate(finish(g_up), axis=1).astype(F32)

    back2, g_gain2 = norm_back(h1, gain2, dn2, r2)
    dh1 = cot_low.astype(F32) + back2
    dhl = dh1.astype(BF)
    dattn = mm(dhl, w_out_t).astype(BF)
    g_out = mm_0(dhl, attn)
    slab, diag = attn_bwd(heads, hw, lens, qkv, dattn, gate_row, kf, vb)
    slab_other = lax.ppermute(slab, "tp", SWAP)
    g_qkv = mm_0(n1, slab[:, : 3 * cols])
    dgate = slab[:, 3 * cols : 3 * cols + 1].astype(F32) + slab_other[:, 3 * cols : 3 * cols + 1].astype(F32)
    dz = dgate * -4.0 * sig * (1.0 - sig)
    g_del = jnp.sum(n1.astype(F32) * dz, axis=0)
    dn1 = (
        mm_t(slab[:, : 3 * cols], w_qkv).astype(BF).astype(F32)
        + mm_t(slab_other[:, : 3 * cols], w_qkv_other).astype(BF).astype(F32)
        + dz * delw
    )
    back1, g_gain1 = norm_back(x, gain1, dn1, r1)
    dx = (dh1 + back1).astype(BF)

    g_vec = jnp.pad(jnp.stack([g_gain1, g_del, g_gain2], axis=1), ((0, 0), (0, 125)))
    both = jnp.stack(
        [
            jnp.concatenate([g_qkv[:, : 2 * cols], g_vec], axis=1),
            jnp.concatenate([g_qkv[:, 2 * cols :], g_out, jnp.zeros_like(g_vec)], axis=1),
        ]
    ).astype(BF)
    got = lax.ppermute(pick(both, 1 - core), "core", SWAP)
    mine = (pick(both, core).astype(F32) + got.astype(F32)).astype(BF)
    first, second = both_cores(reduce_x_dp(mine, count, rank, cx), core)
    first = first.astype(F32)
    second = second.astype(F32)
    table = lax.psum(
        lax.dot_general(
            jnp.asarray(onehot), diag[:heads], (((0,), (1,)), ((), ())), precision=lax.Precision.HIGHEST
        ),
        ("dp", "cx", "core"),
    )

    filler = jnp.zeros((rows, 63), BF)
    packed = jnp.concatenate([out.astype(BF), gate_low, filler], axis=1)

    def deal_out(array, cols_out):
        blocks = array.reshape(4, local, array.shape[1])
        result = jnp.zeros((4, local, array.shape[1]), BF)
        for k in range(4):
            block = pick(blocks, ctx ^ k)
            got = block if k == 0 else cross(block, k)
            result = lax.dynamic_update_slice(result, got[None], (ctx ^ k, 0, 0))
        return result

    packed = deal_out(packed, width)
    hidden_grad = deal_out(dx, width)
    return (
        packed[:, :, :width],
        packed[:, :, width],
        hidden_grad,
        first[:, 2 * cols],
        first[:, :cols],
        first[:, cols : 2 * cols],
        second[:, :cols],
        second[:, cols : 2 * cols].T,
        table,
        first[:, 2 * cols + 1],
        first[:, 2 * cols + 2],
        g_gate,
        g_up,
        g_down,
    )


def solution(mesh):
    dp, ctx, tp = (mesh.shape[name] for name in ("dp", "ctx", "tp"))
    split = Mesh(mesh.devices.reshape(dp, 2, ctx // 2, tp), ("dp", "cx", "core", "tp"))
    tokens = P(None, ("dp", "cx", "core"), None)
    in_specs = (
        tokens,
        tokens,
        P(None, "dp", None),
        P(None, "dp", None),
        P(None, "dp", None),
        P("dp"),
        P("dp", "tp"),
        P("dp", "tp"),
        P("dp", "tp"),
        P("tp", "dp"),
        P(None, "tp"),
        P("dp"),
        P("dp"),
        P("dp", "tp"),
        P("dp", "tp"),
        P("tp", "dp"),
    )
    out_specs = (
        tokens,
        P(None, ("dp", "cx", "core")),
        tokens,
        P("dp"),
        P("dp", "tp"),
        P("dp", "tp"),
        P("dp", "tp"),
        P("tp", "dp"),
        P(None, "tp"),
        P("dp"),
        P("dp"),
        P("dp", "tp"),
        P("dp", "tp"),
        P("tp", "dp"),
    )
    return jax.shard_map(body, mesh=split, in_specs=in_specs, out_specs=out_specs, check_vma=False)
```

```python
import math

import numpy as np

import jax
import jax.numpy as jnp
from jax import lax
from jax.experimental import pallas as pl
from jax.experimental.pallas import tpu as pltpu
from jax.sharding import Mesh, PartitionSpec as P

BUCKETS = 32
MAX_DIST = 128
EPS = 1e-06
FILL = -1e30
BF = jnp.bfloat16
F32 = jnp.float32
SWAP = [(0, 1), (1, 0)]
SPAN = 1024
QB = 128


def bucket_np(relative):
    half_count = BUCKETS // 2
    exact_count = half_count // 2
    distance = np.abs(relative)
    ratio_bits = math.log2(MAX_DIST / exact_count)
    far = np.full(distance.shape, exact_count, np.int32)
    for level in range(1, half_count - exact_count):
        border = math.ceil(exact_count * 2.0 ** (level * ratio_bits / (half_count - exact_count)))
        far = far + (distance >= border).astype(np.int32)
    chosen = np.where(distance < exact_count, distance, far)
    return chosen + half_count * (relative > 0).astype(np.int32)


def span_onehot():
    k = np.arange(SPAN)
    d = np.where(k < SPAN // 2, k, k - SPAN)
    return (bucket_np(d)[:, None] == np.arange(BUCKETS)[None, :]).astype(np.float32)


def dot_n(a, b):
    return lax.dot_general(a, b, (((1,), (0,)), ((), ())), preferred_element_type=F32)


def dot_t(a, b):
    return lax.dot_general(a, b, (((1,), (1,)), ((), ())), preferred_element_type=F32)


def dot_0(a, b):
    return lax.dot_general(a, b, (((0,), (0,)), ((), ())), preferred_element_type=F32)


SMEM_SPEC = pl.BlockSpec(memory_space=pltpu.SMEM)
VMEM_SPEC = pl.BlockSpec(memory_space=pltpu.VMEM)
ANY_SPEC = pl.BlockSpec(memory_space=pl.ANY)
VEC = 16
TINY = pl.CostEstimate(flops=1000, bytes_accessed=1000, transcendentals=0)


def shape(*dims, dtype=BF):
    return jax.ShapeDtypeStruct(dims, dtype)


def call(kernel, outs, args, flops, scratch=(), limit=48, name=None):
    return pl.pallas_call(
        kernel,
        out_shape=tuple(outs),
        in_specs=[SMEM_SPEC] * 2 + [VMEM_SPEC] * (len(args) - 2),
        out_specs=tuple([VMEM_SPEC] * len(outs)),
        scratch_shapes=list(scratch),
        compiler_params=pltpu.CompilerParams(vmem_limit_bytes=limit * 2**20),
        cost_estimate=TINY,
        name=name,
    )(*args)


def allowed_block(lens_ref, kf_ref, b, rows):
    e1 = lens_ref[0, 0]
    e2 = e1 + lens_ref[0, 1]
    tj = lax.broadcasted_iota(jnp.int32, (1, rows), 1)
    ti = lax.broadcasted_iota(jnp.int32, (QB, 1), 0) + b * QB
    sj = (tj >= e1).astype(jnp.int32) + (tj >= e2).astype(jnp.int32)
    si = (ti >= e1).astype(jnp.int32) + (ti >= e2).astype(jnp.int32)
    keep = kf_ref[...] == 1
    return (si == sj) & (keep | (ti == tj))


def window(full, b, rows):
    if b == 0:
        return full[:, :rows]
    return jnp.concatenate([full[:, SPAN - QB * b :], full[:, : rows - QB * b]], axis=1)


def toeplitz(vb_ref, h):
    row = jnp.broadcast_to(vb_ref[h : h + 1, :], (QB, SPAN))
    return pltpu.roll(row, 0, 1, stride=1, stride_axis=0)


def probs(q, k, bias, gate, allowed):
    s = dot_0(q, k) + bias + gate
    s = jnp.where(allowed, s, FILL)
    e = jnp.exp(s - jnp.max(s, axis=1, keepdims=True))
    return e / jnp.sum(e, axis=1, keepdims=True)


def attend(heads, hw, lens_ref, qkv_ref, gate, kf_ref, vb_ref, o_ref):
    rows = qkv_ref.shape[1]
    c = heads * hw
    masks = [allowed_block(lens_ref, kf_ref, b, rows) for b in range(rows // QB)]
    for h in range(heads):
        full = toeplitz(vb_ref, h)
        k = qkv_ref[c + h * hw : c + (h + 1) * hw, :]
        v = qkv_ref[2 * c + h * hw : 2 * c + (h + 1) * hw, :]
        for b in range(rows // QB):
            q = qkv_ref[h * hw : (h + 1) * hw, b * QB : (b + 1) * QB]
            p = probs(q, k, window(full, b, rows), gate, masks[b])
            o_ref[h * hw : (h + 1) * hw, b * QB : (b + 1) * QB] = dot_t(v, p.astype(BF)).astype(BF)


def attend_back(heads, hw, lens_ref, qkv_ref, do_ref, gate, kf_ref, vb_ref, g_ref, t_ref, ds_ref, pl_ref, acc_ref):
    rows = qkv_ref.shape[1]
    c = heads * hw
    masks = [allowed_block(lens_ref, kf_ref, b, rows) for b in range(rows // QB)]
    ones = jnp.ones((VEC, rows), BF)
    dgate = jnp.zeros((VEC, rows), F32)
    t_ref[...] = jnp.zeros_like(t_ref)
    for h in range(heads):
        full = toeplitz(vb_ref, h)
        sl = slice(h * hw, (h + 1) * hw)
        k = qkv_ref[c + h * hw : c + (h + 1) * hw, :]
        v = qkv_ref[2 * c + h * hw : 2 * c + (h + 1) * hw, :]
        acc_ref[...] = jnp.zeros_like(acc_ref)
        for b in range(rows // QB):
            rs = slice(b * QB, (b + 1) * QB)
            p = probs(qkv_ref[sl, rs], k, window(full, b, rows), gate, masks[b])
            dp = dot_0(do_ref[sl, rs], v)
            ds = (p * (dp - jnp.sum(p * dp, axis=1, keepdims=True))).astype(BF)
            ds_ref[rs, :] = ds
            pl_ref[rs, :] = p.astype(BF)
            wide = ds.astype(F32)
            if b == 0:
                acc_ref[:, :rows] += wide
            else:
                acc_ref[:, SPAN - QB * b :] += wide[:, : QB * b]
                acc_ref[:, : rows - QB * b] += wide[:, QB * b :]
        ds_all = ds_ref[...]
        g_ref[sl, :] = dot_t(k, ds_all).astype(BF)
        g_ref[c + h * hw : c + (h + 1) * hw, :] = dot_n(qkv_ref[sl, :], ds_all).astype(BF)
        g_ref[2 * c + h * hw : 2 * c + (h + 1) * hw, :] = dot_n(do_ref[sl, :], pl_ref[...]).astype(BF)
        dgate = dgate + dot_n(ones, ds_all)
        a = acc_ref[...]
        half = QB // 2
        while half >= 8:
            low = a[half:, :]
            a = a[:half, :] + pltpu.roll(low, SPAN - half, 1)
            half //= 2
        tot = a[0:1, :]
        for i in range(1, 8):
            tot = tot + pltpu.roll(a[i : i + 1, :], SPAN - i, 1)
        t_ref[h : h + 1, :] = tot
    g_ref[3 * c :, :] = dgate.astype(BF)


def spots(info_ref, array_ref):
    many, block = array_ref.shape[0], array_ref.shape[2]
    if many == 1:
        return [pl.ds(0, block)]
    return [pl.ds(pl.multiple_of((info_ref[0] ^ k) * block, VEC), block) for k in range(many)]


def spread(w0_ref, k, c, which, rows):
    pickup = (lax.broadcasted_iota(jnp.int32, (VEC, QB), 0) == which).astype(F32).astype(BF)
    block = dot_0(w0_ref[k, 2 * c :, :], pickup)
    return jnp.concatenate([block] * (rows // QB), axis=1)


def inverse_rms(values):
    return lax.rsqrt(jnp.sum(values * values, axis=0, keepdims=True) / values.shape[0] + EPS)


def sum_tokens(values):
    high = values.astype(BF)
    rest = (values - high.astype(F32)).astype(BF)
    ones = jnp.ones((8, values.shape[1]), BF)
    return dot_t(ones, high) + dot_t(ones, rest)


def enter_kernel(heads, hw, info_ref, lens_ref, x_ref, w0_ref, w1_ref, kf_ref, vb_ref, n1_ref, qkv_ref, attn_ref, aux_ref):
    rows = x_ref.shape[1]
    c = heads * hw
    x = x_ref[...].astype(F32)
    r1 = inverse_rms(x)
    qkz = jnp.zeros((2 * c + VEC, rows), F32)
    v = jnp.zeros((c, rows), F32)
    for k, spot in enumerate(spots(info_ref, w0_ref)):
        n1 = (x_ref[spot, :].astype(F32) * r1 * spread(w0_ref, k, c, 0, rows)).astype(BF)
        n1_ref[spot, :] = n1
        qkz = qkz + dot_n(w0_ref[k], n1)
        v = v + dot_n(w1_ref[k, :c, :], n1)
    qkv_ref[: 2 * c, :] = qkz[: 2 * c].astype(BF)
    qkv_ref[2 * c :, :] = v.astype(BF)
    z = qkz[2 * c + 1 : 2 * c + 2]
    gate = (-4.0 * jax.nn.sigmoid(z)).astype(BF).astype(F32)
    aux_ref[...] = jnp.concatenate([z, gate, r1, jnp.zeros((5, rows), F32)], axis=0)
    attend(heads, hw, lens_ref, qkv_ref, gate, kf_ref, vb_ref, attn_ref)


def middle_kernel(c, info_ref, lens_ref, x_ref, attn_ref, other_ref, w0_ref, w1_ref, wo_ref, aux_ref, h1_ref, n2_ref):
    rows = x_ref.shape[1]
    width = x_ref.shape[0]
    total = jnp.zeros((1, rows), F32)
    places = spots(info_ref, w0_ref)
    for k, spot in enumerate(places):
        own = dot_0(w1_ref[k, c : 2 * c, :], attn_ref[...]).astype(BF).astype(F32)
        far = dot_0(wo_ref[k, c : 2 * c, :], other_ref[...]).astype(BF).astype(F32)
        h1 = x_ref[spot, :].astype(F32) + (own + far)
        h1_ref[spot, :] = h1
        total = total + jnp.sum(h1 * h1, axis=0, keepdims=True)
    r2 = lax.rsqrt(total / width + EPS)
    for k, spot in enumerate(places):
        n2_ref[spot, :] = (h1_ref[spot, :] * r2 * spread(w0_ref, k, c, 2, rows)).astype(BF)
    n2_ref[width:, :] = jnp.broadcast_to(aux_ref[1:2, :], (VEC, rows)).astype(BF)


def back_kernel(
    heads,
    hw,
    info_ref,
    lens_ref,
    own_ref,
    other_ref,
    h1_ref,
    cot_ref,
    w0_ref,
    w1_ref,
    qkv_ref,
    attn_ref,
    aux_ref,
    kf_ref,
    vb_ref,
    dh1_ref,
    slab_ref,
    diag_ref,
    gwo_ref,
    gain_ref,
    u_ref,
    do_ref,
    ds_ref,
    pl_ref,
    acc_ref,
):
    rows = h1_ref.shape[1]
    width = h1_ref.shape[0]
    c = heads * hw
    places = spots(info_ref, w0_ref)
    r2 = inverse_rms(h1_ref[...])
    total = jnp.zeros((1, rows), F32)
    for k, spot in enumerate(places):
        dn2 = own_ref[spot, :].astype(F32) + other_ref[spot, :].astype(F32)
        u = dn2 * spread(w0_ref, k, c, 2, rows)
        h1 = h1_ref[spot, :]
        total = total + jnp.sum(h1 * u, axis=0, keepdims=True)
        u_ref[spot, :] = u
        dh1_ref[spot, :] = dn2 * h1 * r2
    gain_ref[...] = sum_tokens(dh1_ref[...])
    back = r2 * r2 * r2 * (total / width)
    dattn = jnp.zeros((c, rows), F32)
    for k, spot in enumerate(places):
        dh1 = cot_ref[0, spot, :].astype(F32) + r2 * u_ref[spot, :] - h1_ref[spot, :] * back
        dh1_ref[spot, :] = dh1
        dhl = dh1.astype(BF)
        dattn = dattn + dot_n(w1_ref[k, c : 2 * c, :], dhl)
        gwo_ref[k] = dot_t(attn_ref[...], dhl).astype(BF)
    do_ref[...] = dattn.astype(BF)
    attend_back(
        heads, hw, lens_ref, qkv_ref, do_ref, aux_ref[1:2, :], kf_ref, vb_ref, slab_ref, diag_ref, ds_ref, pl_ref, acc_ref
    )


def gatt_kernel(c, info_ref, lens_ref, slab_ref, n1_ref, gwo_ref, keep_ref, send_ref):
    first, second = (keep_ref, send_ref), (send_ref, keep_ref)
    for k, spot in enumerate(spots(info_ref, gwo_ref)):
        n1 = n1_ref[spot, :]
        qk = dot_t(slab_ref[: 2 * c, :], n1).astype(BF)
        v = dot_t(slab_ref[2 * c : 3 * c, :], n1).astype(BF)
        for core, (qk_ref, vo_ref) in enumerate((first, second)):

            @pl.when((info_ref[1] & 1) == core)
            def _():
                qk_ref[k] = qk
                vo_ref[k, :c, :] = v
                vo_ref[k, c:, :] = gwo_ref[k]


def leave_kernel(
    c,
    info_ref,
    lens_ref,
    slab_ref,
    other_ref,
    w0_ref,
    w1_ref,
    qk_ref,
    vo_ref,
    x_ref,
    dh1_ref,
    n1_ref,
    aux_ref,
    o0,
    o1,
    o2,
    o3,
    vec_ref,
    dn_ref,
    dx_ref,
):
    rows = x_ref.shape[1]
    width = x_ref.shape[0]
    places = spots(info_ref, w0_ref)
    z = aux_ref[0:1, :]
    r1 = aux_ref[2:3, :]
    sig = jax.nn.sigmoid(z)
    dgate = slab_ref[3 * c : 3 * c + 1, :].astype(F32) + other_ref[3 * c : 3 * c + 1, :].astype(F32)
    dz = dgate * (-4.0 * sig * (1.0 - sig))
    total = jnp.zeros((1, rows), F32)
    for k, spot in enumerate(places):
        own = dot_0(w0_ref[k, : 2 * c, :], slab_ref[: 2 * c, :]) + dot_0(w1_ref[k, :c, :], slab_ref[2 * c : 3 * c, :])
        far = dot_0(qk_ref[k, : 2 * c, :], other_ref[: 2 * c, :]) + dot_0(vo_ref[k, :c, :], other_ref[2 * c : 3 * c, :])
        dn = own.astype(BF).astype(F32) + far.astype(BF).astype(F32) + spread(w0_ref, k, c, 1, rows) * dz
        u = dn * spread(w0_ref, k, c, 0, rows)
        x = x_ref[spot, :].astype(F32)
        total = total + jnp.sum(x * u, axis=0, keepdims=True)
        dx_ref[spot, :] = u
        dn_ref[spot, :] = dn * x * r1
    vec_ref[0:8, :] = sum_tokens(dn_ref[...])
    vec_ref[8:16, :] = sum_tokens(n1_ref[...].astype(F32) * dz)
    back = r1 * r1 * r1 * (total / width)
    dn_ref[...] = dh1_ref[...] + r1 * dx_ref[...] - x_ref[...].astype(F32) * back
    part = rows // 4
    for k, out in enumerate((o0, o1, o2, o3)):
        at = pl.multiple_of((info_ref[1] ^ k) * part, part)
        out[...] = dn_ref[:, pl.ds(at, part)].astype(BF)


def ffn_kernel(n_pieces, shard, units, info_ref, na_ref, nb_ref, cot_ref, *refs):
    pieces = refs[:n_pieces]
    keep_ref, send_ref, inner_ref, dgu_ref, w_ref, wt_ref, n_ref, sems = refs[n_pieces:]
    step = pl.program_id(0)
    mid = pl.num_programs(0) // 2
    width = w_ref.shape[0]

    @pl.when(step == 0)
    def _():
        copies = []
        for k in range(n_pieces):
            at = pl.multiple_of((info_ref[0] ^ k) * shard, VEC) if n_pieces > 1 else 0
            copies.append(pltpu.make_async_copy(pieces[k], w_ref.at[pl.ds(at, pieces[k].shape[0])], sems.at[k]))
        for c in copies:
            c.start()
        for c in copies:
            c.wait()
        wt_ref[...] = w_ref[...].T

    @pl.when(step < mid)
    def _():
        n_ref[...] = na_ref[:width, :]

    @pl.when(step >= mid)
    def _():
        n_ref[...] = nb_ref[:width, :]

    gu = dot_n(wt_ref[: 2 * units, :], n_ref[...])
    din = dot_n(wt_ref[2 * units : 3 * units, :], cot_ref[0])
    ga = gu[:units]
    up = gu[units:]
    c0 = math.sqrt(2.0 / math.pi)
    sq = ga * ga
    th = jnp.tanh(c0 * (ga + 0.044715 * ga * sq))
    hf = 0.5 * (1.0 + th)
    act = ga * hf
    slope = hf + 0.5 * ga * (1.0 - th * th) * (c0 + 3.0 * 0.044715 * c0 * sq)
    inner_ref[...] = (act * up).astype(BF)
    dgu_ref[:units, :] = (din * up * slope).astype(BF)
    dgu_ref[units:, :] = (din * act).astype(BF)
    dn = dot_n(w_ref[:, : 2 * units], dgu_ref[...]).astype(BF)
    bf = dot_n(w_ref[:, 2 * units : 3 * units], inner_ref[...]).astype(BF)

    @pl.when(step < mid)
    def _():
        keep_ref[0] = dn
        keep_ref[1] = bf

    @pl.when(step >= mid)
    def _():
        send_ref[0] = dn
        send_ref[1] = bf


def ffn(info, na, nb, cot, base, pieces, shard, units, tile=256):
    width, rows = cot.shape[1:]
    tall = na.shape[0]
    per = rows // tile
    wide = pieces[0].shape[1]
    first = lambda i, s: (0, jnp.minimum(i, per - 1))
    second = lambda i, s: (0, jnp.maximum(i - per, 0))
    return pl.pallas_call(
        lambda *refs: ffn_kernel(len(pieces), shard, units, *refs),
        grid_spec=pltpu.PrefetchScalarGridSpec(
            num_scalar_prefetch=1,
            grid=(2 * per,),
            in_specs=[
                pl.BlockSpec((tall, tile), first),
                pl.BlockSpec((tall, tile), second),
                pl.BlockSpec((1, width, tile), lambda i, s: (base + i // per, 0, i % per)),
            ]
            + [ANY_SPEC] * len(pieces),
            out_specs=[
                pl.BlockSpec((2, width, tile), lambda i, s: (0,) + first(i, s)),
                pl.BlockSpec((2, width, tile), lambda i, s: (0,) + second(i, s)),
                pl.BlockSpec((units, tile), lambda i, s: (0, i)),
                pl.BlockSpec((2 * units, tile), lambda i, s: (0, i)),
            ],
            scratch_shapes=[
                pltpu.VMEM((width, wide), BF),
                pltpu.VMEM((wide, width), BF),
                pltpu.VMEM((width, tile), BF),
                pltpu.SemaphoreType.DMA((len(pieces),)),
            ],
        ),
        out_shape=[shape(2, width, rows), shape(2, width, rows), shape(units, 2 * rows), shape(2 * units, 2 * rows)],
        compiler_params=pltpu.CompilerParams(vmem_limit_bytes=48 * 2**20),
        cost_estimate=TINY,
        name="ffn",
    )(info, na, nb, cot, *pieces)


def wgrad_kernel(units, info_ref, n0, n1, n2, n3, cot_ref, dgu_b, dgu_a, in_b, in_a, *outs):
    rows = n0.shape[1]
    gu = dot_t(n0[...], dgu_b[:, :rows]) + dot_t(n1[...], dgu_b[:, rows:])
    gu = gu + dot_t(n2[...], dgu_a[:, :rows]) + dot_t(n3[...], dgu_a[:, rows:])
    dw = dot_t(cot_ref[0], in_b[:, :rows]) + dot_t(cot_ref[1], in_b[:, rows:])
    dw = dw + dot_t(cot_ref[2], in_a[:, :rows]) + dot_t(cot_ref[3], in_a[:, rows:])
    for k, out in enumerate(outs):

        @pl.when((len(outs) == 1) | (pl.program_id(0) == k))
        def _():
            out[:, : 2 * units] = gu.astype(BF)
            out[:, 2 * units : 3 * units] = dw.astype(BF)
            out[:, 3 * units :] = jnp.zeros((out.shape[0], out.shape[1] - 3 * units), BF)


def wgrad(info, count, ns, cot, dgu_b, dgu_a, in_b, in_a, wide):
    width, rows = cot.shape[1:]
    units = in_b.shape[0]
    tile = width // 4
    whole = lambda a: pl.BlockSpec(a.shape, lambda i, s: (0,) * a.ndim)
    at = (lambda i, s: s[0] ^ i) if count == 4 else (lambda i, s: i)
    if count == 4:
        outs = [shape(tile, wide)] * 4
        out_specs = [pl.BlockSpec((tile, wide), lambda i, s: (0, 0))] * 4
    else:
        outs = [shape(width, wide)]
        out_specs = [pl.BlockSpec((tile, wide), lambda i, s: (i, 0))]
    return pl.pallas_call(
        lambda *refs: wgrad_kernel(units, *refs),
        grid_spec=pltpu.PrefetchScalarGridSpec(
            num_scalar_prefetch=1,
            grid=(4,),
            in_specs=[pl.BlockSpec((tile, rows), lambda i, s: (at(i, s), 0))] * 4
            + [pl.BlockSpec((4, tile, rows), lambda i, s: (0, at(i, s), 0))]
            + [whole(dgu_b), whole(dgu_a), whole(in_b), whole(in_a)],
            out_specs=out_specs,
        ),
        out_shape=outs,
        compiler_params=pltpu.CompilerParams(vmem_limit_bytes=48 * 2**20),
        cost_estimate=TINY,
        name="wgrad",
    )(info, *ns, cot, dgu_b, dgu_a, in_b, in_a)


def place_kernel(info_ref, deal_ref, *refs):
    *blocks, out_ref = refs
    rows = out_ref.shape[2]
    hit = lax.broadcasted_iota(jnp.int32, (rows, rows), 0) == deal_ref[0]
    if len(blocks) == 1:
        blocks = [blocks[0].at[i] for i in range(4)]
    blocks = jnp.concatenate([b[0] for b in blocks], axis=1)
    out_ref[0] = dot_t(blocks, hit.astype(F32).astype(BF)).astype(BF)


def place_tokens(info, deal, blocks):
    many, _, rows = deal.shape
    width, local = blocks[0].shape[-2:]
    if many == 1:
        specs = [pl.BlockSpec((1, width, local), lambda j, s: (0, 0, 0))] * 4
        order = lambda j, s: (0, 0, 0)
    else:
        specs = [pl.BlockSpec((4, 1, width, local), lambda j, s: (0, s[1] ^ j, 0, 0))]
        order = lambda j, s: (s[1] ^ j, 0, 0)
    return pl.pallas_call(
        place_kernel,
        grid_spec=pltpu.PrefetchScalarGridSpec(
            num_scalar_prefetch=1,
            grid=(many,),
            in_specs=[pl.BlockSpec((1, 1, rows), order)] + specs,
            out_specs=pl.BlockSpec((1, width, rows), lambda j, s: (j, 0, 0)),
        ),
        out_shape=shape(many, width, rows),
        compiler_params=pltpu.CompilerParams(vmem_limit_bytes=48 * 2**20),
        cost_estimate=TINY,
        name="place",
    )(info, deal, *blocks)


def pick(array, index, axis=0):
    return lax.dynamic_index_in_dim(array, index, axis, keepdims=False)


def swap(block, axis):
    return lax.ppermute(block, axis, SWAP)


def cross(block, step):
    if step == 3:
        return lax.ppermute(block, ("cx", "core"), [(0, 3), (1, 2), (2, 1), (3, 0)])
    return swap(block, "core" if step == 1 else "cx")


NEAR = [(0, 1), (1, 0), (2, 3), (3, 2)]
FAR = [(0, 2), (2, 0), (1, 3), (3, 1)]
MID = [(1, 2), (2, 1)]


def gather_dp(piece, count, rank, axis):
    if count != 4:
        return [lax.all_gather(piece, "dp", axis=axis, tiled=True)]
    near = lax.ppermute(piece, "dp", NEAR)
    far = lax.ppermute(piece, "dp", FAR)
    mid = lax.ppermute(piece, "dp", MID)
    passed = lax.ppermute(far, "dp", [(1, 0), (2, 3)])
    return [piece, near, far, jnp.where((rank == 1) | (rank == 2), mid, passed)]


def scatter_dp(parts, axis):
    if len(parts) == 1:
        return lax.psum_scatter(parts[0], "dp", scatter_dimension=axis, tiled=True).astype(F32)
    early = lax.ppermute(parts[3], "dp", [(0, 1), (3, 2)])
    near = lax.ppermute(parts[1], "dp", NEAR)
    mid = lax.ppermute(parts[3], "dp", MID)
    far = lax.ppermute((parts[2].astype(F32) + early.astype(F32)).astype(BF), "dp", FAR)
    return parts[0].astype(F32) + near.astype(F32) + mid.astype(F32) + far.astype(F32)


def in_order(first, second, index):
    return jnp.where(index == 0, first, second), jnp.where(index == 0, second, first)


def xor_list(items, cx, core):
    a, b, c, d = items
    a, b = in_order(a, b, core)
    c, d = in_order(c, d, core)
    (a, c), (b, d) = in_order(a, c, cx), in_order(b, d, cx)
    return [a, b, c, d]


def xor_order(array, axis, cx, core):
    return jnp.concatenate(xor_list([lax.slice_in_dim(array, i, i + 1, axis=axis) for i in range(4)], cx, core), axis)


def body(
    hidden,
    cotangent,
    lengths,
    dealing,
    keep_flags,
    norm1_gain,
    w_query,
    w_key,
    w_value,
    w_out,
    rel_table,
    del_weight,
    norm2_gain,
    w_gate,
    w_up,
    w_down,
):
    count = lax.axis_size("dp")
    rank = lax.axis_index("dp")
    cx = lax.axis_index("cx")
    core = lax.axis_index("core")
    ctx = cx * 2 + core
    local = hidden.shape[1]
    width = hidden.shape[2]
    rows = local * 4
    heads = rel_table.shape[1]
    cols = w_query.shape[1]
    hw = cols // heads
    shard = w_query.shape[0]
    units = w_gate.shape[1] // 4
    info = jnp.stack([rank, ctx]).astype(jnp.int32)

    vectors = jnp.pad(jnp.stack([norm1_gain, del_weight, norm2_gain]), ((0, VEC - 3), (0, 0)))
    piece = jnp.where(
        core == 0,
        jnp.concatenate([w_query.T, w_key.T, vectors], axis=0),
        jnp.concatenate([w_value.T, w_out, jnp.zeros_like(vectors)], axis=0),
    )
    pieces = gather_dp(piece, count, rank, 1)
    att = jnp.stack(pieces)
    w0, w1 = in_order(att, swap(att, "core"), core)
    att_other = swap(att, "tp")

    def unit_cols(w):
        return lax.dynamic_slice(w, (0, ctx * units), (shard, units))

    wide = -(-3 * units // 128) * 128
    w_piece = jnp.concatenate(
        [unit_cols(w_gate), unit_cols(w_up), unit_cols(w_down.T), jnp.zeros((shard, wide - 3 * units), BF)], axis=1
    )
    w_piece, _ = lax.optimization_barrier((w_piece, pieces[-1]))
    w_ffn = [lax.all_gather(w_piece, "dp", axis=0, tiled=True)]

    deal = xor_order(pick(dealing, ctx).reshape(4, local), 0, cx, core).reshape(1, 1, rows)
    keep = xor_order(pick(keep_flags, ctx).reshape(4, local), 0, cx, core).reshape(rows)
    lens = pick(lengths, ctx)
    hit = deal[0] == jnp.arange(rows, dtype=jnp.int32)[:, None]
    kf = jnp.sum(jnp.where(hit, keep[None, :], 0), axis=1)[None, :]
    onehot = span_onehot()
    vb = lax.dot_general(rel_table, jnp.asarray(onehot, BF), (((0,), (1,)), ((), ())), preferred_element_type=F32)
    vb = jnp.pad(vb, ((0, 8 - heads), (0, 0)))

    hid = jnp.transpose(hidden, (0, 2, 1))
    blocks = [pick(hid, ctx)] + [cross(pick(hid, ctx ^ k), k) for k in range(1, 4)]
    x = place_tokens(info, deal, [b[None] for b in blocks])[0]

    cot_own = jnp.transpose(cotangent, (0, 2, 1))
    cot = place_tokens(info, dealing, [lax.all_gather(cot_own, ("cx", "core"))])

    n1, qkv, attn, aux = call(
        lambda *refs: enter_kernel(heads, hw, *refs),
        [shape(width, rows), shape(3 * cols, rows), shape(cols, rows), shape(8, rows, dtype=F32)],
        [info, lens, x, w0, w1, kf, vb],
        2 * rows * width * cols * 3 + 4 * rows * rows * cols,
        name="enter",
    )
    attn_other = swap(attn, "tp")
    late, _ = lax.optimization_barrier((att_other, attn))
    w0_other, w1_other = in_order(att_other, swap(late, "core"), core)
    h1, n2 = call(
        lambda *refs: middle_kernel(cols, *refs),
        [shape(width, rows, dtype=F32), shape(width + VEC, rows)],
        [info, lens, x, attn, attn_other, w0, w1, w1_other, aux],
        2 * rows * width * cols * 2,
        name="middle",
    )

    n2_core = swap(n2, "core")
    n2_x = swap(n2, "cx")
    n2_far = swap(n2_x, "core")
    n2_all = [n2, n2_core, n2_x, n2_far]
    gates = [lax.dynamic_slice(n, (width, ctx * local), (1, local)) for n in n2_all]
    gates = jnp.concatenate(xor_list(gates, cx, core), axis=0)
    keep_b, send_b, in_b, dgu_b = ffn(info, n2, n2_core, cot, 0, w_ffn, shard, units)
    far_later, _ = lax.optimization_barrier((n2_far, in_b))
    keep_a, send_a, in_a, dgu_a = ffn(info, n2_x, far_later, cot, 2, w_ffn, shard, units)
    got_a = swap(send_a, "core")
    got_b = swap(send_b, "core")

    def over_x(i):
        return swap((keep_a[i].astype(F32) + got_a[i].astype(F32)).astype(BF), "cx")

    def come_home(i, arrived):
        return (keep_b[i].astype(F32) + got_b[i].astype(F32) + arrived.astype(F32)).astype(BF)

    dn_own = come_home(0, over_x(0))
    dn_other = swap(dn_own, "tp")
    in_a, _ = lax.optimization_barrier((in_a, got_a))
    parts = wgrad(info, 1, n2_all, cot, dgu_b, dgu_a, in_b, in_a, wide)
    g_ffn = scatter_dp(parts, 0).astype(BF)
    g_parts = lax.all_gather(g_ffn, ("cx", "core"))
    g_parts = [g_parts[i] for i in range(4)]
    g_gate = jnp.concatenate([g[:, :units] for g in g_parts], axis=1).astype(F32)
    g_up = jnp.concatenate([g[:, units : 2 * units] for g in g_parts], axis=1).astype(F32)
    g_down = jnp.concatenate([g[:, 2 * units : 3 * units] for g in g_parts], axis=1).astype(F32).T

    blocks_of = att.shape[0]
    dh1, slab, diag, g_wo, g_gain2 = call(
        lambda *refs: back_kernel(heads, hw, *refs),
        [
            shape(width, rows, dtype=F32),
            shape(3 * cols + VEC, rows),
            shape(8, SPAN, dtype=F32),
            shape(blocks_of, cols, width // blocks_of),
            shape(8, width, dtype=F32),
        ],
        [info, lens, dn_own, dn_other, h1, cot[:1], w0, w1, qkv, attn, aux, kf, vb],
        2 * rows * width * cols * 2 + 10 * rows * rows * cols,
        scratch=[
            pltpu.VMEM((width, rows), F32),
            pltpu.VMEM((cols, rows), BF),
            pltpu.VMEM((rows, rows), BF),
            pltpu.VMEM((rows, rows), BF),
            pltpu.VMEM((QB, SPAN), F32),
        ],
        name="back",
    )
    slab_other = swap(slab, "tp")
    bf_over, _ = lax.optimization_barrier((over_x(1), slab))
    bf_own = come_home(1, bf_over)
    bf_own, _ = lax.optimization_barrier((bf_own, slab_other))
    bf_other = swap(bf_own, "tp")
    keep_g, send_g = call(
        lambda *refs: gatt_kernel(cols, *refs),
        [shape(blocks_of, 2 * cols, width // blocks_of)] * 2,
        [info, lens, slab, n1, g_wo],
        2 * rows * width * cols * 3,
        name="gatt",
    )
    mine = (keep_g.astype(F32) + swap(send_g, "core").astype(F32)).astype(BF)
    mine = scatter_dp([mine[k] for k in range(blocks_of)], 1).astype(BF)
    mine = (mine.astype(F32) + swap(mine, "cx").astype(F32)).astype(BF)
    g_qk, g_vo = in_order(mine, swap(mine, "core"), core)
    g_qk = g_qk.astype(F32)
    g_vo = g_vo.astype(F32)
    *dx, vec = call(
        lambda *refs: leave_kernel(cols, *refs),
        [shape(width, local)] * 4 + [shape(16, width, dtype=F32)],
        [info, lens, slab, slab_other, w0, w1, w0_other, w1_other, x, dh1, n1, aux],
        2 * rows * width * cols * 6,
        scratch=[pltpu.VMEM((width, rows), F32), pltpu.VMEM((width, rows), F32)],
        name="leave",
    )

    table = lax.dot_general(
        diag[:heads], jnp.asarray(onehot), (((1,), (0,)), ((), ())), precision=lax.Precision.HIGHEST
    )
    flat = jnp.pad(table.reshape(1, -1), ((0, 0), (0, width - table.size)))
    sums = jnp.concatenate([vec[0:1], vec[8:9], g_gain2[0:1], flat], axis=0)
    sums = sums + swap(sums, "core")
    sums = sums + swap(sums, "cx")
    if count == 4:
        sums = sums + lax.ppermute(sums, "dp", NEAR)
        sums = sums + lax.ppermute(sums, "dp", FAR)
    else:
        sums = lax.psum(sums, "dp")
    table = sums[3, : table.size].reshape(table.shape).T
    vec = lax.dynamic_slice(sums, (0, rank * shard), (3, shard))

    def block_of(k):
        total = sum(
            lax.dynamic_slice(a, (0, (ctx ^ k) * local), (width, local)).astype(F32) for a in (h1, bf_own, bf_other)
        )
        return total.astype(BF)

    def deal_out(items):
        got = [items[0]] + [cross(items[k], k) for k in range(1, 4)]
        return jnp.transpose(jnp.stack(xor_list(got, cx, core)), (0, 2, 1))

    return (
        deal_out([block_of(k) for k in range(4)]),
        gates,
        deal_out(dx),
        vec[0],
        g_qk[:cols].T,
        g_qk[cols:].T,
        g_vo[:cols].T,
        g_vo[cols:],
        table,
        vec[1],
        vec[2],
        g_gate,
        g_up,
        g_down,
    )


def solution(mesh):
    dp, ctx, tp = (mesh.shape[name] for name in ("dp", "ctx", "tp"))
    split = Mesh(mesh.devices.reshape(dp, 2, ctx // 2, tp), ("dp", "cx", "core", "tp"))
    tokens = P(None, ("dp", "cx", "core"), None)
    in_specs = (
        tokens,
        tokens,
        P(None, "dp", None),
        P(None, "dp", None),
        P(None, "dp", None),
        P("dp"),
        P("dp", "tp"),
        P("dp", "tp"),
        P("dp", "tp"),
        P("tp", "dp"),
        P(None, "tp"),
        P("dp"),
        P("dp"),
        P("dp", "tp"),
        P("dp", "tp"),
        P("tp", "dp"),
    )
    out_specs = (
        tokens,
        P(None, ("dp", "cx", "core")),
        tokens,
        P("dp"),
        P("dp", "tp"),
        P("dp", "tp"),
        P("dp", "tp"),
        P("tp", "dp"),
        P(None, "tp"),
        P("dp"),
        P("dp"),
        P("dp", "tp"),
        P("dp", "tp"),
        P("tp", "dp"),
    )
    return jax.shard_map(body, mesh=split, in_specs=in_specs, out_specs=out_specs, check_vma=False)
```

```python
import math

import numpy as np

import jax
import jax.numpy as jnp
from jax import lax
from jax.experimental import pallas as pl
from jax.experimental.pallas import tpu as pltpu
from jax.sharding import Mesh, PartitionSpec as P

BUCKETS = 32
MAX_DIST = 128
EPS = 1e-06
FILL = -1e30
BF = jnp.bfloat16
F32 = jnp.float32
SWAP = [(0, 1), (1, 0)]
SPAN = 1024
QB = 128


def bucket_np(relative):
    half_count = BUCKETS // 2
    exact_count = half_count // 2
    distance = np.abs(relative)
    ratio_bits = math.log2(MAX_DIST / exact_count)
    far = np.full(distance.shape, exact_count, np.int32)
    for level in range(1, half_count - exact_count):
        border = math.ceil(exact_count * 2.0 ** (level * ratio_bits / (half_count - exact_count)))
        far = far + (distance >= border).astype(np.int32)
    chosen = np.where(distance < exact_count, distance, far)
    return chosen + half_count * (relative > 0).astype(np.int32)


def span_onehot():
    k = np.arange(SPAN)
    d = np.where(k < SPAN // 2, k, k - SPAN)
    return (bucket_np(d)[:, None] == np.arange(BUCKETS)[None, :]).astype(np.float32)


def dot_n(a, b):
    return lax.dot_general(a, b, (((1,), (0,)), ((), ())), preferred_element_type=F32)


def dot_t(a, b):
    return lax.dot_general(a, b, (((1,), (1,)), ((), ())), preferred_element_type=F32)


def dot_0(a, b):
    return lax.dot_general(a, b, (((0,), (0,)), ((), ())), preferred_element_type=F32)


SMEM_SPEC = pl.BlockSpec(memory_space=pltpu.SMEM)
VMEM_SPEC = pl.BlockSpec(memory_space=pltpu.VMEM)
ANY_SPEC = pl.BlockSpec(memory_space=pl.ANY)
VEC = 16
COST = dict(enter=0, middle=0, back=12, leave=10, gatt=4, ffn=44, units=4, place=0, places=0)


def cost(name):
    return pl.CostEstimate(flops=COST[name] * 10**9 + 1000, bytes_accessed=1000, transcendentals=0)


def shape(*dims, dtype=BF):
    return jax.ShapeDtypeStruct(dims, dtype)


def call(kernel, outs, args, flops, scratch=(), limit=48, name=None):
    return pl.pallas_call(
        kernel,
        out_shape=tuple(outs),
        in_specs=[SMEM_SPEC] * 2 + [VMEM_SPEC] * (len(args) - 2),
        out_specs=tuple([VMEM_SPEC] * len(outs)),
        scratch_shapes=list(scratch),
        compiler_params=pltpu.CompilerParams(vmem_limit_bytes=limit * 2**20),
        cost_estimate=cost(name),
        name=name,
    )(*args)


def allowed_block(lens_ref, kf_ref, b, rows):
    e1 = lens_ref[0, 0]
    e2 = e1 + lens_ref[0, 1]
    tj = lax.broadcasted_iota(jnp.int32, (1, rows), 1)
    ti = lax.broadcasted_iota(jnp.int32, (QB, 1), 0) + b * QB
    sj = (tj >= e1).astype(jnp.int32) + (tj >= e2).astype(jnp.int32)
    si = (ti >= e1).astype(jnp.int32) + (ti >= e2).astype(jnp.int32)
    keep = kf_ref[...] == 1
    return (si == sj) & (keep | (ti == tj))


def window(full, b, rows):
    if b == 0:
        return full[:, :rows]
    return jnp.concatenate([full[:, SPAN - QB * b :], full[:, : rows - QB * b]], axis=1)


def toeplitz(vb_ref, h):
    row = jnp.broadcast_to(vb_ref[h : h + 1, :], (QB, SPAN))
    return pltpu.roll(row, 0, 1, stride=1, stride_axis=0)


def probs(q, k, bias, gate, allowed):
    s = dot_0(q, k) + bias + gate
    s = jnp.where(allowed, s, FILL)
    e = jnp.exp(s - jnp.max(s, axis=1, keepdims=True))
    return e / jnp.sum(e, axis=1, keepdims=True)


def attend(heads, hw, lens_ref, qkv_ref, gate, kf_ref, vb_ref, o_ref):
    rows = qkv_ref.shape[1]
    c = heads * hw
    masks = [allowed_block(lens_ref, kf_ref, b, rows) for b in range(rows // QB)]
    for h in range(heads):
        full = toeplitz(vb_ref, h)
        k = qkv_ref[c + h * hw : c + (h + 1) * hw, :]
        v = qkv_ref[2 * c + h * hw : 2 * c + (h + 1) * hw, :]
        for b in range(rows // QB):
            q = qkv_ref[h * hw : (h + 1) * hw, b * QB : (b + 1) * QB]
            p = probs(q, k, window(full, b, rows), gate, masks[b])
            o_ref[h * hw : (h + 1) * hw, b * QB : (b + 1) * QB] = dot_t(v, p.astype(BF)).astype(BF)


def attend_back(heads, hw, lens_ref, qkv_ref, do_ref, gate, kf_ref, vb_ref, g_ref, t_ref, ds_ref, pl_ref, acc_ref):
    rows = qkv_ref.shape[1]
    c = heads * hw
    masks = [allowed_block(lens_ref, kf_ref, b, rows) for b in range(rows // QB)]
    ones = jnp.ones((VEC, rows), BF)
    dgate = jnp.zeros((VEC, rows), F32)
    t_ref[...] = jnp.zeros_like(t_ref)
    for h in range(heads):
        full = toeplitz(vb_ref, h)
        sl = slice(h * hw, (h + 1) * hw)
        k = qkv_ref[c + h * hw : c + (h + 1) * hw, :]
        v = qkv_ref[2 * c + h * hw : 2 * c + (h + 1) * hw, :]
        acc_ref[...] = jnp.zeros_like(acc_ref)
        for b in range(rows // QB):
            rs = slice(b * QB, (b + 1) * QB)
            p = probs(qkv_ref[sl, rs], k, window(full, b, rows), gate, masks[b])
            dp = dot_0(do_ref[sl, rs], v)
            ds = (p * (dp - jnp.sum(p * dp, axis=1, keepdims=True))).astype(BF)
            ds_ref[rs, :] = ds
            pl_ref[rs, :] = p.astype(BF)
            wide = ds.astype(F32)
            if b == 0:
                acc_ref[:, :rows] += wide
            else:
                acc_ref[:, SPAN - QB * b :] += wide[:, : QB * b]
                acc_ref[:, : rows - QB * b] += wide[:, QB * b :]
        ds_all = ds_ref[...]
        g_ref[sl, :] = dot_t(k, ds_all).astype(BF)
        g_ref[c + h * hw : c + (h + 1) * hw, :] = dot_n(qkv_ref[sl, :], ds_all).astype(BF)
        g_ref[2 * c + h * hw : 2 * c + (h + 1) * hw, :] = dot_n(do_ref[sl, :], pl_ref[...]).astype(BF)
        dgate = dgate + dot_n(ones, ds_all)
        a = acc_ref[...]
        half = QB // 2
        while half >= 8:
            low = a[half:, :]
            a = a[:half, :] + pltpu.roll(low, SPAN - half, 1)
            half //= 2
        tot = a[0:1, :]
        for i in range(1, 8):
            tot = tot + pltpu.roll(a[i : i + 1, :], SPAN - i, 1)
        t_ref[h : h + 1, :] = tot
    g_ref[3 * c :, :] = dgate.astype(BF)


def spots(info_ref, array_ref):
    many, block = array_ref.shape[0], array_ref.shape[2]
    if many == 1:
        return [pl.ds(0, block)]
    return [pl.ds(pl.multiple_of((info_ref[0] ^ k) * block, VEC), block) for k in range(many)]


def spread(w0_ref, k, c, which, rows):
    pickup = (lax.broadcasted_iota(jnp.int32, (VEC, QB), 0) == which).astype(F32).astype(BF)
    block = dot_0(w0_ref[k, 2 * c :, :], pickup)
    return jnp.concatenate([block] * (rows // QB), axis=1)


def inverse_rms(values):
    return lax.rsqrt(jnp.sum(values * values, axis=0, keepdims=True) / values.shape[0] + EPS)


def sum_tokens(values):
    values = sum(values[:, i : i + QB] for i in range(0, values.shape[1], QB))
    high = values.astype(BF)
    rest = (values - high.astype(F32)).astype(BF)
    ones = jnp.ones((8, QB), BF)
    return dot_t(ones, high) + dot_t(ones, rest)


def enter_kernel(heads, hw, info_ref, lens_ref, x_ref, w0_ref, w1_ref, kf_ref, vb_ref, n1_ref, qkv_ref, attn_ref, aux_ref):
    rows = x_ref.shape[1]
    c = heads * hw
    x = x_ref[...].astype(F32)
    r1 = inverse_rms(x)
    half = c // 2
    low = jnp.zeros((2 * c + VEC, rows), F32)
    high = jnp.zeros((c + half, rows), F32)
    for k, spot in enumerate(spots(info_ref, w0_ref)):
        n1 = (x_ref[spot, :].astype(F32) * r1 * spread(w0_ref, k, c, 0, rows)).astype(BF)
        n1_ref[spot, :] = n1
        low = low + dot_n(w0_ref[k], n1)
        high = high + dot_n(w1_ref[k, : c + half, :], n1)
    qkv_ref[: c + half, :] = low[: c + half].astype(BF)
    qkv_ref[c + half :, :] = high.astype(BF)
    z = low[2 * c + 1 : 2 * c + 2]
    gate = (-4.0 * jax.nn.sigmoid(z)).astype(BF).astype(F32)
    aux_ref[...] = jnp.concatenate([z, gate, r1, jnp.zeros((5, rows), F32)], axis=0)
    attend(heads, hw, lens_ref, qkv_ref, gate, kf_ref, vb_ref, attn_ref)


def middle_kernel(
    c, info_ref, lens_ref, x_ref, attn_ref, other_ref, w0_ref, w1_ref, wo0_ref, wo1_ref, aux_ref, h1_ref, n2_ref
):
    rows = x_ref.shape[1]
    half = c // 2
    out = slice(c + half, 2 * c)
    width = x_ref.shape[0]
    total = jnp.zeros((1, rows), F32)
    places = spots(info_ref, w0_ref)
    for k, spot in enumerate(places):
        own = dot_0(w0_ref[k, out, :], attn_ref[:half, :]) + dot_0(w1_ref[k, out, :], attn_ref[half:, :])
        far = dot_0(wo0_ref[k], other_ref[:half, :]) + dot_0(wo1_ref[k], other_ref[half:, :])
        h1 = x_ref[spot, :].astype(F32) + (own.astype(BF).astype(F32) + far.astype(BF).astype(F32))
        h1_ref[spot, :] = h1
        total = total + jnp.sum(h1 * h1, axis=0, keepdims=True)
    r2 = lax.rsqrt(total / width + EPS)
    for k, spot in enumerate(places):
        n2_ref[spot, :] = (h1_ref[spot, :] * r2 * spread(w0_ref, k, c, 2, rows)).astype(BF)
    n2_ref[width:, :] = jnp.broadcast_to(aux_ref[1:2, :], (VEC, rows)).astype(BF)


def back_kernel(
    heads,
    hw,
    info_ref,
    lens_ref,
    low0_ref,
    low1_ref,
    high0_ref,
    high1_ref,
    h1_ref,
    cot_ref,
    w0_ref,
    w1_ref,
    qkv_ref,
    attn_ref,
    aux_ref,
    kf_ref,
    vb_ref,
    dh1_ref,
    slab_ref,
    diag_ref,
    gwo_ref,
    gain_ref,
    u_ref,
    do_ref,
    ds_ref,
    pl_ref,
    acc_ref,
):
    rows = h1_ref.shape[1]
    width = h1_ref.shape[0]
    c = heads * hw
    places = spots(info_ref, w0_ref)
    r2 = inverse_rms(h1_ref[...])
    total = jnp.zeros((1, rows), F32)
    cut = low0_ref.shape[0]
    u_ref[:cut, :] = low0_ref[...].astype(F32) + low1_ref[...].astype(F32)
    u_ref[cut:, :] = high0_ref[...].astype(F32) + high1_ref[...].astype(F32)
    for k, spot in enumerate(places):
        dn2 = u_ref[spot, :]
        u = dn2 * spread(w0_ref, k, c, 2, rows)
        h1 = h1_ref[spot, :]
        total = total + jnp.sum(h1 * u, axis=0, keepdims=True)
        u_ref[spot, :] = u
        gain_ref[k] = sum_tokens(dn2 * h1 * r2)
    back = r2 * r2 * r2 * (total / width)
    half = c // 2
    out = slice(c + half, 2 * c)
    dattn = [jnp.zeros((half, rows), F32)] * 2
    for k, spot in enumerate(places):
        dh1 = cot_ref[0, spot, :].astype(F32) + r2 * u_ref[spot, :] - h1_ref[spot, :] * back
        dh1_ref[spot, :] = dh1
        dhl = dh1.astype(BF)
        dattn = [d + dot_n(w_ref[k, out, :], dhl) for d, w_ref in zip(dattn, (w0_ref, w1_ref))]
        gwo_ref[k] = dot_t(attn_ref[...], dhl).astype(BF)
    do_ref[:half, :] = dattn[0].astype(BF)
    do_ref[half:, :] = dattn[1].astype(BF)
    attend_back(
        heads, hw, lens_ref, qkv_ref, do_ref, aux_ref[1:2, :], kf_ref, vb_ref, slab_ref, diag_ref, ds_ref, pl_ref, acc_ref
    )


def gatt_kernel(c, info_ref, lens_ref, slab_ref, n1_ref, gwo_ref, out_ref):
    many = gwo_ref.shape[0]
    for k, spot in enumerate(spots(info_ref, gwo_ref)):
        at = info_ref[0] ^ k if many > 1 else 0
        n1 = n1_ref[spot, :]
        for i in range(3):
            out_ref[at, i] = dot_t(slab_ref[i * c : (i + 1) * c, :], n1).astype(BF)
        out_ref[at, 3] = gwo_ref[k]


def leave_kernel(
    c,
    info_ref,
    lens_ref,
    slab_ref,
    other_ref,
    w0_ref,
    w1_ref,
    far0_ref,
    far1_ref,
    x_ref,
    dh1_ref,
    n1_ref,
    aux_ref,
    o0,
    o1,
    o2,
    o3,
    vec_ref,
    dn_ref,
    dx_ref,
):
    rows = x_ref.shape[1]
    width = x_ref.shape[0]
    half = 3 * c // 2
    places = spots(info_ref, w0_ref)
    z = aux_ref[0:1, :]
    r1 = aux_ref[2:3, :]
    sig = jax.nn.sigmoid(z)
    dgate = slab_ref[3 * c : 3 * c + 1, :].astype(F32) + other_ref[3 * c : 3 * c + 1, :].astype(F32)
    dz = dgate * (-4.0 * sig * (1.0 - sig))
    total = jnp.zeros((1, rows), F32)
    for k, spot in enumerate(places):
        own = dot_0(w0_ref[k, :half, :], slab_ref[:half, :]) + dot_0(w1_ref[k, :half, :], slab_ref[half : 2 * half, :])
        far = dot_0(far0_ref[k], other_ref[:half, :]) + dot_0(far1_ref[k], other_ref[half : 2 * half, :])
        dn = own.astype(BF).astype(F32) + far.astype(BF).astype(F32) + spread(w0_ref, k, c, 1, rows) * dz
        u = dn * spread(w0_ref, k, c, 0, rows)
        x = x_ref[spot, :].astype(F32)
        total = total + jnp.sum(x * u, axis=0, keepdims=True)
        dx_ref[spot, :] = u
        vec_ref[k, 0:8, :] = sum_tokens(dn * x * r1)
        vec_ref[k, 8:16, :] = sum_tokens(n1_ref[spot, :].astype(F32) * dz)
    back = r1 * r1 * r1 * (total / width)
    dn_ref[...] = dh1_ref[...] + r1 * dx_ref[...] - x_ref[...].astype(F32) * back
    part = rows // 4
    for k, out in enumerate((o0, o1, o2, o3)):
        at = pl.multiple_of((info_ref[1] ^ k) * part, part)
        out[...] = dn_ref[:, pl.ds(at, part)].astype(BF)


def ffn_kernel(n_pieces, shard, units, info_ref, n0, n1, n2, n3, cot_ref, *refs):
    pieces = refs[:n_pieces]
    o0, o1, o2, o3, grad_ref, w_ref, n_ref, gu_ref, acc_ref, inner_ref, dgu_ref, sems = refs[n_pieces:]
    step = pl.program_id(0)
    per = pl.num_programs(0) // 4
    width = w_ref.shape[0]

    @pl.when(step == 0)
    def _():
        copies = []
        for k in range(n_pieces):
            at = pl.multiple_of((info_ref[0] ^ k) * shard, VEC) if n_pieces > 1 else 0
            copies.append(pltpu.make_async_copy(pieces[k], w_ref.at[pl.ds(at, pieces[k].shape[0])], sems.at[k]))
        for c in copies:
            c.start()
        acc_ref[...] = jnp.zeros_like(acc_ref)
        for c in copies:
            c.wait()

    for k, source in enumerate((n0, n1, n2, n3)):

        @pl.when(step // per == k)
        def _():
            n_ref[...] = source[:width, :]

    gu_ref[: 2 * units, :] = dot_0(w_ref[:, : 2 * units], n_ref[...])
    gu_ref[2 * units :, :] = dot_0(w_ref[:, 2 * units : 3 * units], cot_ref[0])
    c0 = math.sqrt(2.0 / math.pi)
    chunk = units // 14
    for r in range(0, units, chunk):
        ga = gu_ref[r : r + chunk, :]
        up = gu_ref[units + r : units + r + chunk, :]
        din = gu_ref[2 * units + r : 2 * units + r + chunk, :]
        sq = ga * ga
        th = jnp.tanh(c0 * (ga + 0.044715 * ga * sq))
        hf = 0.5 * (1.0 + th)
        act = ga * hf
        slope = hf + 0.5 * ga * (1.0 - th * th) * (c0 + 3.0 * 0.044715 * c0 * sq)
        inner_ref[r : r + chunk, :] = (act * up).astype(BF)
        dgu_ref[r : r + chunk, :] = (din * up * slope).astype(BF)
        dgu_ref[units + r : units + r + chunk, :] = (din * act).astype(BF)
    for k, out in enumerate((o0, o1, o2, o3)):

        @pl.when(step // per == k)
        def _():
            out[0] = dot_n(w_ref[:, : 2 * units], dgu_ref[...]).astype(BF)
            out[1] = dot_n(w_ref[:, 2 * units : 3 * units], inner_ref[...]).astype(BF)

    acc_ref[:, : 2 * units] += dot_t(n_ref[...], dgu_ref[...])
    acc_ref[:, 2 * units : 3 * units] += dot_t(cot_ref[0], inner_ref[...])

    @pl.when(step == 4 * per - 1)
    def _():
        grad_ref[...] = acc_ref[...].astype(BF)


def ffn(info, ns, cot, pieces, shard, units, tile=256):
    width, rows = cot.shape[1:]
    tall = ns[0].shape[0]
    per = rows // tile
    wide = pieces[0].shape[1]
    part = lambda k: lambda i, s: (0, jnp.clip(i - k * per, 0, per - 1))
    part3 = lambda k: lambda i, s: (0, 0, jnp.clip(i - k * per, 0, per - 1))
    return pl.pallas_call(
        lambda *refs: ffn_kernel(len(pieces), shard, units, *refs),
        grid_spec=pltpu.PrefetchScalarGridSpec(
            num_scalar_prefetch=1,
            grid=(4 * per,),
            in_specs=[pl.BlockSpec((tall, tile), part(k)) for k in range(4)]
            + [pl.BlockSpec((1, width, tile), lambda i, s: (i // per, 0, i % per))]
            + [ANY_SPEC] * len(pieces),
            out_specs=[pl.BlockSpec((2, width, tile), part3(k)) for k in range(4)]
            + [pl.BlockSpec((width, wide), lambda i, s: (0, 0))],
            scratch_shapes=[
                pltpu.VMEM((width, wide), BF),
                pltpu.VMEM((width, tile), BF),
                pltpu.VMEM((3 * units, tile), F32),
                pltpu.VMEM((width, wide), F32),
                pltpu.VMEM((units, tile), BF),
                pltpu.VMEM((2 * units, tile), BF),
                pltpu.SemaphoreType.DMA((len(pieces),)),
            ],
        ),
        out_shape=[shape(2, width, rows)] * 4 + [shape(width, wide)],
        compiler_params=pltpu.CompilerParams(vmem_limit_bytes=56 * 2**20),
        cost_estimate=cost("ffn"),
        name="ffn",
    )(info, *ns, cot, *pieces)


def spread_units_kernel(units, info_ref, a, b, c, d, gate_ref, up_ref, down_ref, part_ref):
    for k, source in enumerate((a, b, c, d)):
        part_ref[k] = source[...]
    for i in range(4):
        at = slice(i * units, (i + 1) * units)
        for n, ref in enumerate((gate_ref, up_ref, down_ref)):
            ref[:, at] = part_ref[info_ref[1] ^ i, :, n * units : (n + 1) * units].astype(F32)


def spread_units(info, parts, units):
    rows, wide = parts[0].shape
    tile = rows // 2 if rows % 32 == 16 else rows
    out = pl.BlockSpec((tile, 4 * units), lambda i, s: (i, 0))
    return pl.pallas_call(
        lambda *refs: spread_units_kernel(units, *refs),
        grid_spec=pltpu.PrefetchScalarGridSpec(
            num_scalar_prefetch=1,
            grid=(rows // tile,),
            in_specs=[pl.BlockSpec((tile, wide), lambda i, s: (i, 0))] * 4,
            out_specs=[out] * 3,
            scratch_shapes=[pltpu.VMEM((4, tile, wide), BF)],
        ),
        out_shape=[shape(rows, 4 * units, dtype=F32)] * 3,
        compiler_params=pltpu.CompilerParams(vmem_limit_bytes=40 * 2**20),
        cost_estimate=cost("units"),
        name="units",
    )(info, *parts)


def place_kernel(info_ref, deal_ref, *refs):
    *blocks, out_ref = refs
    rows = out_ref.shape[2]
    hit = lax.broadcasted_iota(jnp.int32, (rows, rows), 0) == deal_ref[0]
    blocks = jnp.concatenate([b[0] for b in blocks], axis=1)
    out_ref[0] = dot_t(blocks, hit.astype(F32).astype(BF)).astype(BF)


def place_tokens(info, deal, blocks):
    many, _, rows = deal.shape
    width, local = blocks[0].shape[-2:]
    if many == 1:
        specs = [pl.BlockSpec((1, width, local), lambda j, s: (0, 0, 0))] * 4
        order = lambda j, s: (0, 0, 0)
    else:
        specs = [pl.BlockSpec((1, width, local), lambda j, s: (s[1] ^ j, 0, 0))] * 4
        order = lambda j, s: (s[1] ^ j, 0, 0)
    return pl.pallas_call(
        place_kernel,
        grid_spec=pltpu.PrefetchScalarGridSpec(
            num_scalar_prefetch=1,
            grid=(many,),
            in_specs=[pl.BlockSpec((1, 1, rows), order)] + specs,
            out_specs=pl.BlockSpec((1, width, rows), lambda j, s: (j, 0, 0)),
        ),
        out_shape=shape(many, width, rows),
        compiler_params=pltpu.CompilerParams(vmem_limit_bytes=48 * 2**20),
        cost_estimate=cost("place" if many == 1 else "places"),
        name="place",
    )(info, deal, *blocks)


def pick(array, index, axis=0):
    return lax.dynamic_index_in_dim(array, index, axis, keepdims=False)


def swap(block, axis):
    return lax.ppermute(block, axis, SWAP)


def cross(block, step):
    if step == 3:
        return lax.ppermute(block, ("cx", "core"), [(0, 3), (1, 2), (2, 1), (3, 0)])
    return swap(block, "core" if step == 1 else "cx")


NEAR = [(0, 1), (1, 0), (2, 3), (3, 2)]
FAR = [(0, 2), (2, 0), (1, 3), (3, 1)]
MID = [(1, 2), (2, 1)]


def gather_dp(piece, count, rank, axis):
    if count != 4:
        return [lax.all_gather(piece, "dp", axis=axis, tiled=True)]
    near = lax.ppermute(piece, "dp", NEAR)
    far = lax.ppermute(piece, "dp", FAR)
    mid = lax.ppermute(piece, "dp", MID)
    passed = lax.ppermute(far, "dp", [(1, 0), (2, 3)])
    return [piece, near, far, jnp.where((rank == 1) | (rank == 2), mid, passed)]


def scatter_dp(parts, axis):
    if len(parts) == 1:
        return lax.psum_scatter(parts[0], "dp", scatter_dimension=axis, tiled=True).astype(F32)
    early = lax.ppermute(parts[3], "dp", [(0, 1), (3, 2)])
    near = lax.ppermute(parts[1], "dp", NEAR)
    mid = lax.ppermute(parts[3], "dp", MID)
    far = lax.ppermute((parts[2].astype(F32) + early.astype(F32)).astype(BF), "dp", FAR)
    return parts[0].astype(F32) + near.astype(F32) + mid.astype(F32) + far.astype(F32)


def in_order(first, second, index):
    return jnp.where(index == 0, first, second), jnp.where(index == 0, second, first)


def xor_list(items, cx, core):
    a, b, c, d = items
    a, b = in_order(a, b, core)
    c, d = in_order(c, d, core)
    (a, c), (b, d) = in_order(a, c, cx), in_order(b, d, cx)
    return [a, b, c, d]


def xor_order(array, axis, cx, core):
    return jnp.concatenate(xor_list([lax.slice_in_dim(array, i, i + 1, axis=axis) for i in range(4)], cx, core), axis)


def body(
    hidden,
    cotangent,
    lengths,
    dealing,
    keep_flags,
    norm1_gain,
    w_query,
    w_key,
    w_value,
    w_out,
    rel_table,
    del_weight,
    norm2_gain,
    w_gate,
    w_up,
    w_down,
):
    count = lax.axis_size("dp")
    rank = lax.axis_index("dp")
    cx = lax.axis_index("cx")
    core = lax.axis_index("core")
    ctx = cx * 2 + core
    local = hidden.shape[1]
    width = hidden.shape[2]
    rows = local * 4
    heads = rel_table.shape[1]
    cols = w_query.shape[1]
    hw = cols // heads
    shard = w_query.shape[0]
    units = w_gate.shape[1] // 4
    info = jnp.stack([rank, ctx]).astype(jnp.int32)

    half = cols // 2
    w_key_t = w_key.T
    vectors = jnp.pad(jnp.stack([norm1_gain, del_weight, norm2_gain]), ((0, VEC - 3), (0, 0)))
    piece = jnp.where(
        core == 0,
        jnp.concatenate([w_query.T, w_key_t[:half], w_out[:half], vectors], axis=0),
        jnp.concatenate([w_key_t[half:], w_value.T, w_out[half:], jnp.zeros_like(vectors)], axis=0),
    )
    pieces = gather_dp(piece, count, rank, 1)
    att = jnp.stack(pieces)
    w0, w1 = in_order(att, swap(att, "core"), core)
    wo_other = swap(att[:, 3 * half : 4 * half], "tp")

    def unit_cols(w):
        return lax.dynamic_slice(w, (0, ctx * units), (shard, units))

    wide = -(-3 * units // 128) * 128
    w_piece = jnp.concatenate(
        [unit_cols(w_gate), unit_cols(w_up), unit_cols(w_down.T), jnp.zeros((shard, wide - 3 * units), BF)], axis=1
    )
    w_piece, *_ = lax.optimization_barrier((w_piece, *pieces[1:2]))
    w_ffn = [lax.all_gather(w_piece, "dp", axis=0, tiled=True)]

    deal = xor_order(pick(dealing, ctx).reshape(4, local), 0, cx, core).reshape(1, 1, rows)
    keep = xor_order(pick(keep_flags, ctx).reshape(4, local), 0, cx, core).reshape(rows)
    lens = pick(lengths, ctx)
    hit = deal[0] == jnp.arange(rows, dtype=jnp.int32)[:, None]
    kf = jnp.sum(jnp.where(hit, keep[None, :], 0), axis=1)[None, :]
    onehot = span_onehot()
    vb = lax.dot_general(rel_table, jnp.asarray(onehot, BF), (((0,), (1,)), ((), ())), preferred_element_type=F32)
    vb = jnp.pad(vb, ((0, 8 - heads), (0, 0)))

    hid = jnp.transpose(hidden, (0, 2, 1))
    over = swap(jnp.stack([pick(hid, ctx ^ 2), pick(hid, ctx ^ 3)]), "cx")
    across = swap(jnp.stack([pick(hid, ctx ^ 1), over[1]]), "core")
    x = place_tokens(info, deal, [pick(hid, ctx)[None], across[:1], over[:1], across[1:]])[0]

    cot_own = jnp.transpose(cotangent, (0, 2, 1))
    cot_x = swap(cot_own, "cx")
    n1, qkv, attn, aux = call(
        lambda *refs: enter_kernel(heads, hw, *refs),
        [shape(width, rows), shape(3 * cols, rows), shape(cols, rows), shape(8, rows, dtype=F32)],
        [info, lens, x, w0, w1, kf, vb],
        2 * rows * width * cols * 3 + 4 * rows * rows * cols,
        name="enter",
    )
    attn_other = swap(attn, "tp")
    wo_later, _ = lax.optimization_barrier((wo_other, attn))
    wo0_other, wo1_other = in_order(wo_other, swap(wo_later, "core"), core)
    h1, n2 = call(
        lambda *refs: middle_kernel(cols, *refs),
        [shape(width, rows, dtype=F32), shape(width + VEC, rows)],
        [info, lens, x, attn, attn_other, w0, w1, wo0_other, wo1_other, aux],
        2 * rows * width * cols * 2,
        name="middle",
    )

    n2, cot_x = lax.optimization_barrier((n2, cot_x))
    deals = xor_order(dealing.reshape(4, 4, local), 1, cx, core).reshape(4, 1, rows)
    cot = place_tokens(info, deals, [cot_own, swap(cot_own, "core"), cot_x, swap(cot_x, "core")])

    att_later, _ = lax.optimization_barrier((att[:, : 3 * half], attn_other))
    att_other = swap(att_later, "tp")
    n2_core = swap(n2, "core")
    n2_x = swap(n2, "cx")
    n2_x, cot, att_other = lax.optimization_barrier((n2_x, cot, att_other))
    n2_all = [n2, n2_core, n2_x, swap(n2_x, "core")]
    gates = [lax.dynamic_slice(n, (width, ctx * local), (1, local)) for n in n2_all]
    gates = jnp.concatenate(xor_list(gates, cx, core), axis=0)
    n2_all[3], att_core = lax.optimization_barrier((n2_all[3], swap(att_other, "core")))
    w0_other, w1_other = in_order(att_other, att_core, core)
    keep_b, send_b, keep_a, send_a, parts = ffn(info, n2_all, cot, w_ffn, shard, units)
    got_a = swap(send_a, "core")
    got_b = swap(send_b, "core")

    def both(kept, got, i, low=0, high=width):
        return kept[i][low:high].astype(F32) + got[i][low:high].astype(F32)

    cut = width // 48 * 16
    first = jnp.stack([both(keep_a, got_a, 0, 0, cut).astype(BF), both(keep_b, got_b, 0, 0, cut).astype(BF)])
    first = first.astype(F32) + swap(first, "tp").astype(F32)
    late_x = swap(both(keep_a, got_a, 0, cut).astype(BF), "cx")
    late_own = (both(keep_b, got_b, 0, cut) + late_x.astype(F32)).astype(BF)
    dn_pairs = [first[1].astype(BF), swap(first[0].astype(BF), "cx"), late_own, swap(late_own, "tp")]
    bf_over, _ = lax.optimization_barrier((both(keep_a, got_a, 1).astype(BF), dn_pairs[1]))
    bf_x, _ = lax.optimization_barrier((swap(bf_over, "cx"), dn_pairs[3]))
    bf_own = (both(keep_b, got_b, 1) + bf_x.astype(F32)).astype(BF)
    g_ffn = scatter_dp([parts], 0).astype(BF)
    blocks_of = att.shape[0]
    dh1, slab, diag, g_wo, g_gain2 = call(
        lambda *refs: back_kernel(heads, hw, *refs),
        [
            shape(width, rows, dtype=F32),
            shape(3 * cols + VEC, rows),
            shape(8, SPAN, dtype=F32),
            shape(blocks_of, cols, width // blocks_of),
            shape(blocks_of, 8, width // blocks_of, dtype=F32),
        ],
        [info, lens, *dn_pairs, h1, cot[:1], w0, w1, qkv, attn, aux, kf, vb],
        2 * rows * width * cols * 2 + 10 * rows * rows * cols,
        scratch=[
            pltpu.VMEM((width, rows), F32),
            pltpu.VMEM((cols, rows), BF),
            pltpu.VMEM((rows, rows), BF),
            pltpu.VMEM((rows, rows), BF),
            pltpu.VMEM((QB, SPAN), F32),
        ],
        name="back",
    )
    slab_other = swap(slab, "tp")
    g_ffn, _ = lax.optimization_barrier((g_ffn, slab))
    slab_other, bf_own, g_ffn = lax.optimization_barrier((slab_other, bf_own, g_ffn))
    bf_other = swap(bf_own, "tp")
    g_x = swap(g_ffn, "cx")
    *dx, vec = call(
        lambda *refs: leave_kernel(cols, *refs),
        [shape(width, local)] * 4 + [shape(blocks_of, 16, width // blocks_of, dtype=F32)],
        [info, lens, slab, slab_other, w0, w1, w0_other, w1_other, x, dh1, n1, aux],
        2 * rows * width * cols * 6,
        scratch=[pltpu.VMEM((width, rows), F32), pltpu.VMEM((width, rows), F32)],
        name="leave",
    )

    (grads,) = call(
        lambda *refs: gatt_kernel(cols, *refs),
        [shape(blocks_of, 4, cols, width // blocks_of)],
        [info, lens, slab, n1, g_wo],
        2 * rows * width * cols * 3,
        name="gatt",
    )
    if blocks_of == 1:
        grads = jnp.transpose(grads[0].reshape(4, cols, count, shard), (2, 0, 1, 3))
    grads = grads.reshape(count * 4 * cols, shard)
    grads = lax.psum_scatter(grads, ("dp", "cx", "core"), scatter_dimension=0, tiled=True)

    table = lax.dot_general(
        diag[:heads], jnp.asarray(onehot), (((1,), (0,)), ((), ())), precision=lax.Precision.HIGHEST
    )
    bw = width // blocks_of
    size = table.size // 8
    flat = jnp.broadcast_to(jnp.pad(table.reshape(1, 8, size), ((0, 0), (0, 0), (0, bw - size))), (blocks_of, 8, bw))
    sums = jnp.concatenate([vec, g_gain2, flat], axis=1)

    def deal_out(items):
        return [items[0]] + [cross(items[k], k) for k in range(1, 4)]

    def arrange(got):
        return jnp.transpose(jnp.stack(xor_list(got, cx, core)), (0, 2, 1))

    def block_of(k):
        total = sum(
            lax.dynamic_slice(a, (0, (ctx ^ k) * local), (width, local)).astype(F32) for a in (h1, bf_own, bf_other)
        )
        return total.astype(BF)

    if count == 4:
        far = lax.ppermute(sums[2:], "dp", FAR)
    else:
        sums = far = lax.psum(sums, "dp")
    *dx, g_x, far = lax.optimization_barrier((*dx, g_x, far))
    dx = deal_out(dx)
    if count == 4:
        sums = sums[:2] + far
        near = lax.ppermute(sums[1], "dp", NEAR)
    else:
        near = jnp.zeros_like(sums[0])
    bf_other, near, *dx = lax.optimization_barrier((bf_other, near, *dx))
    sums = sums[0] + near
    out = deal_out([block_of(k) for k in range(4)])
    g_gate, g_up, g_down = spread_units(info, [g_ffn, swap(g_ffn, "core"), g_x, swap(g_x, "core")], units)
    out[1], grads, core_sums, g_gate = lax.optimization_barrier((out[1], grads, swap(sums, "core"), g_gate))
    sums = sums + core_sums
    g_weights = lax.all_gather(grads, ("cx", "core"))
    *out, g_weights, x_sums = lax.optimization_barrier((*out, g_weights, swap(sums, "cx")))
    sums = sums + x_sums
    g_weights = g_weights.astype(F32)
    if count == 4:
        vec = sums[:24:8]
    else:
        vec = lax.dynamic_slice(sums[:24:8], (0, rank * shard), (3, shard))
    table = sums[24:, :size].reshape(table.shape).T

    return (
        arrange(out),
        gates,
        arrange(dx),
        vec[0],
        g_weights[0].T,
        g_weights[1].T,
        g_weights[2].T,
        g_weights[3],
        table,
        vec[1],
        vec[2],
        g_gate,
        g_up,
        g_down.T,
    )


def solution(mesh):
    dp, ctx, tp = (mesh.shape[name] for name in ("dp", "ctx", "tp"))
    split = Mesh(mesh.devices.reshape(dp, 2, ctx // 2, tp), ("dp", "cx", "core", "tp"))
    tokens = P(None, ("dp", "cx", "core"), None)
    in_specs = (
        tokens,
        tokens,
        P(None, "dp", None),
        P(None, "dp", None),
        P(None, "dp", None),
        P("dp"),
        P("dp", "tp"),
        P("dp", "tp"),
        P("dp", "tp"),
        P("tp", "dp"),
        P(None, "tp"),
        P("dp"),
        P("dp"),
        P("dp", "tp"),
        P("dp", "tp"),
        P("tp", "dp"),
    )
    out_specs = (
        tokens,
        P(None, ("dp", "cx", "core")),
        tokens,
        P("dp"),
        P("dp", "tp"),
        P("dp", "tp"),
        P("dp", "tp"),
        P("tp", "dp"),
        P(None, "tp"),
        P("dp"),
        P("dp"),
        P("dp", "tp"),
        P("dp", "tp"),
        P("tp", "dp"),
    )
    return jax.shard_map(body, mesh=split, in_specs=in_specs, out_specs=out_specs, check_vma=False)
```

```python
import math

import numpy as np

import jax
import jax.numpy as jnp
from jax import lax
from jax.experimental import pallas as pl
from jax.experimental.pallas import tpu as pltpu
from jax.sharding import Mesh, PartitionSpec as P

BUCKETS = 32
MAX_DIST = 128
EPS = 1e-06
FILL = -1e30
BF = jnp.bfloat16
F32 = jnp.float32
SWAP = [(0, 1), (1, 0)]
SPAN = 1024
QB = 128


def bucket_np(relative):
    half_count = BUCKETS // 2
    exact_count = half_count // 2
    distance = np.abs(relative)
    ratio_bits = math.log2(MAX_DIST / exact_count)
    far = np.full(distance.shape, exact_count, np.int32)
    for level in range(1, half_count - exact_count):
        border = math.ceil(exact_count * 2.0 ** (level * ratio_bits / (half_count - exact_count)))
        far = far + (distance >= border).astype(np.int32)
    chosen = np.where(distance < exact_count, distance, far)
    return chosen + half_count * (relative > 0).astype(np.int32)


def span_onehot():
    k = np.arange(SPAN)
    d = np.where(k < SPAN // 2, k, k - SPAN)
    return (bucket_np(d)[:, None] == np.arange(BUCKETS)[None, :]).astype(np.float32)


def dot_n(a, b):
    return lax.dot_general(a, b, (((1,), (0,)), ((), ())), preferred_element_type=F32)


def dot_t(a, b):
    return lax.dot_general(a, b, (((1,), (1,)), ((), ())), preferred_element_type=F32)


def dot_0(a, b):
    return lax.dot_general(a, b, (((0,), (0,)), ((), ())), preferred_element_type=F32)


SMEM_SPEC = pl.BlockSpec(memory_space=pltpu.SMEM)
VMEM_SPEC = pl.BlockSpec(memory_space=pltpu.VMEM)
ANY_SPEC = pl.BlockSpec(memory_space=pl.ANY)
VEC = 16
COST = dict(enter=0, middle=0, back=12, leave=25, gatt=4, ffn=44, units=4, place=0, places=0)


def cost(name):
    return pl.CostEstimate(flops=COST[name] * 10**9 + 1000, bytes_accessed=1000, transcendentals=0)


def shape(*dims, dtype=BF):
    return jax.ShapeDtypeStruct(dims, dtype)


def call(kernel, outs, args, flops, scratch=(), limit=30, name=None):
    return pl.pallas_call(
        kernel,
        out_shape=tuple(outs),
        in_specs=[SMEM_SPEC] * 2 + [VMEM_SPEC] * (len(args) - 2),
        out_specs=tuple([VMEM_SPEC] * len(outs)),
        scratch_shapes=list(scratch),
        compiler_params=pltpu.CompilerParams(vmem_limit_bytes=limit * 2**20),
        cost_estimate=cost(name),
        name=name,
    )(*args)


def allowed_block(lens_ref, kf_ref, b, rows):
    e1 = lens_ref[0, 0]
    e2 = e1 + lens_ref[0, 1]
    tj = lax.broadcasted_iota(jnp.int32, (1, rows), 1)
    ti = lax.broadcasted_iota(jnp.int32, (QB, 1), 0) + b * QB
    sj = (tj >= e1).astype(jnp.int32) + (tj >= e2).astype(jnp.int32)
    si = (ti >= e1).astype(jnp.int32) + (ti >= e2).astype(jnp.int32)
    keep = kf_ref[...] == 1
    return (si == sj) & (keep | (ti == tj))


def window(full, b, rows):
    if b == 0:
        return full[:, :rows]
    return jnp.concatenate([full[:, SPAN - QB * b :], full[:, : rows - QB * b]], axis=1)


def toeplitz(vb_ref, h):
    row = jnp.broadcast_to(vb_ref[h : h + 1, :], (QB, SPAN))
    return pltpu.roll(row, 0, 1, stride=1, stride_axis=0)


def probs(q, k, bias, gate, allowed):
    s = dot_0(q, k) + bias + gate
    s = jnp.where(allowed, s, FILL)
    e = jnp.exp(s - jnp.max(s, axis=1, keepdims=True))
    return e / jnp.sum(e, axis=1, keepdims=True)


def attend(heads, hw, lens_ref, qkv_ref, gate, kf_ref, vb_ref, o_ref):
    rows = qkv_ref.shape[1]
    c = heads * hw
    masks = [allowed_block(lens_ref, kf_ref, b, rows) for b in range(rows // QB)]
    for h in range(heads):
        full = toeplitz(vb_ref, h)
        k = qkv_ref[c + h * hw : c + (h + 1) * hw, :]
        v = qkv_ref[2 * c + h * hw : 2 * c + (h + 1) * hw, :]
        for b in range(rows // QB):
            q = qkv_ref[h * hw : (h + 1) * hw, b * QB : (b + 1) * QB]
            p = probs(q, k, window(full, b, rows), gate, masks[b])
            o_ref[h * hw : (h + 1) * hw, b * QB : (b + 1) * QB] = dot_t(v, p.astype(BF)).astype(BF)


def attend_back(heads, hw, lens_ref, qkv_ref, do_ref, gate, kf_ref, vb_ref, g_ref, t_ref, ds_ref, pl_ref, acc_ref):
    rows = qkv_ref.shape[1]
    c = heads * hw
    masks = [allowed_block(lens_ref, kf_ref, b, rows) for b in range(rows // QB)]
    ones = jnp.ones((VEC, rows), BF)
    dgate = jnp.zeros((VEC, rows), F32)
    t_ref[...] = jnp.zeros_like(t_ref)
    for h in range(heads):
        full = toeplitz(vb_ref, h)
        sl = slice(h * hw, (h + 1) * hw)
        k = qkv_ref[c + h * hw : c + (h + 1) * hw, :]
        v = qkv_ref[2 * c + h * hw : 2 * c + (h + 1) * hw, :]
        acc_ref[...] = jnp.zeros_like(acc_ref)
        for b in range(rows // QB):
            rs = slice(b * QB, (b + 1) * QB)
            p = probs(qkv_ref[sl, rs], k, window(full, b, rows), gate, masks[b])
            dp = dot_0(do_ref[sl, rs], v)
            ds = (p * (dp - jnp.sum(p * dp, axis=1, keepdims=True))).astype(BF)
            ds_ref[rs, :] = ds
            pl_ref[rs, :] = p.astype(BF)
            wide = ds.astype(F32)
            if b == 0:
                acc_ref[:, :rows] += wide
            else:
                acc_ref[:, SPAN - QB * b :] += wide[:, : QB * b]
                acc_ref[:, : rows - QB * b] += wide[:, QB * b :]
        ds_all = ds_ref[...]
        g_ref[sl, :] = dot_t(k, ds_all).astype(BF)
        g_ref[c + h * hw : c + (h + 1) * hw, :] = dot_n(qkv_ref[sl, :], ds_all).astype(BF)
        g_ref[2 * c + h * hw : 2 * c + (h + 1) * hw, :] = dot_n(do_ref[sl, :], pl_ref[...]).astype(BF)
        dgate = dgate + dot_n(ones, ds_all)
        a = acc_ref[...]
        half = QB // 2
        while half >= 8:
            low = a[half:, :]
            a = a[:half, :] + pltpu.roll(low, SPAN - half, 1)
            half //= 2
        tot = a[0:1, :]
        for i in range(1, 8):
            tot = tot + pltpu.roll(a[i : i + 1, :], SPAN - i, 1)
        t_ref[h : h + 1, :] = tot
    g_ref[3 * c :, :] = dgate.astype(BF)


def spots(info_ref, array_ref):
    many, block = array_ref.shape[0], array_ref.shape[2]
    if many == 1:
        return [pl.ds(0, block)]
    return [pl.ds(pl.multiple_of((info_ref[0] ^ k) * block, VEC), block) for k in range(many)]


def spread(w0_ref, k, c, which, rows):
    pickup = (lax.broadcasted_iota(jnp.int32, (VEC, QB), 0) == which).astype(F32).astype(BF)
    block = dot_0(w0_ref[k, 2 * c :, :], pickup)
    return jnp.concatenate([block] * (rows // QB), axis=1)


def inverse_rms(values):
    return lax.rsqrt(jnp.sum(values * values, axis=0, keepdims=True) / values.shape[0] + EPS)


def sum_tokens(values):
    values = sum(values[:, i : i + QB] for i in range(0, values.shape[1], QB))
    high = values.astype(BF)
    rest = (values - high.astype(F32)).astype(BF)
    ones = jnp.ones((8, QB), BF)
    return dot_t(ones, high) + dot_t(ones, rest)


def enter_kernel(heads, hw, info_ref, lens_ref, x_ref, w0_ref, w1_ref, kf_ref, vb_ref, n1_ref, qkv_ref, attn_ref, aux_ref):
    rows = x_ref.shape[1]
    c = heads * hw
    x = x_ref[...].astype(F32)
    r1 = inverse_rms(x)
    half = c // 2
    low = jnp.zeros((2 * c + VEC, rows), F32)
    high = jnp.zeros((c + half, rows), F32)
    for k, spot in enumerate(spots(info_ref, w0_ref)):
        n1 = (x_ref[spot, :].astype(F32) * r1 * spread(w0_ref, k, c, 0, rows)).astype(BF)
        n1_ref[spot, :] = n1
        low = low + dot_n(w0_ref[k], n1)
        high = high + dot_n(w1_ref[k, : c + half, :], n1)
    qkv_ref[: c + half, :] = low[: c + half].astype(BF)
    qkv_ref[c + half :, :] = high.astype(BF)
    z = low[2 * c + 1 : 2 * c + 2]
    gate = (-4.0 * jax.nn.sigmoid(z)).astype(BF).astype(F32)
    aux_ref[...] = jnp.concatenate([z, gate, r1, jnp.zeros((5, rows), F32)], axis=0)
    attend(heads, hw, lens_ref, qkv_ref, gate, kf_ref, vb_ref, attn_ref)


def middle_kernel(
    c, info_ref, lens_ref, x_ref, attn_ref, other_ref, w0_ref, w1_ref, wo0_ref, wo1_ref, aux_ref, h1_ref, n2_ref
):
    rows = x_ref.shape[1]
    half = c // 2
    out = slice(c + half, 2 * c)
    width = x_ref.shape[0]
    total = jnp.zeros((1, rows), F32)
    places = spots(info_ref, w0_ref)
    for k, spot in enumerate(places):
        own = dot_0(w0_ref[k, out, :], attn_ref[:half, :]) + dot_0(w1_ref[k, out, :], attn_ref[half:, :])
        far = dot_0(wo0_ref[k], other_ref[:half, :]) + dot_0(wo1_ref[k], other_ref[half:, :])
        h1 = x_ref[spot, :].astype(F32) + (own.astype(BF).astype(F32) + far.astype(BF).astype(F32))
        h1_ref[spot, :] = h1
        total = total + jnp.sum(h1 * h1, axis=0, keepdims=True)
    r2 = lax.rsqrt(total / width + EPS)
    for k, spot in enumerate(places):
        n2_ref[spot, :] = (h1_ref[spot, :] * r2 * spread(w0_ref, k, c, 2, rows)).astype(BF)
    n2_ref[width:, :] = jnp.broadcast_to(aux_ref[1:2, :], (VEC, rows)).astype(BF)


def back_kernel(
    heads,
    hw,
    info_ref,
    lens_ref,
    low0_ref,
    low1_ref,
    high0_ref,
    high1_ref,
    h1_ref,
    cot_ref,
    w0_ref,
    w1_ref,
    qkv_ref,
    attn_ref,
    aux_ref,
    kf_ref,
    vb_ref,
    dh1_ref,
    slab_ref,
    diag_ref,
    gwo_ref,
    gain_ref,
    u_ref,
    do_ref,
    ds_ref,
    pl_ref,
    acc_ref,
):
    rows = h1_ref.shape[1]
    width = h1_ref.shape[0]
    c = heads * hw
    places = spots(info_ref, w0_ref)
    r2 = inverse_rms(h1_ref[...])
    total = jnp.zeros((1, rows), F32)
    cut = low0_ref.shape[0]
    u_ref[:cut, :] = low0_ref[...].astype(F32) + low1_ref[...].astype(F32)
    u_ref[cut:, :] = high0_ref[...].astype(F32) + high1_ref[...].astype(F32)
    for k, spot in enumerate(places):
        dn2 = u_ref[spot, :]
        u = dn2 * spread(w0_ref, k, c, 2, rows)
        h1 = h1_ref[spot, :]
        total = total + jnp.sum(h1 * u, axis=0, keepdims=True)
        u_ref[spot, :] = u
        gain_ref[k] = sum_tokens(dn2 * h1 * r2)
    back = r2 * r2 * r2 * (total / width)
    half = c // 2
    out = slice(c + half, 2 * c)
    dattn = [jnp.zeros((half, rows), F32)] * 2
    for k, spot in enumerate(places):
        dh1 = cot_ref[0, spot, :].astype(F32) + r2 * u_ref[spot, :] - h1_ref[spot, :] * back
        dh1_ref[spot, :] = dh1
        dhl = dh1.astype(BF)
        dattn = [d + dot_n(w_ref[k, out, :], dhl) for d, w_ref in zip(dattn, (w0_ref, w1_ref))]
        gwo_ref[k] = dot_t(attn_ref[...], dhl).astype(BF)
    do_ref[:half, :] = dattn[0].astype(BF)
    do_ref[half:, :] = dattn[1].astype(BF)
    attend_back(
        heads, hw, lens_ref, qkv_ref, do_ref, aux_ref[1:2, :], kf_ref, vb_ref, slab_ref, diag_ref, ds_ref, pl_ref, acc_ref
    )


def gatt_kernel(c, info_ref, lens_ref, slab_ref, n1_ref, gwo_ref, keep_ref, send_ref):
    many = gwo_ref.shape[0]
    for k, spot in enumerate(spots(info_ref, gwo_ref)):
        at = info_ref[0] ^ k if many > 1 else 0
        n1 = n1_ref[spot, :]
        parts = [dot_t(slab_ref[i * c : (i + 1) * c, :], n1).astype(BF) for i in range(3)] + [gwo_ref[k]]
        for core, refs in enumerate(((keep_ref, send_ref), (send_ref, keep_ref))):

            @pl.when((info_ref[1] & 1) == core)
            def _():
                for i, part in enumerate(parts):
                    refs[i // 2][at, i % 2] = part


def leave_kernel(
    c,
    info_ref,
    lens_ref,
    slab_ref,
    other_ref,
    w0_ref,
    w1_ref,
    far0_ref,
    far1_ref,
    x_ref,
    dh1_ref,
    n1_ref,
    aux_ref,
    o0,
    o1,
    o2,
    o3,
    vec_ref,
    dn_ref,
    dx_ref,
):
    rows = x_ref.shape[1]
    width = x_ref.shape[0]
    half = 3 * c // 2
    places = spots(info_ref, w0_ref)
    z = aux_ref[0:1, :]
    r1 = aux_ref[2:3, :]
    sig = jax.nn.sigmoid(z)
    dgate = (slab_ref[3 * c :, :].astype(F32) + other_ref[3 * c :, :].astype(F32))[0:1]
    dz = dgate * (-4.0 * sig * (1.0 - sig))
    total = jnp.zeros((1, rows), F32)
    for k, spot in enumerate(places):
        own = dot_0(w0_ref[k, :half, :], slab_ref[:half, :]) + dot_0(w1_ref[k, :half, :], slab_ref[half : 2 * half, :])
        far = dot_0(far0_ref[k], other_ref[:half, :]) + dot_0(far1_ref[k], other_ref[half : 2 * half, :])
        dn = own.astype(BF).astype(F32) + far.astype(BF).astype(F32) + spread(w0_ref, k, c, 1, rows) * dz
        u = dn * spread(w0_ref, k, c, 0, rows)
        x = x_ref[spot, :].astype(F32)
        total = total + jnp.sum(x * u, axis=0, keepdims=True)
        dx_ref[spot, :] = u
        vec_ref[k, 0:8, :] = sum_tokens(dn * x * r1)
        vec_ref[k, 8:16, :] = sum_tokens(n1_ref[spot, :].astype(F32) * dz)
    back = r1 * r1 * r1 * (total / width)
    dn_ref[...] = dh1_ref[...] + r1 * dx_ref[...] - x_ref[...].astype(F32) * back
    part = rows // 4
    for k, out in enumerate((o0, o1, o2, o3)):
        at = pl.multiple_of((info_ref[1] ^ k) * part, part)
        out[...] = dn_ref[:, pl.ds(at, part)].astype(BF)


def ffn_kernel(n_pieces, shard, units, info_ref, n0, n1, n2, n3, cot_ref, *refs):
    pieces = refs[:n_pieces]
    o0, o1, o2, o3, grad_ref, w_ref, n_ref, gu_ref, acc_ref, inner_ref, dgu_ref, sems = refs[n_pieces:]
    step = pl.program_id(0)
    per = pl.num_programs(0) // 4
    width = w_ref.shape[0]

    @pl.when(step == 0)
    def _():
        copies = []
        for k in range(n_pieces):
            at = pl.multiple_of((info_ref[0] ^ k) * shard, VEC) if n_pieces > 1 else 0
            copies.append(pltpu.make_async_copy(pieces[k], w_ref.at[pl.ds(at, pieces[k].shape[0])], sems.at[k]))
        for c in copies:
            c.start()
        acc_ref[...] = jnp.zeros_like(acc_ref)
        for c in copies:
            c.wait()

    for k, source in enumerate((n0, n1, n2, n3)):

        @pl.when(step // per == k)
        def _():
            n_ref[...] = source[:width, :]

    gu_ref[: 2 * units, :] = dot_0(w_ref[:, : 2 * units], n_ref[...])
    gu_ref[2 * units :, :] = dot_0(w_ref[:, 2 * units : 3 * units], cot_ref[0])
    c0 = math.sqrt(2.0 / math.pi)
    chunk = units // 14
    for r in range(0, units, chunk):
        ga = gu_ref[r : r + chunk, :]
        up = gu_ref[units + r : units + r + chunk, :]
        din = gu_ref[2 * units + r : 2 * units + r + chunk, :]
        sq = ga * ga
        th = jnp.tanh(c0 * (ga + 0.044715 * ga * sq))
        hf = 0.5 * (1.0 + th)
        act = ga * hf
        slope = hf + 0.5 * ga * (1.0 - th * th) * (c0 + 3.0 * 0.044715 * c0 * sq)
        inner_ref[r : r + chunk, :] = (act * up).astype(BF)
        dgu_ref[r : r + chunk, :] = (din * up * slope).astype(BF)
        dgu_ref[units + r : units + r + chunk, :] = (din * act).astype(BF)
    for k, out in enumerate((o0, o1, o2, o3)):

        @pl.when(step // per == k)
        def _():
            out[0] = dot_n(w_ref[:, : 2 * units], dgu_ref[...]).astype(BF)
            out[1] = dot_n(w_ref[:, 2 * units : 3 * units], inner_ref[...]).astype(BF)

    acc_ref[:, : 2 * units] += dot_t(n_ref[...], dgu_ref[...])
    acc_ref[:, 2 * units : 3 * units] += dot_t(cot_ref[0], inner_ref[...])

    @pl.when(step == 4 * per - 1)
    def _():
        grad_ref[...] = acc_ref[...].astype(BF)


def ffn(info, ns, cot, pieces, shard, units, tile=256):
    width, rows = cot.shape[1:]
    tall = ns[0].shape[0]
    per = rows // tile
    wide = pieces[0].shape[1]
    part = lambda k: lambda i, s: (0, jnp.clip(i - k * per, 0, per - 1))
    part3 = lambda k: lambda i, s: (0, 0, jnp.clip(i - k * per, 0, per - 1))
    return pl.pallas_call(
        lambda *refs: ffn_kernel(len(pieces), shard, units, *refs),
        grid_spec=pltpu.PrefetchScalarGridSpec(
            num_scalar_prefetch=1,
            grid=(4 * per,),
            in_specs=[pl.BlockSpec((tall, tile), part(k)) for k in range(4)]
            + [pl.BlockSpec((1, width, tile), lambda i, s: (i // per, 0, i % per))]
            + [ANY_SPEC] * len(pieces),
            out_specs=[pl.BlockSpec((2, width, tile), part3(k)) for k in range(4)]
            + [pl.BlockSpec((width, wide), lambda i, s: (0, 0))],
            scratch_shapes=[
                pltpu.VMEM((width, wide), BF),
                pltpu.VMEM((width, tile), BF),
                pltpu.VMEM((3 * units, tile), F32),
                pltpu.VMEM((width, wide), F32),
                pltpu.VMEM((units, tile), BF),
                pltpu.VMEM((2 * units, tile), BF),
                pltpu.SemaphoreType.DMA((len(pieces),)),
            ],
        ),
        out_shape=[shape(2, width, rows)] * 4 + [shape(width, wide)],
        compiler_params=pltpu.CompilerParams(vmem_limit_bytes=56 * 2**20),
        cost_estimate=cost("ffn"),
        name="ffn",
    )(info, *ns, cot, *pieces)


def spread_units_kernel(units, info_ref, a, b, c, d, gate_ref, up_ref, down_ref, part_ref):
    for k, source in enumerate((a, b, c, d)):
        part_ref[k] = source[...]
    for i in range(4):
        at = slice(i * units, (i + 1) * units)
        for n, ref in enumerate((gate_ref, up_ref, down_ref)):
            ref[:, at] = part_ref[info_ref[1] ^ i, :, n * units : (n + 1) * units].astype(F32)


def spread_units(info, parts, units):
    rows, wide = parts[0].shape
    tile = rows
    out = pl.BlockSpec((tile, 4 * units), lambda i, s: (i, 0))
    return pl.pallas_call(
        lambda *refs: spread_units_kernel(units, *refs),
        grid_spec=pltpu.PrefetchScalarGridSpec(
            num_scalar_prefetch=1,
            grid=(rows // tile,),
            in_specs=[pl.BlockSpec((tile, wide), lambda i, s: (i, 0))] * 4,
            out_specs=[out] * 3,
            scratch_shapes=[pltpu.VMEM((4, tile, wide), BF)],
        ),
        out_shape=[shape(rows, 4 * units, dtype=F32)] * 3,
        compiler_params=pltpu.CompilerParams(vmem_limit_bytes=40 * 2**20),
        cost_estimate=cost("units"),
        name="units",
    )(info, *parts)


def place_kernel(info_ref, deal_ref, *refs):
    *blocks, out_ref = refs
    rows = out_ref.shape[2]
    hit = lax.broadcasted_iota(jnp.int32, (rows, rows), 0) == deal_ref[0]
    blocks = jnp.concatenate([b[0] for b in blocks], axis=1)
    out_ref[0] = dot_t(blocks, hit.astype(F32).astype(BF)).astype(BF)


def place_tokens(info, deal, blocks):
    many, _, rows = deal.shape
    width, local = blocks[0].shape[-2:]
    if many == 1:
        specs = [pl.BlockSpec((1, width, local), lambda j, s: (0, 0, 0))] * 4
        order = lambda j, s: (0, 0, 0)
    else:
        specs = [pl.BlockSpec((1, width, local), lambda j, s: (s[1] ^ j, 0, 0))] * 4
        order = lambda j, s: (s[1] ^ j, 0, 0)
    return pl.pallas_call(
        place_kernel,
        grid_spec=pltpu.PrefetchScalarGridSpec(
            num_scalar_prefetch=1,
            grid=(many,),
            in_specs=[pl.BlockSpec((1, 1, rows), order)] + specs,
            out_specs=pl.BlockSpec((1, width, rows), lambda j, s: (j, 0, 0)),
        ),
        out_shape=shape(many, width, rows),
        compiler_params=pltpu.CompilerParams(vmem_limit_bytes=48 * 2**20),
        cost_estimate=cost("place" if many == 1 else "places"),
        name="place",
    )(info, deal, *blocks)


def pick(array, index, axis=0):
    return lax.dynamic_index_in_dim(array, index, axis, keepdims=False)


def swap(block, axis):
    return lax.ppermute(block, axis, SWAP)


def cross(block, step):
    if step == 3:
        return lax.ppermute(block, ("cx", "core"), [(0, 3), (1, 2), (2, 1), (3, 0)])
    return swap(block, "core" if step == 1 else "cx")


NEAR = [(0, 1), (1, 0), (2, 3), (3, 2)]
FAR = [(0, 2), (2, 0), (1, 3), (3, 1)]
MID = [(1, 2), (2, 1)]


def gather_dp(piece, count, rank, axis):
    if count != 4:
        return [lax.all_gather(piece, "dp", axis=axis, tiled=True)]
    near = lax.ppermute(piece, "dp", NEAR)
    far = lax.ppermute(piece, "dp", FAR)
    mid = lax.ppermute(piece, "dp", MID)
    passed = lax.ppermute(far, "dp", [(1, 0), (2, 3)])
    return [piece, near, far, jnp.where((rank == 1) | (rank == 2), mid, passed)]


def scatter_dp(parts, axis):
    if len(parts) == 1:
        return lax.psum_scatter(parts[0], "dp", scatter_dimension=axis, tiled=True).astype(F32)
    early = lax.ppermute(parts[3], "dp", [(0, 1), (3, 2)])
    near = lax.ppermute(parts[1], "dp", NEAR)
    mid = lax.ppermute(parts[3], "dp", MID)
    far = lax.ppermute((parts[2].astype(F32) + early.astype(F32)).astype(BF), "dp", FAR)
    return parts[0].astype(F32) + near.astype(F32) + mid.astype(F32) + far.astype(F32)


def in_order(first, second, index):
    return jnp.where(index == 0, first, second), jnp.where(index == 0, second, first)


def xor_list(items, cx, core):
    a, b, c, d = items
    a, b = in_order(a, b, core)
    c, d = in_order(c, d, core)
    (a, c), (b, d) = in_order(a, c, cx), in_order(b, d, cx)
    return [a, b, c, d]


def xor_order(array, axis, cx, core):
    return jnp.concatenate(xor_list([lax.slice_in_dim(array, i, i + 1, axis=axis) for i in range(4)], cx, core), axis)


def body(
    hidden,
    cotangent,
    lengths,
    dealing,
    keep_flags,
    norm1_gain,
    w_query,
    w_key,
    w_value,
    w_out,
    rel_table,
    del_weight,
    norm2_gain,
    w_gate,
    w_up,
    w_down,
):
    count = lax.axis_size("dp")
    rank = lax.axis_index("dp")
    cx = lax.axis_index("cx")
    core = lax.axis_index("core")
    ctx = cx * 2 + core
    local = hidden.shape[1]
    width = hidden.shape[2]
    rows = local * 4
    heads = rel_table.shape[1]
    cols = w_query.shape[1]
    hw = cols // heads
    shard = w_query.shape[0]
    units = w_gate.shape[1] // 4
    info = jnp.stack([rank, ctx]).astype(jnp.int32)

    half = cols // 2
    vectors = jnp.pad(jnp.stack([norm1_gain, del_weight, norm2_gain]), ((0, VEC - 3), (0, 0)))
    rows_qkv = jnp.concatenate([w_query.T, w_key.T, w_value.T], axis=0)
    piece = jnp.concatenate(
        [
            lax.dynamic_slice(rows_qkv, (core * 3 * half, 0), (3 * half, shard)),
            lax.dynamic_slice(w_out, (core * half, 0), (half, shard)),
            vectors,
        ],
        axis=0,
    )
    pieces = gather_dp(piece, count, rank, 1)
    att = jnp.stack(pieces)
    w0, w1 = in_order(att, swap(att, "core"), core)
    wo_other = swap(att[:, 3 * half : 4 * half], "tp")

    def unit_cols(w):
        return lax.dynamic_slice(w, (0, ctx * units), (shard, units))

    wide = -(-3 * units // 128) * 128
    w_piece = jnp.concatenate(
        [unit_cols(w_gate), unit_cols(w_up), unit_cols(w_down.T), jnp.zeros((shard, wide - 3 * units), BF)], axis=1
    )
    w_piece, *_ = lax.optimization_barrier((w_piece, *pieces[1:2]))
    w_ffn = [lax.all_gather(w_piece, "dp", axis=0, tiled=True)]

    deal = xor_order(pick(dealing, ctx).reshape(4, local), 0, cx, core).reshape(1, 1, rows)
    keep = xor_order(pick(keep_flags, ctx).reshape(4, local), 0, cx, core).reshape(rows)
    lens = pick(lengths, ctx)
    hit = deal[0] == jnp.arange(rows, dtype=jnp.int32)[:, None]
    kf = jnp.sum(jnp.where(hit, keep[None, :], 0), axis=1)[None, :]
    onehot = span_onehot()
    vb = lax.dot_general(rel_table, jnp.asarray(onehot, BF), (((0,), (1,)), ((), ())), preferred_element_type=F32)
    vb = jnp.pad(vb, ((0, 8 - heads), (0, 0)))

    hid = jnp.transpose(hidden, (0, 2, 1))
    over = swap(jnp.stack([pick(hid, ctx ^ 2), pick(hid, ctx ^ 3)]), "cx")
    across = swap(jnp.stack([pick(hid, ctx ^ 1), over[1]]), "core")
    x = place_tokens(info, deal, [pick(hid, ctx)[None], across[:1], over[:1], across[1:]])[0]

    cot_own = jnp.transpose(cotangent, (0, 2, 1))
    cot_x = swap(cot_own, "cx")
    n1, qkv, attn, aux = call(
        lambda *refs: enter_kernel(heads, hw, *refs),
        [shape(width, rows), shape(3 * cols, rows), shape(cols, rows), shape(8, rows, dtype=F32)],
        [info, lens, x, w0, w1, kf, vb],
        2 * rows * width * cols * 3 + 4 * rows * rows * cols,
        name="enter",
    )
    attn_other = swap(attn, "tp")
    wo_later, _ = lax.optimization_barrier((wo_other, attn))
    wo0_other, wo1_other = in_order(wo_other, swap(wo_later, "core"), core)
    h1, n2 = call(
        lambda *refs: middle_kernel(cols, *refs),
        [shape(width, rows, dtype=F32), shape(width + VEC, rows)],
        [info, lens, x, attn, attn_other, w0, w1, wo0_other, wo1_other, aux],
        2 * rows * width * cols * 2,
        name="middle",
    )

    n2, cot_x = lax.optimization_barrier((n2, cot_x))
    deals = xor_order(dealing.reshape(4, 4, local), 1, cx, core).reshape(4, 1, rows)
    cot = place_tokens(info, deals, [cot_own, swap(cot_own, "core"), cot_x, swap(cot_x, "core")])

    att_later, _ = lax.optimization_barrier((att[:, : 3 * half], attn_other))
    att_other = swap(att_later, "tp")
    n2_core = swap(n2, "core")
    n2_x = swap(n2, "cx")
    n2_x, cot, att_other = lax.optimization_barrier((n2_x, cot, att_other))
    n2_all = [n2, n2_core, n2_x, swap(n2_x, "core")]
    gates = [lax.dynamic_slice(n, (width, ctx * local), (1, local)) for n in n2_all]
    gates = jnp.concatenate(xor_list(gates, cx, core), axis=0)
    w0_other, w1_other = in_order(att_other, swap(att_other, "core"), core)
    n2_all[3], w0_other, w1_other = lax.optimization_barrier((n2_all[3], w0_other, w1_other))
    keep_b, send_b, keep_a, send_a, parts = ffn(info, n2_all, cot, w_ffn, shard, units)
    got_a = swap(send_a, "core")
    got_b = swap(send_b, "core")

    def both(kept, got, i, low=0, high=width):
        return kept[i][low:high].astype(F32) + got[i][low:high].astype(F32)

    cut = width // 48 * 16
    first = jnp.stack([both(keep_a, got_a, 0, 0, cut).astype(BF), both(keep_b, got_b, 0, 0, cut).astype(BF)])
    first = first.astype(F32) + swap(first, "tp").astype(F32)
    late_x = swap(both(keep_a, got_a, 0, cut).astype(BF), "cx")
    late_own = (both(keep_b, got_b, 0, cut) + late_x.astype(F32)).astype(BF)
    dn_pairs = [first[1].astype(BF), swap(first[0].astype(BF), "cx"), late_own, swap(late_own, "tp")]
    bf_over, _ = lax.optimization_barrier((both(keep_a, got_a, 1).astype(BF), dn_pairs[1]))
    bf_x, _ = lax.optimization_barrier((swap(bf_over, "cx"), dn_pairs[3]))
    bf_own = (both(keep_b, got_b, 1) + bf_x.astype(F32)).astype(BF)
    g_ffn = scatter_dp([parts], 0).astype(BF)
    blocks_of = att.shape[0]
    dh1, slab, diag, g_wo, g_gain2 = call(
        lambda *refs: back_kernel(heads, hw, *refs),
        [
            shape(width, rows, dtype=F32),
            shape(3 * cols + VEC, rows),
            shape(8, SPAN, dtype=F32),
            shape(blocks_of, cols, width // blocks_of),
            shape(blocks_of, 8, width // blocks_of, dtype=F32),
        ],
        [info, lens, *dn_pairs, h1, cot[:1], w0, w1, qkv, attn, aux, kf, vb],
        2 * rows * width * cols * 2 + 10 * rows * rows * cols,
        scratch=[
            pltpu.VMEM((width, rows), F32),
            pltpu.VMEM((cols, rows), BF),
            pltpu.VMEM((rows, rows), BF),
            pltpu.VMEM((rows, rows), BF),
            pltpu.VMEM((QB, SPAN), F32),
        ],
        name="back",
    )
    slab_other = swap(slab, "tp")
    g_ffn, _ = lax.optimization_barrier((g_ffn, slab))
    grads, sent = call(
        lambda *refs: gatt_kernel(cols, *refs),
        [shape(blocks_of, 2, cols, width // blocks_of)] * 2,
        [info, lens, slab, n1, g_wo],
        2 * rows * width * cols * 3,
        limit=48,
        name="gatt",
    )
    sent = swap(sent, "core")
    slab_other, bf_own, g_ffn, sent = lax.optimization_barrier((slab_other, bf_own, g_ffn, sent))
    grads = (grads.astype(F32) + sent.astype(F32)).astype(BF)
    if blocks_of == 1:
        grads = jnp.transpose(grads[0].reshape(2, cols, count, shard), (2, 0, 1, 3))
    grads = grads.reshape(count * 2 * cols, shard)
    grads = lax.psum_scatter(grads, "dp", scatter_dimension=0, tiled=True)
    bf_other = swap(bf_own, "tp")
    g_x = swap(g_ffn, "cx")
    *dx, vec = call(
        lambda *refs: leave_kernel(cols, *refs),
        [shape(width, local)] * 4 + [shape(blocks_of, 16, width // blocks_of, dtype=F32)],
        [info, lens, slab, slab_other, w0, w1, w0_other, w1_other, x, dh1, n1, aux],
        2 * rows * width * cols * 6,
        scratch=[pltpu.VMEM((width, rows), F32), pltpu.VMEM((width, rows), F32)],
        limit=48,
        name="leave",
    )

    table = lax.dot_general(
        diag[:heads], jnp.asarray(onehot), (((1,), (0,)), ((), ())), precision=lax.Precision.HIGHEST
    )
    bw = width // blocks_of
    size = table.size // 8
    flat = jnp.broadcast_to(jnp.pad(table.reshape(1, 8, size), ((0, 0), (0, 0), (0, bw - size))), (blocks_of, 8, bw))
    sums = jnp.concatenate([vec, g_gain2, flat], axis=1)

    def deal_out(items):
        return [items[0]] + [cross(items[k], k) for k in range(1, 4)]

    def arrange(got):
        return jnp.transpose(jnp.stack(xor_list(got, cx, core)), (0, 2, 1))

    def block_of(k):
        total = sum(
            lax.dynamic_slice(a, (0, (ctx ^ k) * local), (width, local)).astype(F32) for a in (h1, bf_own, bf_other)
        )
        return total.astype(BF)

    *dx, g_x, core_sums = lax.optimization_barrier((*dx, g_x, swap(sums, "core")))
    dx = deal_out(dx)
    sums = sums + core_sums
    bf_other, dx[1], x_sums = lax.optimization_barrier((bf_other, dx[1], swap(sums, "cx")))
    sums = sums + x_sums
    far = lax.ppermute(sums[2:], "dp", FAR) if count == 4 else sums
    out = deal_out([block_of(k) for k in range(4)])
    g_gate, g_up, g_down = spread_units(info, [g_ffn, swap(g_ffn, "core"), g_x, swap(g_x, "core")], units)
    out[1], grads, far, g_gate = lax.optimization_barrier((out[1], grads, far, g_gate))
    if count == 4:
        sums = sums[:2] + far
        near = lax.ppermute(sums[1], "dp", NEAR)
    else:
        near = lax.psum(far, "dp")
    out[2], grads_x, near = lax.optimization_barrier((out[2], swap(grads, "cx"), near))
    grads = (grads.astype(F32) + grads_x.astype(F32)).astype(BF)
    g_weights = jnp.concatenate(in_order(grads, swap(grads, "core"), core), axis=0).astype(F32)
    g_weights = g_weights.reshape(4, cols, shard)
    if count == 4:
        sums = sums[0] + near
        vec = sums[:24:8]
    else:
        sums = near[0]
        vec = lax.dynamic_slice(sums[:24:8], (0, rank * shard), (3, shard))
    table = sums[24:, :size].reshape(table.shape).T

    return (
        arrange(out),
        gates,
        arrange(dx),
        vec[0],
        g_weights[0].T,
        g_weights[1].T,
        g_weights[2].T,
        g_weights[3],
        table,
        vec[1],
        vec[2],
        g_gate,
        g_up,
        g_down.T,
    )


def solution(mesh):
    dp, ctx, tp = (mesh.shape[name] for name in ("dp", "ctx", "tp"))
    split = Mesh(mesh.devices.reshape(dp, 2, ctx // 2, tp), ("dp", "cx", "core", "tp"))
    tokens = P(None, ("dp", "cx", "core"), None)
    in_specs = (
        tokens,
        tokens,
        P(None, "dp", None),
        P(None, "dp", None),
        P(None, "dp", None),
        P("dp"),
        P("dp", "tp"),
        P("dp", "tp"),
        P("dp", "tp"),
        P("tp", "dp"),
        P(None, "tp"),
        P("dp"),
        P("dp"),
        P("dp", "tp"),
        P("dp", "tp"),
        P("tp", "dp"),
    )
    out_specs = (
        tokens,
        P(None, ("dp", "cx", "core")),
        tokens,
        P("dp"),
        P("dp", "tp"),
        P("dp", "tp"),
        P("dp", "tp"),
        P("tp", "dp"),
        P(None, "tp"),
        P("dp"),
        P("dp"),
        P("dp", "tp"),
        P("dp", "tp"),
        P("tp", "dp"),
    )
    return jax.shard_map(body, mesh=split, in_specs=in_specs, out_specs=out_specs, check_vma=False)
```

```python
import math

import numpy as np

import jax
import jax.numpy as jnp
from jax import lax
from jax.experimental import pallas as pl
from jax.experimental.pallas import tpu as pltpu
from jax.sharding import Mesh, PartitionSpec as P

BUCKETS = 32
MAX_DIST = 128
EPS = 1e-06
FILL = -1e30
BF = jnp.bfloat16
F32 = jnp.float32
SWAP = [(0, 1), (1, 0)]
SPAN = 1024
QB = 128


def bucket_np(relative):
    half_count = BUCKETS // 2
    exact_count = half_count // 2
    distance = np.abs(relative)
    ratio_bits = math.log2(MAX_DIST / exact_count)
    far = np.full(distance.shape, exact_count, np.int32)
    for level in range(1, half_count - exact_count):
        border = math.ceil(exact_count * 2.0 ** (level * ratio_bits / (half_count - exact_count)))
        far = far + (distance >= border).astype(np.int32)
    chosen = np.where(distance < exact_count, distance, far)
    return chosen + half_count * (relative > 0).astype(np.int32)


def span_onehot():
    k = np.arange(SPAN)
    d = np.where(k < SPAN // 2, k, k - SPAN)
    return (bucket_np(d)[:, None] == np.arange(BUCKETS)[None, :]).astype(np.float32)


def dot_n(a, b):
    return lax.dot_general(a, b, (((1,), (0,)), ((), ())), preferred_element_type=F32)


def dot_t(a, b):
    return lax.dot_general(a, b, (((1,), (1,)), ((), ())), preferred_element_type=F32)


def dot_0(a, b):
    return lax.dot_general(a, b, (((0,), (0,)), ((), ())), preferred_element_type=F32)


SMEM_SPEC = pl.BlockSpec(memory_space=pltpu.SMEM)
VMEM_SPEC = pl.BlockSpec(memory_space=pltpu.VMEM)
ANY_SPEC = pl.BlockSpec(memory_space=pl.ANY)
VEC = 16
COST = dict(enter=0, middle=0, back=12, leave=25, gatt=4, ffn=44, units=4, place=0, places=0)


def cost(name):
    return pl.CostEstimate(flops=COST[name] * 10**9 + 1000, bytes_accessed=1000, transcendentals=0)


def shape(*dims, dtype=BF):
    return jax.ShapeDtypeStruct(dims, dtype)


def call(kernel, outs, args, flops, scratch=(), limit=30, name=None):
    return pl.pallas_call(
        kernel,
        out_shape=tuple(outs),
        in_specs=[SMEM_SPEC] * 2 + [VMEM_SPEC] * (len(args) - 2),
        out_specs=tuple([VMEM_SPEC] * len(outs)),
        scratch_shapes=list(scratch),
        compiler_params=pltpu.CompilerParams(vmem_limit_bytes=limit * 2**20),
        cost_estimate=cost(name),
        name=name,
    )(*args)


def allowed_block(lens_ref, kf_ref, b, rows):
    e1 = lens_ref[0, 0]
    e2 = e1 + lens_ref[0, 1]
    tj = lax.broadcasted_iota(jnp.int32, (1, rows), 1)
    ti = lax.broadcasted_iota(jnp.int32, (QB, 1), 0) + b * QB
    sj = (tj >= e1).astype(jnp.int32) + (tj >= e2).astype(jnp.int32)
    si = (ti >= e1).astype(jnp.int32) + (ti >= e2).astype(jnp.int32)
    keep = kf_ref[...] == 1
    return (si == sj) & (keep | (ti == tj))


def window(full, b, rows):
    if b == 0:
        return full[:, :rows]
    return jnp.concatenate([full[:, SPAN - QB * b :], full[:, : rows - QB * b]], axis=1)


def toeplitz(vb_ref, h):
    row = jnp.broadcast_to(vb_ref[h : h + 1, :], (QB, SPAN))
    return pltpu.roll(row, 0, 1, stride=1, stride_axis=0)


def probs(q, k, bias, gate, allowed):
    s = dot_0(q, k) + bias + gate
    s = jnp.where(allowed, s, FILL)
    e = jnp.exp(s - jnp.max(s, axis=1, keepdims=True))
    return e / jnp.sum(e, axis=1, keepdims=True)


def attend(heads, hw, lens_ref, qkv_ref, gate, kf_ref, vb_ref, o_ref):
    rows = qkv_ref.shape[1]
    c = heads * hw
    masks = [allowed_block(lens_ref, kf_ref, b, rows) for b in range(rows // QB)]
    for h in range(heads):
        full = toeplitz(vb_ref, h)
        k = qkv_ref[c + h * hw : c + (h + 1) * hw, :]
        v = qkv_ref[2 * c + h * hw : 2 * c + (h + 1) * hw, :]
        for b in range(rows // QB):
            q = qkv_ref[h * hw : (h + 1) * hw, b * QB : (b + 1) * QB]
            p = probs(q, k, window(full, b, rows), gate, masks[b])
            o_ref[h * hw : (h + 1) * hw, b * QB : (b + 1) * QB] = dot_t(v, p.astype(BF)).astype(BF)


def attend_back(heads, hw, lens_ref, qkv_ref, do_ref, gate, kf_ref, vb_ref, g_ref, t_ref, ds_ref, pl_ref, acc_ref):
    rows = qkv_ref.shape[1]
    c = heads * hw
    masks = [allowed_block(lens_ref, kf_ref, b, rows) for b in range(rows // QB)]
    ones = jnp.ones((VEC, rows), BF)
    dgate = jnp.zeros((VEC, rows), F32)
    t_ref[...] = jnp.zeros_like(t_ref)
    for h in range(heads):
        full = toeplitz(vb_ref, h)
        sl = slice(h * hw, (h + 1) * hw)
        k = qkv_ref[c + h * hw : c + (h + 1) * hw, :]
        v = qkv_ref[2 * c + h * hw : 2 * c + (h + 1) * hw, :]
        acc_ref[...] = jnp.zeros_like(acc_ref)
        for b in range(rows // QB):
            rs = slice(b * QB, (b + 1) * QB)
            p = probs(qkv_ref[sl, rs], k, window(full, b, rows), gate, masks[b])
            dp = dot_0(do_ref[sl, rs], v)
            ds = (p * (dp - jnp.sum(p * dp, axis=1, keepdims=True))).astype(BF)
            ds_ref[rs, :] = ds
            pl_ref[rs, :] = p.astype(BF)
            wide = ds.astype(F32)
            if b == 0:
                acc_ref[:, :rows] += wide
            else:
                acc_ref[:, SPAN - QB * b :] += wide[:, : QB * b]
                acc_ref[:, : rows - QB * b] += wide[:, QB * b :]
        ds_all = ds_ref[...]
        g_ref[sl, :] = dot_t(k, ds_all).astype(BF)
        g_ref[c + h * hw : c + (h + 1) * hw, :] = dot_n(qkv_ref[sl, :], ds_all).astype(BF)
        g_ref[2 * c + h * hw : 2 * c + (h + 1) * hw, :] = dot_n(do_ref[sl, :], pl_ref[...]).astype(BF)
        dgate = dgate + dot_n(ones, ds_all)
        a = acc_ref[...]
        half = QB // 2
        while half >= 8:
            low = a[half:, :]
            a = a[:half, :] + pltpu.roll(low, SPAN - half, 1)
            half //= 2
        tot = a[0:1, :]
        for i in range(1, 8):
            tot = tot + pltpu.roll(a[i : i + 1, :], SPAN - i, 1)
        t_ref[h : h + 1, :] = tot
    g_ref[3 * c :, :] = dgate.astype(BF)


def spots(info_ref, array_ref):
    many, block = array_ref.shape[0], array_ref.shape[2]
    if many == 1:
        return [pl.ds(0, block)]
    return [pl.ds(pl.multiple_of((info_ref[0] ^ k) * block, VEC), block) for k in range(many)]


def spread(w0_ref, k, c, which, rows):
    pickup = (lax.broadcasted_iota(jnp.int32, (VEC, QB), 0) == which).astype(F32).astype(BF)
    block = dot_0(w0_ref[k, 2 * c :, :], pickup)
    return jnp.concatenate([block] * (rows // QB), axis=1)


def inverse_rms(values):
    return lax.rsqrt(jnp.sum(values * values, axis=0, keepdims=True) / values.shape[0] + EPS)


def sum_tokens(values):
    values = sum(values[:, i : i + QB] for i in range(0, values.shape[1], QB))
    high = values.astype(BF)
    rest = (values - high.astype(F32)).astype(BF)
    ones = jnp.ones((8, QB), BF)
    return dot_t(ones, high) + dot_t(ones, rest)


def enter_kernel(heads, hw, info_ref, lens_ref, x_ref, w0_ref, w1_ref, kf_ref, vb_ref, n1_ref, qkv_ref, attn_ref, aux_ref):
    rows = x_ref.shape[1]
    c = heads * hw
    x = x_ref[...].astype(F32)
    r1 = inverse_rms(x)
    half = c // 2
    low = jnp.zeros((2 * c + VEC, rows), F32)
    high = jnp.zeros((c + half, rows), F32)
    for k, spot in enumerate(spots(info_ref, w0_ref)):
        n1 = (x_ref[spot, :].astype(F32) * r1 * spread(w0_ref, k, c, 0, rows)).astype(BF)
        n1_ref[spot, :] = n1
        low = low + dot_n(w0_ref[k], n1)
        high = high + dot_n(w1_ref[k, : c + half, :], n1)
    qkv_ref[: c + half, :] = low[: c + half].astype(BF)
    qkv_ref[c + half :, :] = high.astype(BF)
    z = low[2 * c + 1 : 2 * c + 2]
    gate = (-4.0 * jax.nn.sigmoid(z)).astype(BF).astype(F32)
    aux_ref[...] = jnp.concatenate([z, gate, r1, jnp.zeros((5, rows), F32)], axis=0)
    attend(heads, hw, lens_ref, qkv_ref, gate, kf_ref, vb_ref, attn_ref)


def middle_kernel(
    c, info_ref, lens_ref, x_ref, attn_ref, other_ref, w0_ref, w1_ref, wo0_ref, wo1_ref, aux_ref, h1_ref, n2_ref
):
    rows = x_ref.shape[1]
    half = c // 2
    out = slice(c + half, 2 * c)
    width = x_ref.shape[0]
    total = jnp.zeros((1, rows), F32)
    places = spots(info_ref, w0_ref)
    for k, spot in enumerate(places):
        own = dot_0(w0_ref[k, out, :], attn_ref[:half, :]) + dot_0(w1_ref[k, out, :], attn_ref[half:, :])
        far = dot_0(wo0_ref[k], other_ref[:half, :]) + dot_0(wo1_ref[k], other_ref[half:, :])
        h1 = x_ref[spot, :].astype(F32) + (own.astype(BF).astype(F32) + far.astype(BF).astype(F32))
        h1_ref[spot, :] = h1
        total = total + jnp.sum(h1 * h1, axis=0, keepdims=True)
    r2 = lax.rsqrt(total / width + EPS)
    for k, spot in enumerate(places):
        n2_ref[spot, :] = (h1_ref[spot, :] * r2 * spread(w0_ref, k, c, 2, rows)).astype(BF)
    n2_ref[width:, :] = jnp.broadcast_to(aux_ref[1:2, :], (VEC, rows)).astype(BF)


def back_kernel(
    heads,
    hw,
    info_ref,
    lens_ref,
    low0_ref,
    low1_ref,
    high0_ref,
    high1_ref,
    h1_ref,
    cot_ref,
    w0_ref,
    w1_ref,
    qkv_ref,
    attn_ref,
    aux_ref,
    kf_ref,
    vb_ref,
    dh1_ref,
    slab_ref,
    diag_ref,
    gwo_ref,
    gain_ref,
    u_ref,
    do_ref,
    ds_ref,
    pl_ref,
    acc_ref,
):
    rows = h1_ref.shape[1]
    width = h1_ref.shape[0]
    c = heads * hw
    places = spots(info_ref, w0_ref)
    r2 = inverse_rms(h1_ref[...])
    total = jnp.zeros((1, rows), F32)
    cut = low0_ref.shape[0]
    u_ref[:cut, :] = low0_ref[...].astype(F32) + low1_ref[...].astype(F32)
    u_ref[cut:, :] = high0_ref[...].astype(F32) + high1_ref[...].astype(F32)
    for k, spot in enumerate(places):
        dn2 = u_ref[spot, :]
        u = dn2 * spread(w0_ref, k, c, 2, rows)
        h1 = h1_ref[spot, :]
        total = total + jnp.sum(h1 * u, axis=0, keepdims=True)
        u_ref[spot, :] = u
        gain_ref[k] = sum_tokens(dn2 * h1 * r2)
    back = r2 * r2 * r2 * (total / width)
    half = c // 2
    out = slice(c + half, 2 * c)
    dattn = [jnp.zeros((half, rows), F32)] * 2
    for k, spot in enumerate(places):
        dh1 = cot_ref[0, spot, :].astype(F32) + r2 * u_ref[spot, :] - h1_ref[spot, :] * back
        dh1_ref[spot, :] = dh1
        dhl = dh1.astype(BF)
        dattn = [d + dot_n(w_ref[k, out, :], dhl) for d, w_ref in zip(dattn, (w0_ref, w1_ref))]
        gwo_ref[k] = dot_t(attn_ref[...], dhl).astype(BF)
    do_ref[:half, :] = dattn[0].astype(BF)
    do_ref[half:, :] = dattn[1].astype(BF)
    attend_back(
        heads, hw, lens_ref, qkv_ref, do_ref, aux_ref[1:2, :], kf_ref, vb_ref, slab_ref, diag_ref, ds_ref, pl_ref, acc_ref
    )


def gatt_kernel(c, info_ref, lens_ref, slab_ref, n1_ref, gwo_ref, keep_ref, send_ref):
    many = gwo_ref.shape[0]
    for k, spot in enumerate(spots(info_ref, gwo_ref)):
        at = info_ref[0] ^ k if many > 1 else 0
        n1 = n1_ref[spot, :]
        parts = [dot_t(slab_ref[i * c : (i + 1) * c, :], n1).astype(BF) for i in range(3)] + [gwo_ref[k]]
        for core, refs in enumerate(((keep_ref, send_ref), (send_ref, keep_ref))):

            @pl.when((info_ref[1] & 1) == core)
            def _():
                for i, part in enumerate(parts):
                    refs[i // 2][at, i % 2] = part


def leave_kernel(
    c,
    info_ref,
    lens_ref,
    slab_ref,
    other_ref,
    w0_ref,
    w1_ref,
    far0_ref,
    far1_ref,
    x_ref,
    dh1_ref,
    n1_ref,
    aux_ref,
    o0,
    o1,
    o2,
    o3,
    vec_ref,
    dn_ref,
    dx_ref,
):
    rows = x_ref.shape[1]
    width = x_ref.shape[0]
    half = 3 * c // 2
    places = spots(info_ref, w0_ref)
    z = aux_ref[0:1, :]
    r1 = aux_ref[2:3, :]
    sig = jax.nn.sigmoid(z)
    dgate = (slab_ref[3 * c :, :].astype(F32) + other_ref[3 * c :, :].astype(F32))[0:1]
    dz = dgate * (-4.0 * sig * (1.0 - sig))
    total = jnp.zeros((1, rows), F32)
    for k, spot in enumerate(places):
        own = dot_0(w0_ref[k, :half, :], slab_ref[:half, :]) + dot_0(w1_ref[k, :half, :], slab_ref[half : 2 * half, :])
        far = dot_0(far0_ref[k], other_ref[:half, :]) + dot_0(far1_ref[k], other_ref[half : 2 * half, :])
        dn = own.astype(BF).astype(F32) + far.astype(BF).astype(F32) + spread(w0_ref, k, c, 1, rows) * dz
        u = dn * spread(w0_ref, k, c, 0, rows)
        x = x_ref[spot, :].astype(F32)
        total = total + jnp.sum(x * u, axis=0, keepdims=True)
        dx_ref[spot, :] = u
        vec_ref[k, 0:8, :] = sum_tokens(dn * x * r1)
        vec_ref[k, 8:16, :] = sum_tokens(n1_ref[spot, :].astype(F32) * dz)
    back = r1 * r1 * r1 * (total / width)
    dn_ref[...] = dh1_ref[...] + r1 * dx_ref[...] - x_ref[...].astype(F32) * back
    part = rows // 4
    for k, out in enumerate((o0, o1, o2, o3)):
        at = pl.multiple_of((info_ref[1] ^ k) * part, part)
        out[...] = dn_ref[:, pl.ds(at, part)].astype(BF)


def ffn_kernel(n_pieces, shard, units, info_ref, n0, n1, n2, n3, cot_ref, *refs):
    pieces = refs[:n_pieces]
    o0, o1, o2, o3, grad_ref, w_ref, n_ref, gu_ref, acc_ref, inner_ref, dgu_ref, sems = refs[n_pieces:]
    step = pl.program_id(0)
    per = pl.num_programs(0) // 4
    width = w_ref.shape[0]

    @pl.when(step == 0)
    def _():
        copies = []
        for k in range(n_pieces):
            at = pl.multiple_of((info_ref[0] ^ k) * shard, VEC) if n_pieces > 1 else 0
            copies.append(pltpu.make_async_copy(pieces[k], w_ref.at[pl.ds(at, pieces[k].shape[0])], sems.at[k]))
        for c in copies:
            c.start()
        acc_ref[...] = jnp.zeros_like(acc_ref)
        for c in copies:
            c.wait()

    for k, source in enumerate((n0, n1, n2, n3)):

        @pl.when(step // per == k)
        def _():
            n_ref[...] = source[:width, :]

    gu_ref[: 2 * units, :] = dot_0(w_ref[:, : 2 * units], n_ref[...])
    gu_ref[2 * units :, :] = dot_0(w_ref[:, 2 * units : 3 * units], cot_ref[0])
    c0 = math.sqrt(2.0 / math.pi)
    chunk = units // 14
    for r in range(0, units, chunk):
        ga = gu_ref[r : r + chunk, :]
        up = gu_ref[units + r : units + r + chunk, :]
        din = gu_ref[2 * units + r : 2 * units + r + chunk, :]
        sq = ga * ga
        th = jnp.tanh(c0 * (ga + 0.044715 * ga * sq))
        hf = 0.5 * (1.0 + th)
        act = ga * hf
        slope = hf + 0.5 * ga * (1.0 - th * th) * (c0 + 3.0 * 0.044715 * c0 * sq)
        inner_ref[r : r + chunk, :] = (act * up).astype(BF)
        dgu_ref[r : r + chunk, :] = (din * up * slope).astype(BF)
        dgu_ref[units + r : units + r + chunk, :] = (din * act).astype(BF)
    for k, out in enumerate((o0, o1, o2, o3)):

        @pl.when(step // per == k)
        def _():
            out[0] = dot_n(w_ref[:, : 2 * units], dgu_ref[...]).astype(BF)
            out[1] = dot_n(w_ref[:, 2 * units : 3 * units], inner_ref[...]).astype(BF)

    acc_ref[:, : 2 * units] += dot_t(n_ref[...], dgu_ref[...])
    acc_ref[:, 2 * units : 3 * units] += dot_t(cot_ref[0], inner_ref[...])

    @pl.when(step == 4 * per - 1)
    def _():
        grad_ref[...] = acc_ref[...].astype(BF)


def ffn(info, ns, cot, pieces, shard, units, tile=256):
    width, rows = cot.shape[1:]
    tall = ns[0].shape[0]
    per = rows // tile
    wide = pieces[0].shape[1]
    part = lambda k: lambda i, s: (0, jnp.clip(i - k * per, 0, per - 1))
    part3 = lambda k: lambda i, s: (0, 0, jnp.clip(i - k * per, 0, per - 1))
    return pl.pallas_call(
        lambda *refs: ffn_kernel(len(pieces), shard, units, *refs),
        grid_spec=pltpu.PrefetchScalarGridSpec(
            num_scalar_prefetch=1,
            grid=(4 * per,),
            in_specs=[pl.BlockSpec((tall, tile), part(k)) for k in range(4)]
            + [pl.BlockSpec((1, width, tile), lambda i, s: (i // per, 0, i % per))]
            + [ANY_SPEC] * len(pieces),
            out_specs=[pl.BlockSpec((2, width, tile), part3(k)) for k in range(4)]
            + [pl.BlockSpec((width, wide), lambda i, s: (0, 0))],
            scratch_shapes=[
                pltpu.VMEM((width, wide), BF),
                pltpu.VMEM((width, tile), BF),
                pltpu.VMEM((3 * units, tile), F32),
                pltpu.VMEM((width, wide), F32),
                pltpu.VMEM((units, tile), BF),
                pltpu.VMEM((2 * units, tile), BF),
                pltpu.SemaphoreType.DMA((len(pieces),)),
            ],
        ),
        out_shape=[shape(2, width, rows)] * 4 + [shape(width, wide)],
        compiler_params=pltpu.CompilerParams(vmem_limit_bytes=56 * 2**20),
        cost_estimate=cost("ffn"),
        name="ffn",
    )(info, *ns, cot, *pieces)


def spread_units_kernel(units, info_ref, a, b, c, d, gate_ref, up_ref, down_ref, part_ref):
    for k, source in enumerate((a, b, c, d)):
        part_ref[k] = source[...]
    for i in range(4):
        at = slice(i * units, (i + 1) * units)
        for n, ref in enumerate((gate_ref, up_ref, down_ref)):
            ref[:, at] = part_ref[info_ref[1] ^ i, :, n * units : (n + 1) * units].astype(F32)


def spread_units(info, parts, units):
    rows, wide = parts[0].shape
    tile = rows
    out = pl.BlockSpec((tile, 4 * units), lambda i, s: (i, 0))
    return pl.pallas_call(
        lambda *refs: spread_units_kernel(units, *refs),
        grid_spec=pltpu.PrefetchScalarGridSpec(
            num_scalar_prefetch=1,
            grid=(rows // tile,),
            in_specs=[pl.BlockSpec((tile, wide), lambda i, s: (i, 0))] * 4,
            out_specs=[out] * 3,
            scratch_shapes=[pltpu.VMEM((4, tile, wide), BF)],
        ),
        out_shape=[shape(rows, 4 * units, dtype=F32)] * 3,
        compiler_params=pltpu.CompilerParams(vmem_limit_bytes=40 * 2**20),
        cost_estimate=cost("units"),
        name="units",
    )(info, *parts)


def place_kernel(info_ref, deal_ref, *refs):
    *blocks, out_ref = refs
    rows = out_ref.shape[2]
    hit = lax.broadcasted_iota(jnp.int32, (rows, rows), 0) == deal_ref[0]
    blocks = jnp.concatenate([b[0] for b in blocks], axis=1)
    out_ref[0] = dot_t(blocks, hit.astype(F32).astype(BF)).astype(BF)


def place_tokens(info, deal, blocks):
    many, _, rows = deal.shape
    width, local = blocks[0].shape[-2:]
    if many == 1:
        specs = [pl.BlockSpec((1, width, local), lambda j, s: (0, 0, 0))] * 4
        order = lambda j, s: (0, 0, 0)
    else:
        specs = [pl.BlockSpec((1, width, local), lambda j, s: (s[1] ^ j, 0, 0))] * 4
        order = lambda j, s: (s[1] ^ j, 0, 0)
    return pl.pallas_call(
        place_kernel,
        grid_spec=pltpu.PrefetchScalarGridSpec(
            num_scalar_prefetch=1,
            grid=(many,),
            in_specs=[pl.BlockSpec((1, 1, rows), order)] + specs,
            out_specs=pl.BlockSpec((1, width, rows), lambda j, s: (j, 0, 0)),
        ),
        out_shape=shape(many, width, rows),
        compiler_params=pltpu.CompilerParams(vmem_limit_bytes=48 * 2**20),
        cost_estimate=cost("place" if many == 1 else "places"),
        name="place",
    )(info, deal, *blocks)


def pick(array, index, axis=0):
    return lax.dynamic_index_in_dim(array, index, axis, keepdims=False)


def swap(block, axis):
    return lax.ppermute(block, axis, SWAP)


def cross(block, step):
    if step == 3:
        return lax.ppermute(block, ("cx", "core"), [(0, 3), (1, 2), (2, 1), (3, 0)])
    return swap(block, "core" if step == 1 else "cx")


NEAR = [(0, 1), (1, 0), (2, 3), (3, 2)]
FAR = [(0, 2), (2, 0), (1, 3), (3, 1)]
MID = [(1, 2), (2, 1)]


def gather_dp(piece, count, rank, axis):
    if count != 4:
        return [lax.all_gather(piece, "dp", axis=axis, tiled=True)]
    near = lax.ppermute(piece, "dp", NEAR)
    far = lax.ppermute(piece, "dp", FAR)
    mid = lax.ppermute(piece, "dp", MID)
    passed = lax.ppermute(far, "dp", [(1, 0), (2, 3)])
    return [piece, near, far, jnp.where((rank == 1) | (rank == 2), mid, passed)]


def scatter_dp(parts, axis):
    if len(parts) == 1:
        return lax.psum_scatter(parts[0], "dp", scatter_dimension=axis, tiled=True).astype(F32)
    early = lax.ppermute(parts[3], "dp", [(0, 1), (3, 2)])
    near = lax.ppermute(parts[1], "dp", NEAR)
    mid = lax.ppermute(parts[3], "dp", MID)
    far = lax.ppermute((parts[2].astype(F32) + early.astype(F32)).astype(BF), "dp", FAR)
    return parts[0].astype(F32) + near.astype(F32) + mid.astype(F32) + far.astype(F32)


def in_order(first, second, index):
    return jnp.where(index == 0, first, second), jnp.where(index == 0, second, first)


def xor_list(items, cx, core):
    a, b, c, d = items
    a, b = in_order(a, b, core)
    c, d = in_order(c, d, core)
    (a, c), (b, d) = in_order(a, c, cx), in_order(b, d, cx)
    return [a, b, c, d]


def xor_order(array, axis, cx, core):
    return jnp.concatenate(xor_list([lax.slice_in_dim(array, i, i + 1, axis=axis) for i in range(4)], cx, core), axis)


def body(
    hidden,
    cotangent,
    lengths,
    dealing,
    keep_flags,
    norm1_gain,
    w_query,
    w_key,
    w_value,
    w_out,
    rel_table,
    del_weight,
    norm2_gain,
    w_gate,
    w_up,
    w_down,
):
    count = lax.axis_size("dp")
    rank = lax.axis_index("dp")
    cx = lax.axis_index("cx")
    core = lax.axis_index("core")
    ctx = cx * 2 + core
    local = hidden.shape[1]
    width = hidden.shape[2]
    rows = local * 4
    heads = rel_table.shape[1]
    cols = w_query.shape[1]
    hw = cols // heads
    shard = w_query.shape[0]
    units = w_gate.shape[1] // 4
    info = jnp.stack([rank, ctx]).astype(jnp.int32)

    half = cols // 2
    vectors = jnp.pad(jnp.stack([norm1_gain, del_weight, norm2_gain]), ((0, VEC - 3), (0, 0)))
    rows_qkv = jnp.concatenate([w_query.T, w_key.T, w_value.T], axis=0)
    piece = jnp.concatenate(
        [
            lax.dynamic_slice(rows_qkv, (core * 3 * half, 0), (3 * half, shard)),
            lax.dynamic_slice(w_out, (core * half, 0), (half, shard)),
            vectors,
        ],
        axis=0,
    )
    pieces = gather_dp(piece, count, rank, 1)
    att = jnp.stack(pieces)
    w0, w1 = in_order(att, swap(att, "core"), core)
    wo_other = swap(att[:, 3 * half : 4 * half], "tp")

    def unit_cols(w):
        return lax.dynamic_slice(w, (0, ctx * units), (shard, units))

    wide = -(-3 * units // 128) * 128
    w_piece = jnp.concatenate(
        [unit_cols(w_gate), unit_cols(w_up), unit_cols(w_down.T), jnp.zeros((shard, wide - 3 * units), BF)], axis=1
    )
    w_piece, *_ = lax.optimization_barrier((w_piece, *pieces[1:2]))
    w_ffn = [lax.all_gather(w_piece, "dp", axis=0, tiled=True)]

    deal = xor_order(pick(dealing, ctx).reshape(4, local), 0, cx, core).reshape(1, 1, rows)
    keep = xor_order(pick(keep_flags, ctx).reshape(4, local), 0, cx, core).reshape(rows)
    lens = pick(lengths, ctx)
    hit = deal[0] == jnp.arange(rows, dtype=jnp.int32)[:, None]
    kf = jnp.sum(jnp.where(hit, keep[None, :], 0), axis=1)[None, :]
    onehot = span_onehot()
    vb = lax.dot_general(rel_table, jnp.asarray(onehot, BF), (((0,), (1,)), ((), ())), preferred_element_type=F32)
    vb = jnp.pad(vb, ((0, 8 - heads), (0, 0)))

    hid = jnp.transpose(hidden, (0, 2, 1))
    over = swap(jnp.stack([pick(hid, ctx ^ 2), pick(hid, ctx ^ 3)]), "cx")
    across = swap(jnp.stack([pick(hid, ctx ^ 1), over[1]]), "core")
    x = place_tokens(info, deal, [pick(hid, ctx)[None], across[:1], over[:1], across[1:]])[0]

    cot_own = jnp.transpose(cotangent, (0, 2, 1))
    cot_x = swap(cot_own, "cx")
    n1, qkv, attn, aux = call(
        lambda *refs: enter_kernel(heads, hw, *refs),
        [shape(width, rows), shape(3 * cols, rows), shape(cols, rows), shape(8, rows, dtype=F32)],
        [info, lens, x, w0, w1, kf, vb],
        2 * rows * width * cols * 3 + 4 * rows * rows * cols,
        name="enter",
    )
    attn_other = swap(attn, "tp")
    wo_later, _ = lax.optimization_barrier((wo_other, attn))
    wo0_other, wo1_other = in_order(wo_other, swap(wo_later, "core"), core)
    h1, n2 = call(
        lambda *refs: middle_kernel(cols, *refs),
        [shape(width, rows, dtype=F32), shape(width + VEC, rows)],
        [info, lens, x, attn, attn_other, w0, w1, wo0_other, wo1_other, aux],
        2 * rows * width * cols * 2,
        name="middle",
    )

    n2, cot_x = lax.optimization_barrier((n2, cot_x))
    deals = xor_order(dealing.reshape(4, 4, local), 1, cx, core).reshape(4, 1, rows)
    cot = place_tokens(info, deals, [cot_own, swap(cot_own, "core"), cot_x, swap(cot_x, "core")])

    att_later, _ = lax.optimization_barrier((att[:, : 3 * half], attn_other))
    att_other = swap(att_later, "tp")
    n2_core = swap(n2, "core")
    n2_x = swap(n2, "cx")
    n2_x, cot, att_other = lax.optimization_barrier((n2_x, cot, att_other))
    n2_all = [n2, n2_core, n2_x, swap(n2_x, "core")]
    gates = [lax.dynamic_slice(n, (width, ctx * local), (1, local)) for n in n2_all]
    gates = jnp.concatenate(xor_list(gates, cx, core), axis=0)
    w0_other, w1_other = in_order(att_other, swap(att_other, "core"), core)
    n2_all[3], w0_other, w1_other = lax.optimization_barrier((n2_all[3], w0_other, w1_other))
    keep_b, send_b, keep_a, send_a, parts = ffn(info, n2_all, cot, w_ffn, shard, units)
    got_a = swap(send_a, "core")
    got_b = swap(send_b, "core")

    def both(kept, got, i, low=0, high=width):
        return kept[i][low:high].astype(F32) + got[i][low:high].astype(F32)

    cut = width // 48 * 16
    first = jnp.stack([both(keep_a, got_a, 0, 0, cut).astype(BF), both(keep_b, got_b, 0, 0, cut).astype(BF)])
    first = first.astype(F32) + swap(first, "tp").astype(F32)
    late_x = swap(both(keep_a, got_a, 0, cut).astype(BF), "cx")
    late_own = (both(keep_b, got_b, 0, cut) + late_x.astype(F32)).astype(BF)
    dn_pairs = [first[1].astype(BF), swap(first[0].astype(BF), "cx"), late_own, swap(late_own, "tp")]
    bf_over, _ = lax.optimization_barrier((both(keep_a, got_a, 1).astype(BF), dn_pairs[1]))
    bf_x, _ = lax.optimization_barrier((swap(bf_over, "cx"), dn_pairs[3]))
    bf_own = (both(keep_b, got_b, 1) + bf_x.astype(F32)).astype(BF)
    g_ffn = scatter_dp([parts], 0).astype(BF)
    blocks_of = att.shape[0]
    dh1, slab, diag, g_wo, g_gain2 = call(
        lambda *refs: back_kernel(heads, hw, *refs),
        [
            shape(width, rows, dtype=F32),
            shape(3 * cols + VEC, rows),
            shape(8, SPAN, dtype=F32),
            shape(blocks_of, cols, width // blocks_of),
            shape(blocks_of, 8, width // blocks_of, dtype=F32),
        ],
        [info, lens, *dn_pairs, h1, cot[:1], w0, w1, qkv, attn, aux, kf, vb],
        2 * rows * width * cols * 2 + 10 * rows * rows * cols,
        scratch=[
            pltpu.VMEM((width, rows), F32),
            pltpu.VMEM((cols, rows), BF),
            pltpu.VMEM((rows, rows), BF),
            pltpu.VMEM((rows, rows), BF),
            pltpu.VMEM((QB, SPAN), F32),
        ],
        name="back",
    )
    slab_other = swap(slab, "tp")
    g_ffn, _ = lax.optimization_barrier((g_ffn, slab))
    grads, sent = call(
        lambda *refs: gatt_kernel(cols, *refs),
        [shape(blocks_of, 2, cols, width // blocks_of)] * 2,
        [info, lens, slab, n1, g_wo],
        2 * rows * width * cols * 3,
        limit=48,
        name="gatt",
    )
    sent = swap(sent, "core")
    slab_other, bf_own, g_ffn, sent = lax.optimization_barrier((slab_other, bf_own, g_ffn, sent))
    grads = (grads.astype(F32) + sent.astype(F32)).astype(BF)
    if blocks_of == 1:
        grads = jnp.transpose(grads[0].reshape(2, cols, count, shard), (2, 0, 1, 3))
    grads = grads.reshape(count * 2 * cols, shard)
    grads = lax.psum_scatter(grads, "dp", scatter_dimension=0, tiled=True)
    bf_other = swap(bf_own, "tp")
    g_x = swap(g_ffn, "cx")
    *dx, vec = call(
        lambda *refs: leave_kernel(cols, *refs),
        [shape(width, local)] * 4 + [shape(blocks_of, 16, width // blocks_of, dtype=F32)],
        [info, lens, slab, slab_other, w0, w1, w0_other, w1_other, x, dh1, n1, aux],
        2 * rows * width * cols * 6,
        scratch=[pltpu.VMEM((width, rows), F32), pltpu.VMEM((width, rows), F32)],
        limit=48,
        name="leave",
    )

    table = lax.dot_general(
        diag[:heads], jnp.asarray(onehot), (((1,), (0,)), ((), ())), precision=lax.Precision.HIGHEST
    )
    bw = width // blocks_of
    size = table.size // 8
    flat = jnp.broadcast_to(jnp.pad(table.reshape(1, 8, size), ((0, 0), (0, 0), (0, bw - size))), (blocks_of, 8, bw))
    sums = jnp.concatenate([vec, g_gain2, flat], axis=1)

    def deal_out(items):
        return [items[0]] + [cross(items[k], k) for k in range(1, 4)]

    def arrange(got):
        return jnp.transpose(jnp.stack(xor_list(got, cx, core)), (0, 2, 1))

    def block_of(k):
        total = sum(
            lax.dynamic_slice(a, (0, (ctx ^ k) * local), (width, local)).astype(F32) for a in (h1, bf_own, bf_other)
        )
        return total.astype(BF)

    *dx, g_x, core_sums = lax.optimization_barrier((*dx, g_x, swap(sums, "core")))
    dx = deal_out(dx)
    sums = sums + core_sums
    bf_other, dx[1], x_sums, grads = lax.optimization_barrier((bf_other, dx[1], swap(sums, "cx"), grads))
    sums = sums + x_sums
    far = lax.ppermute(sums[2:], "dp", FAR) if count == 4 else sums
    grads_x = swap(grads, "cx")
    g_ffn, g_x, *blocks = lax.optimization_barrier((g_ffn, g_x, *[block_of(k) for k in range(4)]))
    out = deal_out(blocks)
    g_gate, g_up, g_down = spread_units(info, [g_ffn, swap(g_ffn, "core"), g_x, swap(g_x, "core")], units)
    out[1], grads_x, far = lax.optimization_barrier((out[1], grads_x, far))
    grads = (grads.astype(F32) + grads_x.astype(F32)).astype(BF)
    if count == 4:
        sums = sums[:2] + far
        near = lax.ppermute(sums[1], "dp", NEAR)
    else:
        near = lax.psum(far, "dp")
    out[2], grads_core, near, g_gate = lax.optimization_barrier((out[2], swap(grads, "core"), near, g_gate))
    g_weights = jnp.concatenate(in_order(grads, grads_core, core), axis=0).astype(F32)
    g_weights = g_weights.reshape(4, cols, shard)
    if count == 4:
        sums = sums[0] + near
        vec = sums[:24:8]
    else:
        sums = near[0]
        vec = lax.dynamic_slice(sums[:24:8], (0, rank * shard), (3, shard))
    table = sums[24:, :size].reshape(table.shape).T

    return (
        arrange(out),
        gates,
        arrange(dx),
        vec[0],
        g_weights[0].T,
        g_weights[1].T,
        g_weights[2].T,
        g_weights[3],
        table,
        vec[1],
        vec[2],
        g_gate,
        g_up,
        g_down.T,
    )


def solution(mesh):
    dp, ctx, tp = (mesh.shape[name] for name in ("dp", "ctx", "tp"))
    split = Mesh(mesh.devices.reshape(dp, 2, ctx // 2, tp), ("dp", "cx", "core", "tp"))
    tokens = P(None, ("dp", "cx", "core"), None)
    in_specs = (
        tokens,
        tokens,
        P(None, "dp", None),
        P(None, "dp", None),
        P(None, "dp", None),
        P("dp"),
        P("dp", "tp"),
        P("dp", "tp"),
        P("dp", "tp"),
        P("tp", "dp"),
        P(None, "tp"),
        P("dp"),
        P("dp"),
        P("dp", "tp"),
        P("dp", "tp"),
        P("tp", "dp"),
    )
    out_specs = (
        tokens,
        P(None, ("dp", "cx", "core")),
        tokens,
        P("dp"),
        P("dp", "tp"),
        P("dp", "tp"),
        P("dp", "tp"),
        P("tp", "dp"),
        P(None, "tp"),
        P("dp"),
        P("dp"),
        P("dp", "tp"),
        P("dp", "tp"),
        P("tp", "dp"),
    )
    return jax.shard_map(body, mesh=split, in_specs=in_specs, out_specs=out_specs, check_vma=False)
```

```python
import math

import numpy as np

import jax
import jax.numpy as jnp
from jax import lax
from jax.experimental import pallas as pl
from jax.experimental.pallas import tpu as pltpu
from jax.sharding import Mesh, PartitionSpec as P

BUCKETS = 32
MAX_DIST = 128
EPS = 1e-06
FILL = -1e30
BF = jnp.bfloat16
F32 = jnp.float32
SWAP = [(0, 1), (1, 0)]
SPAN = 1024
QB = 128


def bucket_np(relative):
    half_count = BUCKETS // 2
    exact_count = half_count // 2
    distance = np.abs(relative)
    ratio_bits = math.log2(MAX_DIST / exact_count)
    far = np.full(distance.shape, exact_count, np.int32)
    for level in range(1, half_count - exact_count):
        border = math.ceil(exact_count * 2.0 ** (level * ratio_bits / (half_count - exact_count)))
        far = far + (distance >= border).astype(np.int32)
    chosen = np.where(distance < exact_count, distance, far)
    return chosen + half_count * (relative > 0).astype(np.int32)


def span_onehot():
    k = np.arange(SPAN)
    d = np.where(k < SPAN // 2, k, k - SPAN)
    return (bucket_np(d)[:, None] == np.arange(BUCKETS)[None, :]).astype(np.float32)


def dot_n(a, b):
    return lax.dot_general(a, b, (((1,), (0,)), ((), ())), preferred_element_type=F32)


def dot_t(a, b):
    return lax.dot_general(a, b, (((1,), (1,)), ((), ())), preferred_element_type=F32)


def dot_0(a, b):
    return lax.dot_general(a, b, (((0,), (0,)), ((), ())), preferred_element_type=F32)


SMEM_SPEC = pl.BlockSpec(memory_space=pltpu.SMEM)
VMEM_SPEC = pl.BlockSpec(memory_space=pltpu.VMEM)
ANY_SPEC = pl.BlockSpec(memory_space=pl.ANY)
VEC = 16
COST = dict(enter=0, middle=0, back=12, leave=25, gatt=4, ffn=44, units=4, place=0, places=0)


def cost(name):
    return pl.CostEstimate(flops=COST[name] * 10**9 + 1000, bytes_accessed=1000, transcendentals=0)


def shape(*dims, dtype=BF):
    return jax.ShapeDtypeStruct(dims, dtype)


def call(kernel, outs, args, flops, scratch=(), limit=30, name=None):
    return pl.pallas_call(
        kernel,
        out_shape=tuple(outs),
        in_specs=[SMEM_SPEC] * 2 + [VMEM_SPEC] * (len(args) - 2),
        out_specs=tuple([VMEM_SPEC] * len(outs)),
        scratch_shapes=list(scratch),
        compiler_params=pltpu.CompilerParams(vmem_limit_bytes=limit * 2**20),
        cost_estimate=cost(name),
        name=name,
    )(*args)


def allowed_block(lens_ref, kf_ref, b, rows):
    e1 = lens_ref[0, 0]
    e2 = e1 + lens_ref[0, 1]
    tj = lax.broadcasted_iota(jnp.int32, (1, rows), 1)
    ti = lax.broadcasted_iota(jnp.int32, (QB, 1), 0) + b * QB
    sj = (tj >= e1).astype(jnp.int32) + (tj >= e2).astype(jnp.int32)
    si = (ti >= e1).astype(jnp.int32) + (ti >= e2).astype(jnp.int32)
    keep = kf_ref[...] == 1
    return (si == sj) & (keep | (ti == tj))


def window(full, b, rows):
    if b == 0:
        return full[:, :rows]
    return jnp.concatenate([full[:, SPAN - QB * b :], full[:, : rows - QB * b]], axis=1)


def toeplitz(vb_ref, h):
    row = jnp.broadcast_to(vb_ref[h : h + 1, :], (QB, SPAN))
    return pltpu.roll(row, 0, 1, stride=1, stride_axis=0)


def probs(q, k, bias, gate, allowed):
    s = dot_0(q, k) + bias + gate
    s = jnp.where(allowed, s, FILL)
    e = jnp.exp(s - jnp.max(s, axis=1, keepdims=True))
    return e / jnp.sum(e, axis=1, keepdims=True)


def attend(heads, hw, lens_ref, qkv_ref, gate, kf_ref, vb_ref, o_ref):
    rows = qkv_ref.shape[1]
    c = heads * hw
    masks = [allowed_block(lens_ref, kf_ref, b, rows) for b in range(rows // QB)]
    for h in range(heads):
        full = toeplitz(vb_ref, h)
        k = qkv_ref[c + h * hw : c + (h + 1) * hw, :]
        v = qkv_ref[2 * c + h * hw : 2 * c + (h + 1) * hw, :]
        for b in range(rows // QB):
            q = qkv_ref[h * hw : (h + 1) * hw, b * QB : (b + 1) * QB]
            p = probs(q, k, window(full, b, rows), gate, masks[b])
            o_ref[h * hw : (h + 1) * hw, b * QB : (b + 1) * QB] = dot_t(v, p.astype(BF)).astype(BF)


def attend_back(heads, hw, lens_ref, qkv_ref, do_ref, gate, kf_ref, vb_ref, g_ref, t_ref, ds_ref, pl_ref, acc_ref):
    rows = qkv_ref.shape[1]
    c = heads * hw
    masks = [allowed_block(lens_ref, kf_ref, b, rows) for b in range(rows // QB)]
    ones = jnp.ones((VEC, rows), BF)
    dgate = jnp.zeros((VEC, rows), F32)
    t_ref[...] = jnp.zeros_like(t_ref)
    for h in range(heads):
        full = toeplitz(vb_ref, h)
        sl = slice(h * hw, (h + 1) * hw)
        k = qkv_ref[c + h * hw : c + (h + 1) * hw, :]
        v = qkv_ref[2 * c + h * hw : 2 * c + (h + 1) * hw, :]
        acc_ref[...] = jnp.zeros_like(acc_ref)
        for b in range(rows // QB):
            rs = slice(b * QB, (b + 1) * QB)
            p = probs(qkv_ref[sl, rs], k, window(full, b, rows), gate, masks[b])
            dp = dot_0(do_ref[sl, rs], v)
            ds = (p * (dp - jnp.sum(p * dp, axis=1, keepdims=True))).astype(BF)
            ds_ref[rs, :] = ds
            pl_ref[rs, :] = p.astype(BF)
            wide = ds.astype(F32)
            if b == 0:
                acc_ref[:, :rows] += wide
            else:
                acc_ref[:, SPAN - QB * b :] += wide[:, : QB * b]
                acc_ref[:, : rows - QB * b] += wide[:, QB * b :]
        ds_all = ds_ref[...]
        g_ref[sl, :] = dot_t(k, ds_all).astype(BF)
        g_ref[c + h * hw : c + (h + 1) * hw, :] = dot_n(qkv_ref[sl, :], ds_all).astype(BF)
        g_ref[2 * c + h * hw : 2 * c + (h + 1) * hw, :] = dot_n(do_ref[sl, :], pl_ref[...]).astype(BF)
        dgate = dgate + dot_n(ones, ds_all)
        a = acc_ref[...]
        half = QB // 2
        while half >= 8:
            low = a[half:, :]
            a = a[:half, :] + pltpu.roll(low, SPAN - half, 1)
            half //= 2
        tot = a[0:1, :]
        for i in range(1, 8):
            tot = tot + pltpu.roll(a[i : i + 1, :], SPAN - i, 1)
        t_ref[h : h + 1, :] = tot
    g_ref[3 * c :, :] = dgate.astype(BF)


def spots(info_ref, array_ref):
    many, block = array_ref.shape[0], array_ref.shape[2]
    if many == 1:
        return [pl.ds(0, block)]
    return [pl.ds(pl.multiple_of((info_ref[0] ^ k) * block, VEC), block) for k in range(many)]


def spread(w0_ref, k, c, which, rows):
    pickup = (lax.broadcasted_iota(jnp.int32, (VEC, QB), 0) == which).astype(F32).astype(BF)
    block = dot_0(w0_ref[k, 2 * c :, :], pickup)
    return jnp.concatenate([block] * (rows // QB), axis=1)


def inverse_rms(values):
    return lax.rsqrt(jnp.sum(values * values, axis=0, keepdims=True) / values.shape[0] + EPS)


def sum_tokens(values):
    values = sum(values[:, i : i + QB] for i in range(0, values.shape[1], QB))
    high = values.astype(BF)
    rest = (values - high.astype(F32)).astype(BF)
    ones = jnp.ones((8, QB), BF)
    return dot_t(ones, high) + dot_t(ones, rest)


def enter_kernel(heads, hw, info_ref, lens_ref, x_ref, w0_ref, w1_ref, kf_ref, vb_ref, n1_ref, qkv_ref, attn_ref, aux_ref):
    rows = x_ref.shape[1]
    c = heads * hw
    x = x_ref[...].astype(F32)
    r1 = inverse_rms(x)
    half = c // 2
    low = jnp.zeros((2 * c + VEC, rows), F32)
    high = jnp.zeros((c + half, rows), F32)
    for k, spot in enumerate(spots(info_ref, w0_ref)):
        n1 = (x_ref[spot, :].astype(F32) * r1 * spread(w0_ref, k, c, 0, rows)).astype(BF)
        n1_ref[spot, :] = n1
        low = low + dot_n(w0_ref[k], n1)
        high = high + dot_n(w1_ref[k, : c + half, :], n1)
    qkv_ref[: c + half, :] = low[: c + half].astype(BF)
    qkv_ref[c + half :, :] = high.astype(BF)
    z = low[2 * c + 1 : 2 * c + 2]
    gate = (-4.0 * jax.nn.sigmoid(z)).astype(BF).astype(F32)
    aux_ref[...] = jnp.concatenate([z, gate, r1, jnp.zeros((5, rows), F32)], axis=0)
    attend(heads, hw, lens_ref, qkv_ref, gate, kf_ref, vb_ref, attn_ref)


def middle_kernel(
    c, info_ref, lens_ref, x_ref, attn_ref, other_ref, w0_ref, w1_ref, wo0_ref, wo1_ref, aux_ref, h1_ref, n2_ref
):
    rows = x_ref.shape[1]
    half = c // 2
    out = slice(c + half, 2 * c)
    width = x_ref.shape[0]
    total = jnp.zeros((1, rows), F32)
    places = spots(info_ref, w0_ref)
    for k, spot in enumerate(places):
        own = dot_0(w0_ref[k, out, :], attn_ref[:half, :]) + dot_0(w1_ref[k, out, :], attn_ref[half:, :])
        far = dot_0(wo0_ref[k], other_ref[:half, :]) + dot_0(wo1_ref[k], other_ref[half:, :])
        h1 = x_ref[spot, :].astype(F32) + (own.astype(BF).astype(F32) + far.astype(BF).astype(F32))
        h1_ref[spot, :] = h1
        total = total + jnp.sum(h1 * h1, axis=0, keepdims=True)
    r2 = lax.rsqrt(total / width + EPS)
    for k, spot in enumerate(places):
        n2_ref[spot, :] = (h1_ref[spot, :] * r2 * spread(w0_ref, k, c, 2, rows)).astype(BF)
    n2_ref[width:, :] = jnp.broadcast_to(aux_ref[1:2, :], (VEC, rows)).astype(BF)


def back_kernel(
    heads,
    hw,
    info_ref,
    lens_ref,
    low0_ref,
    low1_ref,
    high0_ref,
    high1_ref,
    h1_ref,
    cot_ref,
    w0_ref,
    w1_ref,
    qkv_ref,
    attn_ref,
    aux_ref,
    kf_ref,
    vb_ref,
    dh1_ref,
    slab_ref,
    diag_ref,
    gwo_ref,
    gain_ref,
    u_ref,
    do_ref,
    ds_ref,
    pl_ref,
    acc_ref,
):
    rows = h1_ref.shape[1]
    width = h1_ref.shape[0]
    c = heads * hw
    places = spots(info_ref, w0_ref)
    r2 = inverse_rms(h1_ref[...])
    total = jnp.zeros((1, rows), F32)
    cut = low0_ref.shape[0]
    u_ref[:cut, :] = low0_ref[...].astype(F32) + low1_ref[...].astype(F32)
    u_ref[cut:, :] = high0_ref[...].astype(F32) + high1_ref[...].astype(F32)
    for k, spot in enumerate(places):
        dn2 = u_ref[spot, :]
        u = dn2 * spread(w0_ref, k, c, 2, rows)
        h1 = h1_ref[spot, :]
        total = total + jnp.sum(h1 * u, axis=0, keepdims=True)
        u_ref[spot, :] = u
        gain_ref[k] = sum_tokens(dn2 * h1 * r2)
    back = r2 * r2 * r2 * (total / width)
    half = c // 2
    out = slice(c + half, 2 * c)
    dattn = [jnp.zeros((half, rows), F32)] * 2
    for k, spot in enumerate(places):
        dh1 = cot_ref[0, spot, :].astype(F32) + r2 * u_ref[spot, :] - h1_ref[spot, :] * back
        dh1_ref[spot, :] = dh1
        dhl = dh1.astype(BF)
        dattn = [d + dot_n(w_ref[k, out, :], dhl) for d, w_ref in zip(dattn, (w0_ref, w1_ref))]
        gwo_ref[k] = dot_t(attn_ref[...], dhl).astype(BF)
    do_ref[:half, :] = dattn[0].astype(BF)
    do_ref[half:, :] = dattn[1].astype(BF)
    attend_back(
        heads, hw, lens_ref, qkv_ref, do_ref, aux_ref[1:2, :], kf_ref, vb_ref, slab_ref, diag_ref, ds_ref, pl_ref, acc_ref
    )


def gatt_kernel(c, info_ref, lens_ref, slab_ref, n1_ref, gwo_ref, keep_ref, send_ref):
    many = gwo_ref.shape[0]
    for k, spot in enumerate(spots(info_ref, gwo_ref)):
        at = info_ref[0] ^ k if many > 1 else 0
        n1 = n1_ref[spot, :]
        all_three = dot_t(slab_ref[: 3 * c, :], n1).astype(BF)
        parts = [all_three[i * c : (i + 1) * c] for i in range(3)] + [gwo_ref[k]]
        for core, refs in enumerate(((keep_ref, send_ref), (send_ref, keep_ref))):

            @pl.when((info_ref[1] & 1) == core)
            def _():
                for i, part in enumerate(parts):
                    refs[i // 2][at, i % 2] = part


def leave_kernel(
    c,
    info_ref,
    lens_ref,
    slab_ref,
    other_ref,
    w0_ref,
    w1_ref,
    far0_ref,
    far1_ref,
    x_ref,
    dh1_ref,
    n1_ref,
    aux_ref,
    o0,
    o1,
    o2,
    o3,
    vec_ref,
    dn_ref,
    dx_ref,
):
    rows = x_ref.shape[1]
    width = x_ref.shape[0]
    half = 3 * c // 2
    places = spots(info_ref, w0_ref)
    z = aux_ref[0:1, :]
    r1 = aux_ref[2:3, :]
    sig = jax.nn.sigmoid(z)
    dgate = (slab_ref[3 * c :, :].astype(F32) + other_ref[3 * c :, :].astype(F32))[0:1]
    dz = dgate * (-4.0 * sig * (1.0 - sig))
    total = jnp.zeros((1, rows), F32)
    for k, spot in enumerate(places):
        own = dot_0(w0_ref[k, :half, :], slab_ref[:half, :]) + dot_0(w1_ref[k, :half, :], slab_ref[half : 2 * half, :])
        far = dot_0(far0_ref[k], other_ref[:half, :]) + dot_0(far1_ref[k], other_ref[half : 2 * half, :])
        dn = own.astype(BF).astype(F32) + far.astype(BF).astype(F32) + spread(w0_ref, k, c, 1, rows) * dz
        u = dn * spread(w0_ref, k, c, 0, rows)
        x = x_ref[spot, :].astype(F32)
        total = total + jnp.sum(x * u, axis=0, keepdims=True)
        dx_ref[spot, :] = u
        vec_ref[k, 0:8, :] = sum_tokens(dn * x * r1)
        vec_ref[k, 8:16, :] = sum_tokens(n1_ref[spot, :].astype(F32) * dz)
    back = r1 * r1 * r1 * (total / width)
    dn_ref[...] = dh1_ref[...] + r1 * dx_ref[...] - x_ref[...].astype(F32) * back
    part = rows // 4
    for k, out in enumerate((o0, o1, o2, o3)):
        at = pl.multiple_of((info_ref[1] ^ k) * part, part)
        out[...] = dn_ref[:, pl.ds(at, part)].astype(BF)


def ffn_kernel(n_pieces, shard, units, info_ref, n0, n1, n2, n3, cot_ref, *refs):
    pieces = refs[:n_pieces]
    o0, o1, o2, o3, grad_ref, w_ref, n_ref, gu_ref, acc_ref, inner_ref, dgu_ref, sems = refs[n_pieces:]
    step = pl.program_id(0)
    per = pl.num_programs(0) // 4
    width = w_ref.shape[0]

    @pl.when(step == 0)
    def _():
        copies = []
        for k in range(n_pieces):
            at = pl.multiple_of((info_ref[0] ^ k) * shard, VEC) if n_pieces > 1 else 0
            copies.append(pltpu.make_async_copy(pieces[k], w_ref.at[pl.ds(at, pieces[k].shape[0])], sems.at[k]))
        for c in copies:
            c.start()
        acc_ref[...] = jnp.zeros_like(acc_ref)
        for c in copies:
            c.wait()

    for k, source in enumerate((n0, n1, n2, n3)):

        @pl.when(step // per == k)
        def _():
            n_ref[...] = source[:width, :]

    gu_ref[: 2 * units, :] = dot_0(w_ref[:, : 2 * units], n_ref[...])
    gu_ref[2 * units :, :] = dot_0(w_ref[:, 2 * units : 3 * units], cot_ref[0])
    c0 = math.sqrt(2.0 / math.pi)
    chunk = units // 14
    for r in range(0, units, chunk):
        ga = gu_ref[r : r + chunk, :]
        up = gu_ref[units + r : units + r + chunk, :]
        din = gu_ref[2 * units + r : 2 * units + r + chunk, :]
        sq = ga * ga
        th = jnp.tanh(c0 * (ga + 0.044715 * ga * sq))
        hf = 0.5 * (1.0 + th)
        act = ga * hf
        slope = hf + 0.5 * ga * (1.0 - th * th) * (c0 + 3.0 * 0.044715 * c0 * sq)
        inner_ref[r : r + chunk, :] = (act * up).astype(BF)
        dgu_ref[r : r + chunk, :] = (din * up * slope).astype(BF)
        dgu_ref[units + r : units + r + chunk, :] = (din * act).astype(BF)
    for k, out in enumerate((o0, o1, o2, o3)):

        @pl.when(step // per == k)
        def _():
            out[0] = dot_n(w_ref[:, : 2 * units], dgu_ref[...]).astype(BF)
            out[1] = dot_n(w_ref[:, 2 * units : 3 * units], inner_ref[...]).astype(BF)

    acc_ref[:, : 2 * units] += dot_t(n_ref[...], dgu_ref[...])
    acc_ref[:, 2 * units : 3 * units] += dot_t(cot_ref[0], inner_ref[...])

    @pl.when(step == 4 * per - 1)
    def _():
        grad_ref[...] = acc_ref[...].astype(BF)


def ffn(info, ns, cot, pieces, shard, units, tile=256):
    width, rows = cot.shape[1:]
    tall = ns[0].shape[0]
    per = rows // tile
    wide = pieces[0].shape[1]
    part = lambda k: lambda i, s: (0, jnp.clip(i - k * per, 0, per - 1))
    part3 = lambda k: lambda i, s: (0, 0, jnp.clip(i - k * per, 0, per - 1))
    return pl.pallas_call(
        lambda *refs: ffn_kernel(len(pieces), shard, units, *refs),
        grid_spec=pltpu.PrefetchScalarGridSpec(
            num_scalar_prefetch=1,
            grid=(4 * per,),
            in_specs=[pl.BlockSpec((tall, tile), part(k)) for k in range(4)]
            + [pl.BlockSpec((1, width, tile), lambda i, s: (i // per, 0, i % per))]
            + [ANY_SPEC] * len(pieces),
            out_specs=[pl.BlockSpec((2, width, tile), part3(k)) for k in range(4)]
            + [pl.BlockSpec((width, wide), lambda i, s: (0, 0))],
            scratch_shapes=[
                pltpu.VMEM((width, wide), BF),
                pltpu.VMEM((width, tile), BF),
                pltpu.VMEM((3 * units, tile), F32),
                pltpu.VMEM((width, wide), F32),
                pltpu.VMEM((units, tile), BF),
                pltpu.VMEM((2 * units, tile), BF),
                pltpu.SemaphoreType.DMA((len(pieces),)),
            ],
        ),
        out_shape=[shape(2, width, rows)] * 4 + [shape(width, wide)],
        compiler_params=pltpu.CompilerParams(vmem_limit_bytes=56 * 2**20),
        cost_estimate=cost("ffn"),
        name="ffn",
    )(info, *ns, cot, *pieces)


def spread_units_kernel(units, info_ref, a, b, c, d, gate_ref, up_ref, down_ref, part_ref):
    for k, source in enumerate((a, b, c, d)):
        part_ref[k] = source[...]
    for i in range(4):
        at = slice(i * units, (i + 1) * units)
        for n, ref in enumerate((gate_ref, up_ref, down_ref)):
            ref[:, at] = part_ref[info_ref[1] ^ i, :, n * units : (n + 1) * units].astype(F32)


def spread_units(info, parts, units):
    rows, wide = parts[0].shape
    tile = rows
    out = pl.BlockSpec((tile, 4 * units), lambda i, s: (i, 0))
    return pl.pallas_call(
        lambda *refs: spread_units_kernel(units, *refs),
        grid_spec=pltpu.PrefetchScalarGridSpec(
            num_scalar_prefetch=1,
            grid=(rows // tile,),
            in_specs=[pl.BlockSpec((tile, wide), lambda i, s: (i, 0))] * 4,
            out_specs=[out] * 3,
            scratch_shapes=[pltpu.VMEM((4, tile, wide), BF)],
        ),
        out_shape=[shape(rows, 4 * units, dtype=F32)] * 3,
        compiler_params=pltpu.CompilerParams(vmem_limit_bytes=40 * 2**20),
        cost_estimate=cost("units"),
        name="units",
    )(info, *parts)


def place_kernel(info_ref, deal_ref, *refs):
    *blocks, out_ref = refs
    rows = out_ref.shape[2]
    hit = lax.broadcasted_iota(jnp.int32, (rows, rows), 0) == deal_ref[0]
    blocks = jnp.concatenate([b[0] for b in blocks], axis=1)
    out_ref[0] = dot_t(blocks, hit.astype(F32).astype(BF)).astype(BF)


def place_tokens(info, deal, blocks):
    many, _, rows = deal.shape
    width, local = blocks[0].shape[-2:]
    if many == 1:
        specs = [pl.BlockSpec((1, width, local), lambda j, s: (0, 0, 0))] * 4
        order = lambda j, s: (0, 0, 0)
    else:
        specs = [pl.BlockSpec((1, width, local), lambda j, s: (s[1] ^ j, 0, 0))] * 4
        order = lambda j, s: (s[1] ^ j, 0, 0)
    return pl.pallas_call(
        place_kernel,
        grid_spec=pltpu.PrefetchScalarGridSpec(
            num_scalar_prefetch=1,
            grid=(many,),
            in_specs=[pl.BlockSpec((1, 1, rows), order)] + specs,
            out_specs=pl.BlockSpec((1, width, rows), lambda j, s: (j, 0, 0)),
        ),
        out_shape=shape(many, width, rows),
        compiler_params=pltpu.CompilerParams(vmem_limit_bytes=48 * 2**20),
        cost_estimate=cost("place" if many == 1 else "places"),
        name="place",
    )(info, deal, *blocks)


def pick(array, index, axis=0):
    return lax.dynamic_index_in_dim(array, index, axis, keepdims=False)


def swap(block, axis):
    return lax.ppermute(block, axis, SWAP)


def cross(block, step):
    if step == 3:
        return lax.ppermute(block, ("cx", "core"), [(0, 3), (1, 2), (2, 1), (3, 0)])
    return swap(block, "core" if step == 1 else "cx")


NEAR = [(0, 1), (1, 0), (2, 3), (3, 2)]
FAR = [(0, 2), (2, 0), (1, 3), (3, 1)]
MID = [(1, 2), (2, 1)]


def gather_dp(piece, count, rank, axis):
    if count != 4:
        return [lax.all_gather(piece, "dp", axis=axis, tiled=True)]
    near = lax.ppermute(piece, "dp", NEAR)
    far = lax.ppermute(piece, "dp", FAR)
    mid = lax.ppermute(piece, "dp", MID)
    passed = lax.ppermute(far, "dp", [(1, 0), (2, 3)])
    return [piece, near, far, jnp.where((rank == 1) | (rank == 2), mid, passed)]


def scatter_dp(parts, axis):
    if len(parts) == 1:
        return lax.psum_scatter(parts[0], "dp", scatter_dimension=axis, tiled=True).astype(F32)
    early = lax.ppermute(parts[3], "dp", [(0, 1), (3, 2)])
    near = lax.ppermute(parts[1], "dp", NEAR)
    mid = lax.ppermute(parts[3], "dp", MID)
    far = lax.ppermute((parts[2].astype(F32) + early.astype(F32)).astype(BF), "dp", FAR)
    return parts[0].astype(F32) + near.astype(F32) + mid.astype(F32) + far.astype(F32)


def in_order(first, second, index):
    return jnp.where(index == 0, first, second), jnp.where(index == 0, second, first)


def xor_list(items, cx, core):
    a, b, c, d = items
    a, b = in_order(a, b, core)
    c, d = in_order(c, d, core)
    (a, c), (b, d) = in_order(a, c, cx), in_order(b, d, cx)
    return [a, b, c, d]


def xor_order(array, axis, cx, core):
    return jnp.concatenate(xor_list([lax.slice_in_dim(array, i, i + 1, axis=axis) for i in range(4)], cx, core), axis)


def body(
    hidden,
    cotangent,
    lengths,
    dealing,
    keep_flags,
    norm1_gain,
    w_query,
    w_key,
    w_value,
    w_out,
    rel_table,
    del_weight,
    norm2_gain,
    w_gate,
    w_up,
    w_down,
):
    count = lax.axis_size("dp")
    rank = lax.axis_index("dp")
    cx = lax.axis_index("cx")
    core = lax.axis_index("core")
    ctx = cx * 2 + core
    local = hidden.shape[1]
    width = hidden.shape[2]
    rows = local * 4
    heads = rel_table.shape[1]
    cols = w_query.shape[1]
    hw = cols // heads
    shard = w_query.shape[0]
    units = w_gate.shape[1] // 4
    info = jnp.stack([rank, ctx]).astype(jnp.int32)

    half = cols // 2
    vectors = jnp.pad(jnp.stack([norm1_gain, del_weight, norm2_gain]), ((0, VEC - 3), (0, 0)))
    rows_qkv = jnp.concatenate([w_query.T, w_key.T, w_value.T], axis=0)
    piece = jnp.concatenate(
        [
            lax.dynamic_slice(rows_qkv, (core * 3 * half, 0), (3 * half, shard)),
            lax.dynamic_slice(w_out, (core * half, 0), (half, shard)),
            vectors,
        ],
        axis=0,
    )
    pieces = gather_dp(piece, count, rank, 1)
    att = jnp.stack(pieces)
    w0, w1 = in_order(att, swap(att, "core"), core)
    wo_other = swap(att[:, 3 * half : 4 * half], "tp")

    def unit_cols(w):
        return lax.dynamic_slice(w, (0, ctx * units), (shard, units))

    wide = -(-3 * units // 128) * 128
    w_piece = jnp.concatenate(
        [unit_cols(w_gate), unit_cols(w_up), unit_cols(w_down.T), jnp.zeros((shard, wide - 3 * units), BF)], axis=1
    )
    w_piece, *_ = lax.optimization_barrier((w_piece, *pieces[1:2]))
    w_ffn = [lax.all_gather(w_piece, "dp", axis=0, tiled=True)]

    deal = xor_order(pick(dealing, ctx).reshape(4, local), 0, cx, core).reshape(1, 1, rows)
    keep = xor_order(pick(keep_flags, ctx).reshape(4, local), 0, cx, core).reshape(rows)
    lens = pick(lengths, ctx)
    hit = deal[0] == jnp.arange(rows, dtype=jnp.int32)[:, None]
    kf = jnp.sum(jnp.where(hit, keep[None, :], 0), axis=1)[None, :]
    onehot = span_onehot()
    vb = lax.dot_general(rel_table, jnp.asarray(onehot, BF), (((0,), (1,)), ((), ())), preferred_element_type=F32)
    vb = jnp.pad(vb, ((0, 8 - heads), (0, 0)))

    hid = jnp.transpose(hidden, (0, 2, 1))
    over = swap(jnp.stack([pick(hid, ctx ^ 2), pick(hid, ctx ^ 3)]), "cx")
    across = swap(jnp.stack([pick(hid, ctx ^ 1), over[1]]), "core")
    x = place_tokens(info, deal, [pick(hid, ctx)[None], across[:1], over[:1], across[1:]])[0]

    cot_own = jnp.transpose(cotangent, (0, 2, 1))
    cot_x = swap(cot_own, "cx")
    n1, qkv, attn, aux = call(
        lambda *refs: enter_kernel(heads, hw, *refs),
        [shape(width, rows), shape(3 * cols, rows), shape(cols, rows), shape(8, rows, dtype=F32)],
        [info, lens, x, w0, w1, kf, vb],
        2 * rows * width * cols * 3 + 4 * rows * rows * cols,
        name="enter",
    )
    attn_other = swap(attn, "tp")
    wo_later, _ = lax.optimization_barrier((wo_other, attn))
    wo0_other, wo1_other = in_order(wo_other, swap(wo_later, "core"), core)
    h1, n2 = call(
        lambda *refs: middle_kernel(cols, *refs),
        [shape(width, rows, dtype=F32), shape(width + VEC, rows)],
        [info, lens, x, attn, attn_other, w0, w1, wo0_other, wo1_other, aux],
        2 * rows * width * cols * 2,
        name="middle",
    )

    n2, cot_x = lax.optimization_barrier((n2, cot_x))
    deals = xor_order(dealing.reshape(4, 4, local), 1, cx, core).reshape(4, 1, rows)
    cot = place_tokens(info, deals, [cot_own, swap(cot_own, "core"), cot_x, swap(cot_x, "core")])

    att_later, _ = lax.optimization_barrier((att[:, : 3 * half], attn_other))
    att_other = swap(att_later, "tp")
    n2_core = swap(n2, "core")
    n2_x = swap(n2, "cx")
    n2_x, cot, att_other = lax.optimization_barrier((n2_x, cot, att_other))
    n2_all = [n2, n2_core, n2_x, swap(n2_x, "core")]
    gates = [lax.dynamic_slice(n, (width, ctx * local), (1, local)) for n in n2_all]
    gates = jnp.concatenate(xor_list(gates, cx, core), axis=0)
    w0_other, w1_other = in_order(att_other, swap(att_other, "core"), core)
    n2_all[3], w0_other, w1_other = lax.optimization_barrier((n2_all[3], w0_other, w1_other))
    keep_b, send_b, keep_a, send_a, parts = ffn(info, n2_all, cot, w_ffn, shard, units)
    got_a = swap(send_a, "core")
    got_b = swap(send_b, "core")

    def both(kept, got, i, low=0, high=width):
        return kept[i][low:high].astype(F32) + got[i][low:high].astype(F32)

    cut = width // 48 * 16
    first = jnp.stack([both(keep_a, got_a, 0, 0, cut).astype(BF), both(keep_b, got_b, 0, 0, cut).astype(BF)])
    first = first.astype(F32) + swap(first, "tp").astype(F32)
    late_x = swap(both(keep_a, got_a, 0, cut).astype(BF), "cx")
    late_own = (both(keep_b, got_b, 0, cut) + late_x.astype(F32)).astype(BF)
    dn_pairs = [first[1].astype(BF), swap(first[0].astype(BF), "cx"), late_own, swap(late_own, "tp")]
    bf_over, _ = lax.optimization_barrier((both(keep_a, got_a, 1).astype(BF), dn_pairs[1]))
    bf_x, _ = lax.optimization_barrier((swap(bf_over, "cx"), dn_pairs[3]))
    g_ffn = scatter_dp([parts], 0).astype(BF)
    blocks_of = att.shape[0]
    dh1, slab, diag, g_wo, g_gain2 = call(
        lambda *refs: back_kernel(heads, hw, *refs),
        [
            shape(width, rows, dtype=F32),
            shape(3 * cols + VEC, rows),
            shape(8, SPAN, dtype=F32),
            shape(blocks_of, cols, width // blocks_of),
            shape(blocks_of, 8, width // blocks_of, dtype=F32),
        ],
        [info, lens, *dn_pairs, h1, cot[:1], w0, w1, qkv, attn, aux, kf, vb],
        2 * rows * width * cols * 2 + 10 * rows * rows * cols,
        scratch=[
            pltpu.VMEM((width, rows), F32),
            pltpu.VMEM((cols, rows), BF),
            pltpu.VMEM((rows, rows), BF),
            pltpu.VMEM((rows, rows), BF),
            pltpu.VMEM((QB, SPAN), F32),
        ],
        name="back",
    )
    slab_other = swap(slab, "tp")
    g_ffn, _ = lax.optimization_barrier((g_ffn, slab))
    grads, sent = call(
        lambda *refs: gatt_kernel(cols, *refs),
        [shape(blocks_of, 2, cols, width // blocks_of)] * 2,
        [info, lens, slab, n1, g_wo],
        2 * rows * width * cols * 3,
        limit=48,
        name="gatt",
    )
    sent = swap(sent, "core")
    slab_other, bf_x, g_ffn, sent = lax.optimization_barrier((slab_other, bf_x, g_ffn, sent))
    bf_own = (both(keep_b, got_b, 1) + bf_x.astype(F32)).astype(BF)
    slab_other, bf_own = lax.optimization_barrier((slab_other, bf_own))
    grads = (grads.astype(F32) + sent.astype(F32)).astype(BF)
    if blocks_of == 1:
        grads = jnp.transpose(grads[0].reshape(2, cols, count, shard), (2, 0, 1, 3))
    grads = grads.reshape(count * 2 * cols, shard)
    grads = lax.psum_scatter(grads, "dp", scatter_dimension=0, tiled=True)
    bf_other = swap(bf_own, "tp")
    g_x = swap(g_ffn, "cx")
    *dx, vec = call(
        lambda *refs: leave_kernel(cols, *refs),
        [shape(width, local)] * 4 + [shape(blocks_of, 16, width // blocks_of, dtype=F32)],
        [info, lens, slab, slab_other, w0, w1, w0_other, w1_other, x, dh1, n1, aux],
        2 * rows * width * cols * 6,
        scratch=[pltpu.VMEM((width, rows), F32), pltpu.VMEM((width, rows), F32)],
        limit=48,
        name="leave",
    )

    table = lax.dot_general(
        diag[:heads], jnp.asarray(onehot), (((1,), (0,)), ((), ())), precision=lax.Precision.HIGHEST
    )
    bw = width // blocks_of
    size = table.size // 8
    flat = jnp.broadcast_to(jnp.pad(table.reshape(1, 8, size), ((0, 0), (0, 0), (0, bw - size))), (blocks_of, 8, bw))
    sums = jnp.concatenate([vec, g_gain2, flat], axis=1)

    def deal_out(items):
        return [items[0]] + [cross(items[k], k) for k in range(1, 4)]

    def arrange(got):
        return jnp.transpose(jnp.stack(xor_list(got, cx, core)), (0, 2, 1))

    def block_of(k):
        total = sum(
            lax.dynamic_slice(a, (0, (ctx ^ k) * local), (width, local)).astype(F32) for a in (h1, bf_own, bf_other)
        )
        return total.astype(BF)

    *dx, g_x, core_sums = lax.optimization_barrier((*dx, g_x, swap(sums, "core")))
    dx = deal_out(dx)
    sums = sums + core_sums
    bf_other, dx[1], x_sums, grads = lax.optimization_barrier((bf_other, dx[1], swap(sums, "cx"), grads))
    sums = sums + x_sums
    far = lax.ppermute(sums[2:], "dp", FAR) if count == 4 else sums
    grads_x = swap(grads, "cx")
    g_ffn, g_x, *blocks = lax.optimization_barrier((g_ffn, g_x, *[block_of(k) for k in range(4)]))
    out = deal_out(blocks)
    g_gate, g_up, g_down = spread_units(info, [g_ffn, swap(g_ffn, "core"), g_x, swap(g_x, "core")], units)
    out[1], grads_x, far = lax.optimization_barrier((out[1], grads_x, far))
    grads = (grads.astype(F32) + grads_x.astype(F32)).astype(BF)
    if count == 4:
        sums = sums[:2] + far
        near = lax.ppermute(sums[1], "dp", NEAR)
    else:
        near = lax.psum(far, "dp")
    out[2], grads_core, near, g_gate = lax.optimization_barrier((out[2], swap(grads, "core"), near, g_gate))
    g_weights = jnp.concatenate(in_order(grads, grads_core, core), axis=0).astype(F32)
    g_weights = g_weights.reshape(4, cols, shard)
    if count == 4:
        sums = sums[0] + near
        vec = sums[:24:8]
    else:
        sums = near[0]
        vec = lax.dynamic_slice(sums[:24:8], (0, rank * shard), (3, shard))
    table = sums[24:, :size].reshape(table.shape).T

    return (
        arrange(out),
        gates,
        arrange(dx),
        vec[0],
        g_weights[0].T,
        g_weights[1].T,
        g_weights[2].T,
        g_weights[3],
        table,
        vec[1],
        vec[2],
        g_gate,
        g_up,
        g_down.T,
    )


def solution(mesh):
    dp, ctx, tp = (mesh.shape[name] for name in ("dp", "ctx", "tp"))
    split = Mesh(mesh.devices.reshape(dp, 2, ctx // 2, tp), ("dp", "cx", "core", "tp"))
    tokens = P(None, ("dp", "cx", "core"), None)
    in_specs = (
        tokens,
        tokens,
        P(None, "dp", None),
        P(None, "dp", None),
        P(None, "dp", None),
        P("dp"),
        P("dp", "tp"),
        P("dp", "tp"),
        P("dp", "tp"),
        P("tp", "dp"),
        P(None, "tp"),
        P("dp"),
        P("dp"),
        P("dp", "tp"),
        P("dp", "tp"),
        P("tp", "dp"),
    )
    out_specs = (
        tokens,
        P(None, ("dp", "cx", "core")),
        tokens,
        P("dp"),
        P("dp", "tp"),
        P("dp", "tp"),
        P("dp", "tp"),
        P("tp", "dp"),
        P(None, "tp"),
        P("dp"),
        P("dp"),
        P("dp", "tp"),
        P("dp", "tp"),
        P("tp", "dp"),
    )
    return jax.shard_map(body, mesh=split, in_specs=in_specs, out_specs=out_specs, check_vma=False)
```
